32 devices in a mesh: tok: 2 (over core), blk: 16 (over z, y, x).
Axes of the slice: x: 2, y: 2, z: 4, core: 2. Of those that a mesh axis runs over, the one named last changes fastest.
Arguments:
- q_proj: bfloat16 [2048, 2048], P('blk', 'tok'), may hold values from -6 to 6
- k_proj: bfloat16 [2048, 2048], P('blk', 'tok'), may hold values from -6 to 6
- v_proj: bfloat16 [2048, 2048], P('blk', 'tok'), may hold values from -6 to 6
- residual: bfloat16 [2048, 2048], P('blk', 'tok'), may hold values from -6 to 6
- prompt_lengths: int32 [8], replicated, may hold values from 1 to 512, 2048 in all
- expert_ids: int32 [2048, 6], P('blk'), may hold values from 0 to 15, all different within a row; in each aligned block of 128 rows (0 to 127, 128 to 255, ...) at most 96 rows name the same one
- gate_weights: float32 [2048, 6], P('blk'), may hold values from 0.02 to 0.6
- page_table: int32 [128], P('blk'), may hold values from 0 to 127, as said below
- out_weight: bfloat16 [2048, 2048], P('tok'), may hold values from -0.125 to 0.125
- norm_gain: float32 [2048], replicated, may hold values from 0.1 to 1.9
- w_gate: bfloat16 [16, 2048, 1408], P('blk', None, 'tok'), may hold values from -0.125 to 0.125
- w_up: bfloat16 [16, 2048, 1408], P('blk', None, 'tok'), may hold values from -0.125 to 0.125
- w_down: bfloat16 [16, 1408, 2048], P('blk', 'tok'), may hold values from -0.15625 to 0.15625
Outputs:
- layer_out: bfloat16 [2048, 2048], P('blk', 'tok')
- kv_cache: bfloat16 [128, 16, 2, 2048], P('blk', None, None, 'tok')
The draws below stay inside these ranges and needn't reach their ends.
Inputs may be any that keep to these rules, and one draw needn't show every extreme that they name: `prompt_lengths`: the prompts fill the pack of 2048 tokens; the longest has exactly 512 tokens. `expert_ids`: each token names 6 different experts. Among the 128 tokens of one index of blk (aligned blocks) no expert is named by more than 96 tokens, a bound that some block reaches. `page_table`: each aligned block of 8 entries is a permutation of the same block's page numbers.
All inputs are finite; a program needn't handle non-finite values.
Results may differ from the reference program's by a relative error of at most 0.012.
Values may be sent and summed in bfloat16 or wider, within the bound.
No kernel may reach another device: no remote copies, remote signals or barrier semaphores. Data moves between devices by JAX's collectives and lax.ppermute only.
A program may use at most 64 MiB of HBM per device.

```python
import math
import jax
import jax.numpy as jnp
import numpy as np
from jax import lax

D = 2048
HEADS = 16
HEAD_DIM = 128
FF = 1408
TOPK = 6
TOK_DEV = 128
PAGE = 16
TOKENS = 2048
HID = 2048
EXPERTS = 16
LMAX = 512
NSEG = 8
CAP = 96
PAGES = 128
PAGES_DEV = 8
N_TOK = 2
N_BLK = 16


def draw_q_proj(key, part):
    base_draw = jnp.clip(jax.random.normal(jax.random.fold_in(key, 1), (TOKENS, HEADS * HEAD_DIM), jnp.float32), -5.0, 5.0)
    return base_draw.astype(jnp.bfloat16)


def draw_k_proj(key, part):
    base_draw = jnp.clip(jax.random.normal(jax.random.fold_in(key, 2), (TOKENS, HEADS * HEAD_DIM), jnp.float32), -5.0, 5.0)
    return base_draw.astype(jnp.bfloat16)


def one_order(block_key):
    return jax.random.permutation(block_key, PAGES_DEV)


def draw_page_table(key, part):
    blocks = TOKENS // TOK_DEV
    keys_all = jax.random.split(key, blocks)
    orders = jax.vmap(one_order)(keys_all)
    return (orders + (jnp.arange(blocks) * PAGES_DEV)[:, None]).reshape(-1).astype(jnp.int32)


def levels(rng, dims, cuts, least, top_value):
    factor_of, own = 1.0, jax.random.fold_in(rng, 6)
    for dim, parts in cuts:
        steps = jnp.exp(jax.random.uniform(jax.random.fold_in(own, dim), (parts,), jnp.float32, least / len(cuts), top_value / len(cuts)))
        factor_of = factor_of * jnp.repeat(steps, dims[dim] // parts).reshape([-1 if axis == dim else 1 for axis in range(len(dims))])
    return factor_of


def length_profile(amount, total, bound, slope):
    weights = [(1 << 20) // math.isqrt(grade ** slope) + 1 for grade in range(2, amount + 1)]
    surplus, given = total - bound - (amount - 1), [1] * (amount - 1)
    while surplus > 0:
        candidates = [i for i in range(amount - 1) if given[i] < bound]
        whole, remaining = sum([weights[i] for i in candidates]), surplus
        for i in candidates:
            more = min(bound - given[i], max(1, remaining * weights[i] // whole), surplus)
            given[i] = given[i] + more
            surplus = surplus - more
    return np.array([bound] + given)


def ragged(stream_key, number_of, total, limit, slope):
    if number_of == 2:
        one = jax.random.randint(stream_key, (), max(1, total - limit), min(limit, total - 1) + 1)
        return jnp.stack([one, total - one])
    tallies = jnp.asarray(length_profile(number_of, total, limit, slope), jnp.int32)
    pairs = (number_of - 1) // 2
    source_of, sink = tallies[1:1 + 2 * pairs:2], tallies[2:2 + 2 * pairs:2]
    room = jnp.minimum(source_of - 1, limit - sink)
    passed = jax.random.randint(jax.random.fold_in(stream_key, 1), (pairs,), 0, 1 << 20) % (room + 1)
    tallies = tallies.at[1:1 + 2 * pairs:2].set(source_of - passed).at[2:2 + 2 * pairs:2].set(sink + passed)
    return tallies[jax.random.permutation(jax.random.fold_in(stream_key, 2), number_of)]


def assign_block(rng, own, number, rows, count, top, most, skew):
    order = jax.random.permutation(rng, count)
    heavy_load, usual = load_shares(count, rows * top, most, skew, True), load_shares(count, rows * top, most, skew, False)
    places = jnp.arange(count)

    def named(tallies, rotation):
        used = int((tallies > 0).sum())
        fixed = max(1, used // 4)
        passed = fixed + (places - fixed + rotation * (used - fixed)) % max(1, count - fixed)
        return jnp.zeros((count,), jnp.int32).at[order[jnp.where(places < fixed, places, passed)]].set(jnp.asarray(tallies, jnp.int32))

    tallies = jnp.where(number % 4 == 0, named(heavy_load, number // 4), named(usual, number - number // 4 - 1))
    mixed = jax.random.permutation(jax.random.fold_in(own, 3), count)
    giver, receiver = mixed[0:count // 2 * 2:2], mixed[1:count // 2 * 2:2]
    room = jnp.minimum(tallies[giver] - 1, most - tallies[receiver]) // 2
    room = jnp.where((giver == order[0]) | (receiver == order[0]) | (tallies[receiver] == 0), 0, jnp.maximum(room, 0))
    passed = jax.random.randint(jax.random.fold_in(own, 4), (count // 2,), 0, 1 << 20) % (room + 1)
    tallies = tallies.at[giver].add(-passed).at[receiver].add(passed)
    labels = jnp.searchsorted(jnp.cumsum(tallies), jnp.arange(rows * top), side="right").astype(jnp.int32)
    grid = labels.reshape(top, rows).T
    grid = grid[jax.random.permutation(jax.random.fold_in(own, 1), rows)]
    rotation = jax.random.randint(jax.random.fold_in(own, 2), (rows, 1), 0, top)
    return jnp.take_along_axis(grid, (jnp.arange(top)[None, :] + rotation) % top, axis=1)


def load_shares(amount, total, most, skew, full):
    loads = [(1 << 20) // math.isqrt(standing ** skew) + 1 for standing in range(1, amount + 1)]
    largest = most if full else min(most, max(-(-total // amount), total * loads[0] // sum(loads)))
    least = 1 if total - largest >= amount - 1 else 0
    given, spare = [largest] + [least] * (amount - 1), total - largest - least * (amount - 1)
    while spare > 0:
        free = [i for i in range(1, amount) if given[i] < largest] or [i for i in range(1, amount) if given[i] < most]
        pool, budget = sum([loads[i] for i in free]), spare
        for i in free:
            more = min(most - given[i], max(1, budget * loads[i] // pool), spare)
            given[i] = given[i] + more
            spare = spare - more
    return np.array(given)


def gaussian(rng, extent, scale, limit, cuts=(), kind=jnp.bfloat16):
    result = jax.random.normal(rng, extent, jnp.float32) * scale
    if len(cuts) > 0:
        result = levels(rng, extent, cuts, -0.22, 0.18) * result
    return jnp.clip(result, min=-limit, max=limit).astype(kind)


def setup_inputs(seed: int = 0) -> dict:
    key_list = jax.random.split(jax.random.key(seed), 14)
    q_proj = draw_q_proj(jax.random.fold_in(key_list[13], 71), 0)
    k_proj = draw_k_proj(jax.random.fold_in(key_list[13], 71), 0)
    v_proj = gaussian(key_list[2], (TOKENS, HID), 1.0, 6.0, ((0, 16), (1, 2)))
    residual = gaussian(key_list[3], (TOKENS, D), 1.0, 6.0, ((0, 16), (1, 2)))
    prompt_lengths = ragged(key_list[4], NSEG, TOKENS, LMAX, 2).astype(jnp.int32)
    expert_ids_keys = jax.random.split(jax.random.fold_in(key_list[5], 1), TOKENS // TOK_DEV)
    expert_ids_turns = jax.random.permutation(jax.random.fold_in(key_list[5], 3), TOKENS // TOK_DEV)
    expert_ids = jax.vmap(lambda own, number: assign_block(jax.random.fold_in(key_list[5], 2), own, number, TOK_DEV, EXPERTS, TOPK, CAP, 2))(expert_ids_keys, expert_ids_turns).reshape((TOKENS, TOPK))
    gate_weights = jnp.clip(jnp.exp(math.log(0.6) - 3.4011974 * jax.random.uniform(key_list[6], (TOKENS, TOPK), jnp.float32) ** levels(key_list[6], (TOKENS, TOPK), ((0, 16),), -0.2, 0.2)), 0.02, 0.6)
    page_table = draw_page_table(jax.random.fold_in(key_list[13], 71), 0)
    out_weight = gaussian(key_list[8], (HID, D), HID ** -0.5, 0.125, ((0, 2),))
    norm_gain = jnp.clip(1.0 + 0.18 * jax.random.normal(key_list[9], (D,), jnp.float32), 0.1, 1.9)
    w_gate = gaussian(key_list[10], (EXPERTS, D, FF), D ** -0.5, 0.125, ((0, 16), (2, 2)))
    w_up = gaussian(key_list[11], (EXPERTS, D, FF), D ** -0.5, 0.125, ((0, 16), (2, 2)))
    w_down = gaussian(key_list[12], (EXPERTS, FF, D), FF ** -0.5, 0.15625, ((0, 16), (1, 2)))
    return dict(q_proj=q_proj, k_proj=k_proj, v_proj=v_proj, residual=residual, prompt_lengths=prompt_lengths, expert_ids=expert_ids, gate_weights=gate_weights, page_table=page_table, out_weight=out_weight, norm_gain=norm_gain, w_gate=w_gate, w_up=w_up, w_down=w_down)


def positions_of(token_ids, prompt_lengths):
    seg_ends = jnp.cumsum(prompt_lengths)
    before = token_ids[:, None] >= seg_ends[None, :]
    segment = lax.optimization_barrier(jnp.sum(before.astype(jnp.int32), axis=1))
    seg_start = lax.optimization_barrier(jnp.max(jnp.where(before, seg_ends[None, :], 0), axis=1))
    return (segment, token_ids - seg_start)

def rotate(block_rows, position):
    row_count = block_rows.shape[0]
    half_dim = HEAD_DIM // 2
    head_view = block_rows.reshape(row_count, -1, HEAD_DIM).astype(jnp.float32)
    inv_freq = 10000.0 ** (-jnp.arange(half_dim, dtype=jnp.float32) / half_dim)
    angles = position.astype(jnp.float32)[:, None] * inv_freq[None, :]
    cosine = jnp.cos(angles)[:, None, :]
    sine_part = jnp.sin(angles)[:, None, :]
    lower_half = head_view[..., :half_dim]
    upper_half = head_view[..., half_dim:]
    turned = jnp.concatenate([lower_half * cosine - upper_half * sine_part, upper_half * cosine + lower_half * sine_part], axis=-1)
    return turned.reshape(row_count, -1).astype(jnp.bfloat16)

def attend(rot_query, key_rows, value_rows, q_seg, q_index, k_seg, k_index):
    q_count = rot_query.shape[0]
    k_count = key_rows.shape[0]
    q_heads = rot_query.reshape(q_count, -1, HEAD_DIM).astype(jnp.float32)
    k_heads = key_rows.reshape(k_count, -1, HEAD_DIM).astype(jnp.float32)
    v_heads = value_rows.reshape(k_count, -1, HEAD_DIM).astype(jnp.float32)
    scores = jnp.einsum('qhd,khd->hqk', q_heads, k_heads) * HEAD_DIM ** (-0.5)
    allowed = (k_seg[None, :] == q_seg[:, None]) & (k_index[None, :] <= q_index[:, None]) & (k_index[None, :] >= 0)
    scores = jnp.where(allowed[None], scores, -1e+30)
    top_score = lax.optimization_barrier(jnp.max(scores, axis=2, keepdims=True))
    exp_terms = jnp.where(allowed[None], jnp.exp(scores - top_score), 0.0)
    soft_weights = (exp_terms / lax.optimization_barrier(jnp.sum(exp_terms, axis=2, keepdims=True))).astype(jnp.bfloat16)
    mixed_heads = jnp.einsum('hqk,khd->qhd', soft_weights.astype(jnp.float32), v_heads)
    return mixed_heads.reshape(q_count, -1).astype(jnp.bfloat16)

def expert_rows(sel_rows, gate_mat, up_mat, down_mat):
    rows_f = sel_rows.astype(jnp.float32)
    gate_act = jnp.dot(rows_f, gate_mat.astype(jnp.float32))
    up_act = jnp.dot(rows_f, up_mat.astype(jnp.float32))
    hidden = (jax.nn.silu(gate_act) * up_act).astype(jnp.bfloat16)
    group = FF // N_TOK
    summed = jnp.zeros((sel_rows.shape[0], D), jnp.float32)
    for member in range(N_TOK):
        piece = jnp.dot(hidden[:, member * group:(member + 1) * group].astype(jnp.float32), down_mat[member * group:(member + 1) * group].astype(jnp.float32))
        summed = summed + piece.astype(jnp.bfloat16).astype(jnp.float32)
    return summed.astype(jnp.bfloat16)

def reference(q_proj, k_proj, v_proj, residual, prompt_lengths, expert_ids, gate_weights, page_table, out_weight, norm_gain, w_gate, w_up, w_down):
    token_ids = jnp.arange(TOKENS, dtype=jnp.int32)
    segment, position = positions_of(token_ids, prompt_lengths)
    rot_query = rotate(q_proj, position)
    rot_keys = rotate(k_proj, position)
    kv_rows = jnp.stack([rot_keys, v_proj], axis=1).reshape(PAGES, PAGE, 2, HID)
    kv_cache = jnp.zeros((PAGES, PAGE, 2, HID), jnp.bfloat16).at[page_table].set(kv_rows)
    pad_keys = jnp.concatenate([jnp.zeros((LMAX, HID), jnp.bfloat16), rot_keys])
    pad_values = jnp.concatenate([jnp.zeros((LMAX, HID), jnp.bfloat16), v_proj])

    def one_block(start):
        q_rows = lax.dynamic_slice_in_dim(rot_query, start, TOK_DEV)
        q_seg = lax.dynamic_slice_in_dim(segment, start, TOK_DEV)
        q_index = lax.dynamic_slice_in_dim(token_ids, start, TOK_DEV)
        key_rows = lax.dynamic_slice_in_dim(pad_keys, start, LMAX + TOK_DEV)
        value_rows = lax.dynamic_slice_in_dim(pad_values, start, LMAX + TOK_DEV)
        key_ids = start - LMAX + jnp.arange(LMAX + TOK_DEV, dtype=jnp.int32)
        key_seg, unused = positions_of(key_ids, prompt_lengths)
        return attend(q_rows, key_rows, value_rows, q_seg, q_index, key_seg, key_ids)
    starts = jnp.arange(TOKENS // TOK_DEV, dtype=jnp.int32) * TOK_DEV
    attention = lax.map(one_block, starts).reshape(TOKENS, HID)
    projected = jnp.dot(attention.astype(jnp.float32), out_weight.astype(jnp.float32))
    stream = (residual.astype(jnp.float32) + projected).astype(jnp.bfloat16)
    wide_rows = stream.astype(jnp.float32)
    inv_scale = lax.rsqrt(lax.optimization_barrier(jnp.mean(wide_rows * wide_rows, axis=1, keepdims=True)) + 1e-06)
    normed = (wide_rows * inv_scale * norm_gain[None, :]).astype(jnp.bfloat16)
    slot_total = N_BLK * CAP

    def one_expert(moe_sum, inputs):
        expert, gate_mat, up_mat, down_mat = inputs
        matches = expert_ids == expert
        weight = lax.optimization_barrier(jnp.sum(jnp.where(matches, gate_weights, 0.0), axis=1))
        chosen = jnp.any(matches, axis=1)
        sel_index = jnp.nonzero(chosen, size=slot_total, fill_value=0)[0].astype(jnp.int32)
        is_valid = jnp.arange(slot_total, dtype=jnp.int32) < jnp.sum(chosen.astype(jnp.int32))
        expert_out = expert_rows(normed[sel_index], gate_mat, up_mat, down_mat)
        scaled = jnp.where(is_valid, weight[sel_index], 0.0)[:, None] * expert_out.astype(jnp.float32)
        return (moe_sum.at[sel_index].add(scaled), None)
    moe, unused = lax.scan(one_expert, jnp.zeros((TOKENS, D), jnp.float32), (jnp.arange(EXPERTS, dtype=jnp.int32), w_gate, w_up, w_down))
    layer_out = (stream.astype(jnp.float32) + moe).astype(jnp.bfloat16)
    return (layer_out, kv_cache)
```

```python
import functools

import jax
import jax.numpy as jnp
from jax import lax
from jax.experimental import pallas as pl
from jax.experimental.pallas import tpu as pltpu
from jax.sharding import PartitionSpec as P

HEAD_DIM = 128
REACH = 4
PAGE = 16
PLANE = 4
EPSILON = 1e-06


def shifted(block, axis, distance):
    devices = range(lax.axis_size(axis))
    route = [(i - distance, i) for i in devices if i - distance in devices]
    return lax.ppermute(block, axis, route)


def flipped(block, mask):
    return lax.ppermute(block, "blk", [(i, i ^ mask) for i in range(lax.axis_size("blk"))])


def from_plane(block, ahead):
    count = lax.axis_size("blk")
    return lax.ppermute(
        block, "blk", [((i + PLANE * ahead) % count, i) for i in range(count)]
    )


def to_plane(block, ahead):
    count = lax.axis_size("blk")
    return lax.ppermute(
        block, "blk", [(i, (i + PLANE * ahead) % count) for i in range(count)]
    )


def from_core(block, ahead):
    count = lax.axis_size("tok")
    return lax.ppermute(block, "tok", [((i + ahead) % count, i) for i in range(count)])


def core_sum(block):
    if lax.axis_size("tok") == 2:
        return block + from_core(block, 1)
    return lax.psum(block, "tok")


def positions_of(token_ids, prompt_lengths):
    seg_ends = jnp.cumsum(prompt_lengths)
    before = token_ids[:, None] >= seg_ends[None, :]
    segment = jnp.sum(before.astype(jnp.int32), axis=1)
    seg_start = jnp.max(jnp.where(before, seg_ends[None, :], 0), axis=1)
    return (segment, token_ids - seg_start)


def rotate(block_rows, position):
    row_count = block_rows.shape[0]
    half_dim = HEAD_DIM // 2
    head_view = block_rows.reshape(row_count, -1, HEAD_DIM).astype(jnp.float32)
    inv_freq = 10000.0 ** (-jnp.arange(half_dim, dtype=jnp.float32) / half_dim)
    angles = position.astype(jnp.float32)[:, None] * inv_freq[None, :]
    cosine = jnp.cos(angles)[:, None, :]
    sine_part = jnp.sin(angles)[:, None, :]
    lower_half = head_view[..., :half_dim]
    upper_half = head_view[..., half_dim:]
    turned = jnp.concatenate(
        [
            lower_half * cosine - upper_half * sine_part,
            upper_half * cosine + lower_half * sine_part,
        ],
        axis=-1,
    )
    return turned.reshape(row_count, -1).astype(jnp.bfloat16)


def attend(rot_query, key_rows, value_rows, q_seg, q_index, k_seg, k_index):
    q_count = rot_query.shape[0]
    k_count = key_rows.shape[0]
    q_heads = rot_query.reshape(q_count, -1, HEAD_DIM)
    k_heads = key_rows.reshape(k_count, -1, HEAD_DIM)
    v_heads = value_rows.reshape(k_count, -1, HEAD_DIM)
    scores = jnp.einsum(
        "qhd,khd->hqk", q_heads, k_heads, preferred_element_type=jnp.float32
    ) * HEAD_DIM ** (-0.5)
    allowed = (
        (k_seg[None, :] == q_seg[:, None])
        & (k_index[None, :] <= q_index[:, None])
        & (k_index[None, :] >= 0)
    )
    scores = jnp.where(allowed[None], scores, -1e30)
    top_score = jnp.max(scores, axis=2, keepdims=True)
    exp_terms = jnp.where(allowed[None], jnp.exp(scores - top_score), 0.0)
    soft_weights = (exp_terms / jnp.sum(exp_terms, axis=2, keepdims=True)).astype(jnp.bfloat16)
    mixed_heads = jnp.einsum(
        "hqk,khd->qhd", soft_weights, v_heads, preferred_element_type=jnp.float32
    )
    return mixed_heads.reshape(q_count, -1).astype(jnp.bfloat16)


def gate_lanes(expert_ids, gate_weights, experts):
    hits = expert_ids[:, :, None] == jnp.arange(experts, dtype=jnp.int32)[None, None, :]
    gates = jnp.sum(jnp.where(hits, gate_weights[:, :, None], 0.0), axis=1)
    pieces = []
    for _ in range(3):
        piece = lax.reduce_precision(gates, 8, 7)
        pieces.append(piece.astype(jnp.bfloat16))
        gates = gates - piece
    lanes = jnp.concatenate(pieces, axis=1)
    return jnp.pad(lanes, ((0, 0), (0, -lanes.shape[1] % 128)))


def expert_kernel(experts, place_ref, rows_ref, gate_ref, up_ref, down_ref, out_ref):
    width = gate_ref.shape[1]
    parts, _, part_width = out_ref.shape
    rows = rows_ref[:, :width]
    lanes = rows_ref[:, width:].astype(jnp.float32)
    lane_ids = lax.broadcasted_iota(jnp.int32, lanes.shape, 1)
    named = (lane_ids < 3 * experts) & (lane_ids % experts == place_ref[0])
    weight = jnp.sum(jnp.where(named, lanes, 0.0), axis=1, keepdims=True)
    turned = (((1,), (1,)), ((), ()))
    gate_act = lax.dot_general(rows, gate_ref[...], turned, preferred_element_type=jnp.float32)
    up_act = lax.dot_general(rows, up_ref[...], turned, preferred_element_type=jnp.float32)
    hidden = (gate_act / (1.0 + jnp.exp(-gate_act)) * up_act).astype(jnp.bfloat16)
    for part in range(parts):
        columns = slice(part * part_width, (part + 1) * part_width)
        product = jnp.dot(hidden, down_ref[:, columns], preferred_element_type=jnp.float32)
        slot = lax.rem(part - place_ref[1] + parts, parts)
        out_ref[pl.ds(slot, 1)] = (weight * product).astype(jnp.bfloat16)[None]


def run_expert(place, rows, w_gate, w_up, w_down, experts, parts, tile):
    count, full_width = rows.shape
    units, width = w_gate.shape
    whole = functools.partial(pl.BlockSpec, memory_space=pltpu.VMEM)
    return pl.pallas_call(
        functools.partial(expert_kernel, experts),
        grid_spec=pltpu.PrefetchScalarGridSpec(
            num_scalar_prefetch=1,
            grid=(count // tile,),
            in_specs=[
                pl.BlockSpec((tile, full_width), lambda i, place: (i, 0)),
                whole(),
                whole(),
                whole(),
            ],
            out_specs=pl.BlockSpec((parts, tile, width // parts), lambda i, place: (0, i, 0)),
        ),
        out_shape=jax.ShapeDtypeStruct((parts, count, width // parts), jnp.bfloat16),
        cost_estimate=pl.CostEstimate(
            flops=6 * count * width * units,
            bytes_accessed=2 * (3 * width * units + 2 * count * width),
            transcendentals=count * units,
        ),
        compiler_params=pltpu.CompilerParams(vmem_limit_bytes=48 << 20),
    )(place, rows, w_gate, w_up, w_down)


def plane_gather(blocks):
    half = blocks.shape[1] // 2
    first, second = blocks[:, :half], blocks[:, half:]
    first_pair = jnp.stack([first, flipped(first, 1)])
    second_pair = jnp.stack([second, flipped(second, 2)])
    first_other = flipped(first_pair, 2)
    second_other = flipped(second_pair, 1)
    firsts = [first_pair[0], first_pair[1], first_other[0], first_other[1]]
    seconds = [second_pair[0], second_other[0], second_pair[1], second_other[1]]
    return jnp.stack(
        [jnp.concatenate([a, b], axis=1) for a, b in zip(firsts, seconds, strict=True)]
    )


def wide(block):
    return block.astype(jnp.float32)


def narrow(block):
    return block.astype(jnp.bfloat16)


def plane_scatter(kept, came):
    half = kept.shape[-1] // 2
    total = wide(kept) + wide(came)
    first, second = total[..., :half], total[..., half:]
    got = flipped(narrow(first[2:4]), 2)
    first = first[0:2] + wide(got)
    got = flipped(narrow(jnp.stack([second[1], second[3]])), 1)
    second = jnp.stack([second[0], second[2]]) + wide(got)
    got_first = flipped(narrow(first[1]), 1)
    got_second = flipped(narrow(second[1]), 2)
    return jnp.concatenate([first[0] + wide(got_first), second[0] + wide(got_second)], axis=-1)


def on_device(
    q_proj,
    k_proj,
    v_proj,
    residual,
    prompt_lengths,
    expert_ids,
    gate_weights,
    page_table,
    out_weight,
    norm_gain,
    w_gate,
    w_up,
    w_down,
):
    tok_rows = q_proj.shape[0]
    col_width = residual.shape[1]
    model_width = norm_gain.shape[0]
    blk_index = lax.axis_index("blk")
    tok_index = lax.axis_index("tok")
    cores = lax.axis_size("tok")
    experts = lax.axis_size("blk")
    planes = experts // PLANE
    token_ids = blk_index * tok_rows + jnp.arange(tok_rows, dtype=jnp.int32)
    segment, position = positions_of(token_ids, prompt_lengths)
    rot_query = rotate(q_proj, position)
    rot_keys = rotate(k_proj, position)
    own_pair = jnp.stack([rot_keys, v_proj])
    pair_list = [own_pair]
    id_list = [token_ids]
    carried = own_pair
    for distance in range(1, REACH + 1):
        carried = shifted(carried, "blk", 1)
        pair_list.append(carried)
        id_list.append(token_ids - distance * tok_rows)
    all_pairs = jnp.concatenate(pair_list, axis=1)
    key_ids = jnp.concatenate(id_list)
    key_seg, unused = positions_of(key_ids, prompt_lengths)
    attention = attend(rot_query, all_pairs[0], all_pairs[1], segment, token_ids, key_seg, key_ids)
    partial_value = jnp.dot(attention, out_weight, preferred_element_type=jnp.float32)
    placed_residual = lax.dynamic_update_slice_in_dim(
        jnp.zeros((tok_rows, model_width), jnp.bfloat16), residual, tok_index * col_width, 1
    )
    stream = core_sum(partial_value + wide(placed_residual)).astype(jnp.bfloat16)
    wide_rows = stream.astype(jnp.float32)
    inv_scale = lax.rsqrt(jnp.mean(wide_rows * wide_rows, axis=1, keepdims=True) + EPSILON)
    normed = (wide_rows * inv_scale * norm_gain[None, :]).astype(jnp.bfloat16)
    own_share = lax.dynamic_slice_in_dim(stream, tok_index * col_width, col_width, 1)

    part_rows = tok_rows // cores
    lanes = gate_lanes(expert_ids, gate_weights, experts)
    payload = lax.dynamic_slice_in_dim(
        jnp.concatenate([normed, lanes], axis=1), tok_index * part_rows, part_rows, 0
    )[None]
    place = jnp.stack([blk_index, tok_index]).astype(jnp.int32)
    groups = [[0]] + [sorted({ahead, planes - ahead}) for ahead in range(1, planes // 2 + 1)]
    came = {0: payload}
    for ahead in range(1, planes):
        came[ahead] = from_plane(payload, ahead)
    gate_turned, up_turned = w_gate[0].T, w_up[0].T
    results = {}
    for group in groups:
        column = jnp.concatenate([came[ahead] for ahead in group])
        if planes > 4 and results:
            column, results = lax.optimization_barrier((column, results))
        held = plane_gather(column)
        count = len(group)
        own_rows = held.reshape(PLANE * count * part_rows, held.shape[-1])
        outs = []
        for ahead in range(cores):
            rows = own_rows if ahead == 0 else from_core(own_rows, ahead)
            outs.append(
                run_expert(
                    place, rows, gate_turned, up_turned, w_down[0], experts, cores, PLANE * part_rows
                )
            )
        full = (PLANE, count, part_rows, col_width)
        kept = jnp.stack([outs[j][0].reshape(full) for j in range(cores)], axis=2)
        arrived = 0.0
        for ahead in range(1, cores):
            sent = jnp.stack([outs[(ahead + j) % cores][ahead] for j in range(cores)])
            got = from_core(sent, cores - ahead)
            arrived = arrived + wide(got)
        arrived = jnp.stack([arrived[j].reshape(full) for j in range(cores)], axis=2)
        merged = (PLANE, count, cores * part_rows, col_width)
        summed = plane_scatter(kept.reshape(merged), arrived.reshape(merged))
        for place_in, ahead in enumerate(group):
            results[ahead] = summed[place_in]
    moe = results[0]
    for ahead in range(1, planes):
        moe = moe + wide(to_plane(narrow(results[ahead]), ahead))
    moe = jnp.roll(moe.reshape(cores, part_rows, col_width), tok_index, axis=0)
    moe = moe.reshape(tok_rows, col_width)
    layer_out = (own_share.astype(jnp.float32) + moe).astype(jnp.bfloat16)
    page_count = tok_rows // PAGE
    local_page = page_table - blk_index * page_count
    kv_rows = jnp.stack([rot_keys, v_proj], axis=1).reshape(page_count, PAGE, 2, -1)
    kv_pages = jnp.zeros_like(kv_rows).at[local_page].set(kv_rows)
    return (layer_out, kv_pages)


def solution(mesh):
    placed = (
        P("blk", "tok"),
        P("blk", "tok"),
        P("blk", "tok"),
        P("blk", "tok"),
        P(),
        P("blk", None),
        P("blk", None),
        P("blk"),
        P("tok", None),
        P(),
        P("blk", None, "tok"),
        P("blk", None, "tok"),
        P("blk", "tok", None),
    )
    return jax.shard_map(
        on_device,
        mesh=mesh,
        in_specs=placed,
        out_specs=(P("blk", "tok"), P("blk", None, None, "tok")),
        check_vma=False,
    )
```

```python
import functools

import jax
import jax.numpy as jnp
from jax import lax
from jax.experimental import pallas as pl
from jax.experimental.pallas import tpu as pltpu
from jax.sharding import PartitionSpec as P

HEAD_DIM = 128
REACH = 4
PAGE = 16
PLANE = 4
EPSILON = 1e-06


def shifted(block, axis, distance):
    devices = range(lax.axis_size(axis))
    route = [(i - distance, i) for i in devices if i - distance in devices]
    return lax.ppermute(block, axis, route)


def from_plane(block, ahead):
    count = lax.axis_size("blk")
    return lax.ppermute(
        block, "blk", [((i + PLANE * ahead) % count, i) for i in range(count)]
    )


def to_plane(block, ahead):
    count = lax.axis_size("blk")
    return lax.ppermute(
        block, "blk", [(i, (i + PLANE * ahead) % count) for i in range(count)]
    )


def from_core(block, ahead):
    count = lax.axis_size("tok")
    return lax.ppermute(block, "tok", [((i + ahead) % count, i) for i in range(count)])


def core_sum(block):
    if lax.axis_size("tok") == 2:
        return block + from_core(block, 1)
    return lax.psum(block, "tok")


def positions_of(token_ids, prompt_lengths):
    seg_ends = jnp.cumsum(prompt_lengths)
    before = token_ids[:, None] >= seg_ends[None, :]
    segment = jnp.sum(before.astype(jnp.int32), axis=1)
    seg_start = jnp.max(jnp.where(before, seg_ends[None, :], 0), axis=1)
    return (segment, token_ids - seg_start)


def rotate(block_rows, position):
    row_count = block_rows.shape[0]
    half_dim = HEAD_DIM // 2
    head_view = block_rows.reshape(row_count, -1, HEAD_DIM).astype(jnp.float32)
    inv_freq = 10000.0 ** (-jnp.arange(half_dim, dtype=jnp.float32) / half_dim)
    angles = position.astype(jnp.float32)[:, None] * inv_freq[None, :]
    cosine = jnp.cos(angles)[:, None, :]
    sine_part = jnp.sin(angles)[:, None, :]
    lower_half = head_view[..., :half_dim]
    upper_half = head_view[..., half_dim:]
    turned = jnp.concatenate(
        [
            lower_half * cosine - upper_half * sine_part,
            upper_half * cosine + lower_half * sine_part,
        ],
        axis=-1,
    )
    return turned.reshape(row_count, -1).astype(jnp.bfloat16)


def attend(rot_query, key_rows, value_rows, q_seg, q_index, k_seg, k_index):
    q_count = rot_query.shape[0]
    k_count = key_rows.shape[0]
    q_heads = rot_query.reshape(q_count, -1, HEAD_DIM)
    k_heads = key_rows.reshape(k_count, -1, HEAD_DIM)
    v_heads = value_rows.reshape(k_count, -1, HEAD_DIM)
    scores = jnp.einsum(
        "qhd,khd->hqk", q_heads, k_heads, preferred_element_type=jnp.float32
    ) * HEAD_DIM ** (-0.5)
    allowed = (
        (k_seg[None, :] == q_seg[:, None])
        & (k_index[None, :] <= q_index[:, None])
        & (k_index[None, :] >= 0)
    )
    scores = jnp.where(allowed[None], scores, -1e30)
    top_score = jnp.max(scores, axis=2, keepdims=True)
    exp_terms = jnp.where(allowed[None], jnp.exp(scores - top_score), 0.0)
    soft_weights = (exp_terms / jnp.sum(exp_terms, axis=2, keepdims=True)).astype(jnp.bfloat16)
    mixed_heads = jnp.einsum(
        "hqk,khd->qhd", soft_weights, v_heads, preferred_element_type=jnp.float32
    )
    return mixed_heads.reshape(q_count, -1).astype(jnp.bfloat16)


def gate_lanes(expert_ids, gate_weights, experts):
    hits = expert_ids[:, :, None] == jnp.arange(experts, dtype=jnp.int32)[None, None, :]
    gates = jnp.sum(jnp.where(hits, gate_weights[:, :, None], 0.0), axis=1)
    pieces = []
    for _ in range(3):
        piece = lax.reduce_precision(gates, 8, 7)
        pieces.append(piece.astype(jnp.bfloat16))
        gates = gates - piece
    lanes = jnp.concatenate(pieces, axis=1)
    return jnp.pad(lanes, ((0, 0), (0, -lanes.shape[1] % 128)))


def crossed(block, first):
    cores, count = lax.axis_size("tok"), lax.axis_size("blk")
    route = []
    for core in range(cores):
        mask = 1 if (core % 2 == 0) == first else 2
        route += [(core * count + i, core * count + (i ^ mask)) for i in range(count)]
    return lax.ppermute(block, ("tok", "blk"), route)


def expert_kernel(experts, ahead, place_ref, near_ref, far_ref, gate_ref, up_ref, down_ref, *outs):
    width = gate_ref.shape[1]
    parts = len(outs)
    blocks, part_rows, part_width = outs[0].shape
    held = jnp.concatenate([near_ref[...], far_ref[...]], axis=0)
    rows = held[:, :width]
    lanes = held[:, width:].astype(jnp.float32)
    lane_ids = lax.broadcasted_iota(jnp.int32, lanes.shape, 1)
    named = (lane_ids < 3 * experts) & (lane_ids % experts == place_ref[0])
    weight = jnp.sum(jnp.where(named, lanes, 0.0), axis=1, keepdims=True)
    turned = (((1,), (1,)), ((), ()))
    gate_act = lax.dot_general(rows, gate_ref[...], turned, preferred_element_type=jnp.float32)
    up_act = lax.dot_general(rows, up_ref[...], turned, preferred_element_type=jnp.float32)
    hidden = (gate_act / (1.0 + jnp.exp(-gate_act)) * up_act).astype(jnp.bfloat16)
    for part in range(parts):
        start = lax.rem(place_ref[1] + part, parts) * part_width
        columns = pl.ds(pl.multiple_of(start, 128), part_width)
        product = jnp.dot(hidden, down_ref[:, columns], preferred_element_type=jnp.float32)
        product = (weight * product).astype(jnp.bfloat16)
        order = (0, 2, 1, 3) if (part - ahead) % 2 else (0, 1, 2, 3)
        for block in range(blocks):
            outs[part][order[block]] = product[block * part_rows : (block + 1) * part_rows]


def run_expert(place, near, far, w_gate, w_up, w_down, experts, parts, ahead):
    count = 2 * near.shape[0]
    units, width = w_gate.shape
    whole = pl.BlockSpec(memory_space=pltpu.VMEM)
    out_shape = jax.ShapeDtypeStruct((PLANE, count // PLANE, width // parts), jnp.bfloat16)
    return pl.pallas_call(
        functools.partial(expert_kernel, experts, ahead),
        in_specs=[pl.BlockSpec(memory_space=pltpu.SMEM)] + [whole] * 5,
        out_specs=[whole] * parts,
        out_shape=[out_shape] * parts,
        cost_estimate=pl.CostEstimate(
            flops=6 * count * width * units,
            bytes_accessed=2 * (3 * width * units + 2 * count * width),
            transcendentals=count * units,
        ),
        compiler_params=pltpu.CompilerParams(vmem_limit_bytes=24 << 20),
    )(place, near, far, w_gate, w_up, w_down)


def wide(block):
    return block.astype(jnp.float32)


def narrow(block):
    return block.astype(jnp.bfloat16)


def plane_scatter(totals):
    sent = narrow(jnp.stack([total[2:4] for total in totals]))
    got = crossed(sent, False)
    totals = [total[0:2] + wide(got[i]) for i, total in enumerate(totals)]
    sent = narrow(jnp.stack([total[1] for total in totals]))
    got = crossed(sent, True)
    return [total[0] + wide(got[i]) for i, total in enumerate(totals)]


def on_device(
    q_proj,
    k_proj,
    v_proj,
    residual,
    prompt_lengths,
    expert_ids,
    gate_weights,
    page_table,
    out_weight,
    norm_gain,
    w_gate,
    w_up,
    w_down,
):
    tok_rows = q_proj.shape[0]
    col_width = residual.shape[1]
    model_width = norm_gain.shape[0]
    blk_index = lax.axis_index("blk")
    tok_index = lax.axis_index("tok")
    cores = lax.axis_size("tok")
    experts = lax.axis_size("blk")
    planes = experts // PLANE
    token_ids = blk_index * tok_rows + jnp.arange(tok_rows, dtype=jnp.int32)
    segment, position = positions_of(token_ids, prompt_lengths)
    rot_query = rotate(q_proj, position)
    rot_keys = rotate(k_proj, position)
    own_pair = jnp.stack([rot_keys, v_proj])
    pair_list = [own_pair]
    id_list = [token_ids]
    carried = own_pair
    for distance in range(1, REACH + 1):
        carried = shifted(carried, "blk", 1)
        pair_list.append(carried)
        id_list.append(token_ids - distance * tok_rows)
    all_pairs = jnp.concatenate(pair_list, axis=1)
    key_ids = jnp.concatenate(id_list)
    key_seg, unused = positions_of(key_ids, prompt_lengths)
    attention = attend(rot_query, all_pairs[0], all_pairs[1], segment, token_ids, key_seg, key_ids)
    partial_value = jnp.dot(attention, out_weight, preferred_element_type=jnp.float32)
    placed_residual = lax.dynamic_update_slice_in_dim(
        jnp.zeros((tok_rows, model_width), jnp.bfloat16), residual, tok_index * col_width, 1
    )
    stream = core_sum(partial_value + wide(placed_residual)).astype(jnp.bfloat16)
    wide_rows = stream.astype(jnp.float32)
    inv_scale = lax.rsqrt(jnp.mean(wide_rows * wide_rows, axis=1, keepdims=True) + EPSILON)
    normed = (wide_rows * inv_scale * norm_gain[None, :]).astype(jnp.bfloat16)
    own_share = lax.dynamic_slice_in_dim(stream, tok_index * col_width, col_width, 1)

    part_rows = tok_rows // cores
    lanes = gate_lanes(expert_ids, gate_weights, experts)
    payload = lax.dynamic_slice_in_dim(
        jnp.concatenate([normed, lanes], axis=1), tok_index * part_rows, part_rows, 0
    )
    place = jnp.stack([blk_index, tok_index]).astype(jnp.int32)
    gate_turned, up_turned = w_gate[0].T, w_up[0].T
    came = {0: payload}
    for ahead in range(1, planes):
        came[ahead] = from_plane(payload, ahead)
    if planes <= 4:
        groups = [[0]] + [sorted({i, planes - i}) for i in range(1, planes // 2 + 1)]
    else:
        groups = [[0]] + [list(range(i, min(i + 8, planes))) for i in range(1, planes, 8)]
    results = {}
    for group in groups:
        column = jnp.concatenate([came[ahead] for ahead in group])
        if planes > 4 and results:
            column, results = lax.optimization_barrier((column, results))
        near = jnp.concatenate([column, crossed(column, True)])
        far = crossed(near, False)
        outs = []
        for ahead in range(cores):
            near_rows = from_core(near, ahead) if ahead else near
            far_rows = from_core(far, ahead) if ahead else far
            outs.append(
                run_expert(
                    place,
                    near_rows,
                    far_rows,
                    gate_turned,
                    up_turned,
                    w_down[0],
                    experts,
                    cores,
                    ahead,
                )
            )
        totals = []
        for rows_of in range(cores):
            total = wide(outs[rows_of][0])
            for ahead in range(1, cores):
                sent = outs[(rows_of + ahead) % cores][ahead]
                total = total + wide(from_core(sent, cores - ahead))
            totals.append(total)
        summed = plane_scatter(totals)
        for i, ahead in enumerate(group):
            results[ahead] = jnp.concatenate(
                [total[i * part_rows : (i + 1) * part_rows] for total in summed]
            )
    moe = results[0]
    for ahead in range(1, planes):
        moe = moe + wide(to_plane(narrow(results[ahead]), ahead))
    moe = jnp.roll(moe.reshape(cores, part_rows, col_width), tok_index, axis=0)
    moe = moe.reshape(tok_rows, col_width)
    layer_out = (own_share.astype(jnp.float32) + moe).astype(jnp.bfloat16)
    page_count = tok_rows // PAGE
    local_page = page_table - blk_index * page_count
    kv_rows = jnp.stack([rot_keys, v_proj], axis=1).reshape(page_count, PAGE, 2, -1)
    kv_pages = jnp.zeros_like(kv_rows).at[local_page].set(kv_rows)
    return (layer_out, kv_pages)


def solution(mesh):
    placed = (
        P("blk", "tok"),
        P("blk", "tok"),
        P("blk", "tok"),
        P("blk", "tok"),
        P(),
        P("blk", None),
        P("blk", None),
        P("blk"),
        P("tok", None),
        P(),
        P("blk", None, "tok"),
        P("blk", None, "tok"),
        P("blk", "tok", None),
    )
    return jax.shard_map(
        on_device,
        mesh=mesh,
        in_specs=placed,
        out_specs=(P("blk", "tok"), P("blk", None, None, "tok")),
        check_vma=False,
    )
```

```python
import functools

import jax
import jax.numpy as jnp
from jax import lax
from jax.experimental import pallas as pl
from jax.experimental.pallas import tpu as pltpu
from jax.sharding import PartitionSpec as P

HEAD_DIM = 128
REACH = 4
PAGE = 16
PLANE = 4
EPSILON = 1e-06


def after(value, *others):
    return lax.optimization_barrier((value, *others))[0]


def flipped(block, mask):
    return lax.ppermute(block, "blk", [(i, i ^ mask) for i in range(lax.axis_size("blk"))])


def next_plane(block):
    count = lax.axis_size("blk")
    return lax.ppermute(block, "blk", [(i, i + PLANE) for i in range(count - PLANE)])


def from_plane(block, ahead):
    count = lax.axis_size("blk")
    return lax.ppermute(
        block, "blk", [((i + PLANE * ahead) % count, i) for i in range(count)]
    )


def to_plane(block, ahead):
    count = lax.axis_size("blk")
    return lax.ppermute(
        block, "blk", [(i, (i + PLANE * ahead) % count) for i in range(count)]
    )


def from_core(block, ahead):
    count = lax.axis_size("tok")
    return lax.ppermute(block, "tok", [((i + ahead) % count, i) for i in range(count)])


def segment_starts(place_ref, lengths_ref, shape):
    token = place_ref[0] * shape[0] + lax.broadcasted_iota(jnp.int32, shape, 0)
    start = jnp.zeros(shape, jnp.int32)
    end = jnp.int32(0)
    for i in range(lengths_ref.shape[0]):
        end = end + lengths_ref[i]
        start = jnp.where(token >= end, end, start)
    return token, start


def rope_kernel(place_ref, lengths_ref, freq_ref, q_ref, k_ref, q_out, k_out):
    rows, width = q_ref.shape
    shape = (rows, HEAD_DIM)
    token, start = segment_starts(place_ref, lengths_ref, shape)
    angle = (token - start).astype(jnp.float32) * freq_ref[...]
    cosine, sine = jnp.cos(angle), jnp.sin(angle)
    lane = lax.broadcasted_iota(jnp.int32, shape, 1)
    sine = jnp.where(lane < HEAD_DIM // 2, -sine, sine)
    for source, target in ((k_ref, k_out), (q_ref, q_out)):
        for head in range(width // HEAD_DIM):
            columns = slice(head * HEAD_DIM, (head + 1) * HEAD_DIM)
            x = source[:, columns].astype(jnp.float32)
            turned = x * cosine + pltpu.roll(x, HEAD_DIM // 2, 1) * sine
            target[:, columns] = turned.astype(jnp.bfloat16)


def score_kernel(place_ref, lengths_ref, q_ref, *rest):
    *keys, out_ref = rest
    rows, width = q_ref.shape
    shape = (rows, rows)
    token, start = segment_starts(place_ref, lengths_ref, shape)
    blk = place_ref[0]
    column = lax.rem(blk, PLANE)
    bases = [blk, blk - PLANE]
    for mask in range(1, PLANE):
        other = column ^ mask
        bases.append(blk - column + other - jnp.where(other > column, PLANE, 0))
    lane = lax.broadcasted_iota(jnp.int32, shape, 1)
    ids = jnp.concatenate([base * rows + lane for base in bases], axis=1)
    token = jnp.concatenate([token] * len(keys), axis=1)
    start = jnp.concatenate([start] * len(keys), axis=1)
    allowed = (ids >= start) & (ids <= token)
    for head in range(width // HEAD_DIM):
        columns = slice(head * HEAD_DIM, (head + 1) * HEAD_DIM)
        key = jnp.concatenate([ref[:, columns] for ref in keys], axis=0)
        scores = lax.dot_general(
            q_ref[:, columns],
            key,
            (((1,), (1,)), ((), ())),
            preferred_element_type=jnp.float32,
        )
        scores = jnp.where(allowed, scores * HEAD_DIM ** (-0.5), -1e30)
        terms = jnp.exp(scores - jnp.max(scores, axis=1, keepdims=True))
        share = 1.0 / jnp.sum(terms, axis=1, keepdims=True)
        out_ref[head] = (terms * share).astype(jnp.bfloat16)


def mix_kernel(place_ref, prob_ref, weight_ref, residual_ref, *rest):
    *values, out_ref = rest
    heads = prob_ref.shape[0]
    mixed = []
    for head in range(heads):
        columns = slice(head * HEAD_DIM, (head + 1) * HEAD_DIM)
        value = jnp.concatenate([ref[:, columns] for ref in values], axis=0)
        product = jnp.dot(prob_ref[head], value, preferred_element_type=jnp.float32)
        mixed.append(product.astype(jnp.bfloat16))
    attention = jnp.concatenate(mixed, axis=1)
    out_ref[...] = jnp.dot(attention, weight_ref[...], preferred_element_type=jnp.float32)
    width = residual_ref.shape[1]
    own = pl.ds(pl.multiple_of(place_ref[1] * width, 128), width)
    out_ref[:, own] = out_ref[:, own] + residual_ref[...].astype(jnp.float32)


def norm_kernel(place_ref, gain_ref, lanes_ref, *rest):
    *addends, rows_out, share_out = rest
    rows, width = addends[0].shape
    part_rows = rows_out.shape[0]
    part_width = share_out.shape[1]
    own = pl.ds(pl.multiple_of(place_ref[1] * part_width, 128), part_width)
    share_out[...] = sum(ref[:, own] for ref in addends).astype(jnp.bfloat16)
    part = pl.ds(pl.multiple_of(place_ref[1] * part_rows, 16), part_rows)
    stream = sum(ref[part, :] for ref in addends).astype(jnp.bfloat16).astype(jnp.float32)
    scale = lax.rsqrt(jnp.mean(stream * stream, axis=1, keepdims=True) + EPSILON)
    rows_out[:, :width] = (stream * scale * gain_ref[...]).astype(jnp.bfloat16)
    rows_out[:, width:] = lanes_ref[part, :]


def local_call(body, out_shapes, scalars, arrays, flops=0, limit=16):
    whole = pl.BlockSpec(memory_space=pltpu.VMEM)
    scalar = pl.BlockSpec(memory_space=pltpu.SMEM)
    moved = sum(x.size * x.dtype.itemsize for x in (*arrays, *out_shapes))
    return pl.pallas_call(
        body,
        in_specs=[scalar] * len(scalars) + [whole] * len(arrays),
        out_specs=[whole] * len(out_shapes),
        out_shape=out_shapes,
        cost_estimate=pl.CostEstimate(flops=flops, bytes_accessed=moved, transcendentals=0),
        compiler_params=pltpu.CompilerParams(vmem_limit_bytes=limit << 20),
    )(*scalars, *arrays)


def gate_lanes(expert_ids, gate_weights, experts):
    hits = expert_ids[:, :, None] == jnp.arange(experts, dtype=jnp.int32)[None, None, :]
    gates = jnp.sum(jnp.where(hits, gate_weights[:, :, None], 0.0), axis=1)
    pieces = []
    for _ in range(3):
        piece = lax.reduce_precision(gates, 8, 7)
        pieces.append(piece.astype(jnp.bfloat16))
        gates = gates - piece
    lanes = jnp.concatenate(pieces, axis=1)
    return jnp.pad(lanes, ((0, 0), (0, -lanes.shape[1] % 128)))


def crossed(block, first):
    cores, count = lax.axis_size("tok"), lax.axis_size("blk")
    route = []
    for core in range(cores):
        mask = 1 if (core % 2 == 0) == first else 2
        route += [(core * count + i, core * count + (i ^ mask)) for i in range(count)]
    return lax.ppermute(block, ("tok", "blk"), route)


def expert_kernel(experts, ahead, place_ref, near_ref, far_ref, gate_ref, up_ref, down_ref, *outs):
    width = gate_ref.shape[1]
    parts = len(outs)
    blocks, part_rows, part_width = outs[0].shape
    held = jnp.concatenate([near_ref[...], far_ref[...]], axis=0)
    rows = held[:, :width]
    lanes = held[:, width:].astype(jnp.float32)
    lane_ids = lax.broadcasted_iota(jnp.int32, lanes.shape, 1)
    named = (lane_ids < 3 * experts) & (lane_ids % experts == place_ref[0])
    weight = jnp.sum(jnp.where(named, lanes, 0.0), axis=1, keepdims=True)
    turned = (((1,), (1,)), ((), ()))
    gate_act = lax.dot_general(rows, gate_ref[...], turned, preferred_element_type=jnp.float32)
    up_act = lax.dot_general(rows, up_ref[...], turned, preferred_element_type=jnp.float32)
    hidden = (gate_act / (1.0 + jnp.exp(-gate_act)) * up_act).astype(jnp.bfloat16)
    for part in range(parts):
        start = lax.rem(place_ref[1] + part, parts) * part_width
        columns = pl.ds(pl.multiple_of(start, 128), part_width)
        product = jnp.dot(hidden, down_ref[:, columns], preferred_element_type=jnp.float32)
        product = (weight * product).astype(jnp.bfloat16)
        order = (0, 2, 1, 3) if (part - ahead) % 2 else (0, 1, 2, 3)
        for block in range(blocks):
            outs[part][order[block]] = product[block * part_rows : (block + 1) * part_rows]


def run_expert(place, near, far, w_gate, w_up, w_down, experts, parts, ahead):
    count = 2 * near.shape[0]
    units, width = w_gate.shape
    out_shape = jax.ShapeDtypeStruct((PLANE, count // PLANE, width // parts), jnp.bfloat16)
    return local_call(
        functools.partial(expert_kernel, experts, ahead),
        [out_shape] * parts,
        [place],
        [near, far, w_gate, w_up, w_down],
        flops=6 * count * width * units,
    )


def wide(block):
    return block.astype(jnp.float32)


def narrow(block):
    return block.astype(jnp.bfloat16)


def plane_scatter(totals):
    sent = narrow(jnp.stack([total[2:4] for total in totals]))
    got = crossed(sent, False)
    totals = [total[0:2] + wide(got[i]) for i, total in enumerate(totals)]
    sent = narrow(jnp.stack([total[1] for total in totals]))
    got = crossed(sent, True)
    return [total[0] + wide(got[i]) for i, total in enumerate(totals)]


def expert_group(place, near, far, weights, experts, cores):
    outs = []
    for ahead in range(cores):
        near_rows = from_core(near, ahead) if ahead else near
        far_rows = from_core(far, ahead) if ahead else far
        outs.append(run_expert(place, near_rows, far_rows, *weights, experts, cores, ahead))
    totals = []
    for rows_of in range(cores):
        total = wide(outs[rows_of][0])
        for ahead in range(1, cores):
            sent = outs[(rows_of + ahead) % cores][ahead]
            total = total + wide(from_core(sent, cores - ahead))
        totals.append(total)
    return plane_scatter(totals)


def on_device(
    q_proj,
    k_proj,
    v_proj,
    residual,
    prompt_lengths,
    expert_ids,
    gate_weights,
    page_table,
    out_weight,
    norm_gain,
    w_gate,
    w_up,
    w_down,
):
    tok_rows = q_proj.shape[0]
    col_width = residual.shape[1]
    model_width = norm_gain.shape[0]
    blk_index = lax.axis_index("blk")
    tok_index = lax.axis_index("tok")
    cores = lax.axis_size("tok")
    experts = lax.axis_size("blk")
    planes = experts // PLANE
    place = jnp.stack([blk_index, tok_index]).astype(jnp.int32)
    part_rows = tok_rows // cores
    half_dim = HEAD_DIM // 2
    inv_freq = 10000.0 ** (-jnp.arange(half_dim, dtype=jnp.float32) / half_dim)
    freq = jnp.concatenate([inv_freq, inv_freq])[None, :]
    rotated = jax.ShapeDtypeStruct(q_proj.shape, jnp.bfloat16)
    rot_query, rot_keys = local_call(
        rope_kernel, [rotated] * 2, [place, prompt_lengths], [freq, q_proj, k_proj]
    )
    column = blk_index % PLANE
    key_blocks, value_blocks = [
        [block, next_plane(block)] for block in (rot_keys, after(v_proj, rot_keys))
    ]
    for blocks in (key_blocks, value_blocks):
        own, below = blocks
        for mask in range(1, PLANE):
            blocks.append(flipped(jnp.where(column < column ^ mask, own, below), mask))
    heads = q_proj.shape[1] // HEAD_DIM
    probs_shape = (heads, tok_rows, len(key_blocks) * tok_rows)
    probs = local_call(
        score_kernel,
        [jax.ShapeDtypeStruct(probs_shape, jnp.bfloat16)],
        [place, prompt_lengths],
        [rot_query, *key_blocks],
        flops=2 * tok_rows * probs_shape[2] * heads * HEAD_DIM,
    )[0]
    page_count = tok_rows // PAGE
    local_page = page_table - blk_index * page_count
    kv_rows = jnp.stack([rot_keys, v_proj], axis=1).reshape(page_count, PAGE, 2, -1)
    kv_pages = jnp.zeros_like(kv_rows).at[local_page].set(kv_rows)
    lanes = gate_lanes(expert_ids, gate_weights, experts)
    probs = after(probs, kv_pages, lanes)
    mixed = local_call(
        mix_kernel,
        [jax.ShapeDtypeStruct((tok_rows, model_width), jnp.float32)],
        [place],
        [probs, out_weight, residual, *value_blocks],
        flops=2 * tok_rows * (probs_shape[2] + model_width) * heads * HEAD_DIM,
    )[0]
    if cores == 2:
        addends = [mixed, from_core(mixed, 1)]
    else:
        addends = [lax.psum(mixed, "tok")]
    payload, own_share = local_call(
        norm_kernel,
        [
            jax.ShapeDtypeStruct((part_rows, model_width + lanes.shape[1]), jnp.bfloat16),
            jax.ShapeDtypeStruct((tok_rows, col_width), jnp.bfloat16),
        ],
        [place],
        [norm_gain[None, :], lanes, *addends],
    )
    weights = (w_gate[0].T, w_up[0].T, w_down[0])
    came = {0: payload}
    for ahead in range(1, planes):
        came[ahead] = from_plane(payload, ahead)
    if planes <= 4:
        groups = [[0]] + [sorted({i, planes - i}) for i in range(1, planes // 2 + 1)]
    else:
        groups = [[0]] + [list(range(i, min(i + 8, planes))) for i in range(1, planes, 8)]
    results = {}
    near_before = None
    done_before = None
    held = []
    for number, group in enumerate(groups):
        column = jnp.concatenate([came[ahead] for ahead in group])
        if near_before is not None:
            if number > 1:
                column = after(column, near_before)
            if planes > 4:
                column = after(column, done_before)
        near = jnp.concatenate([column, crossed(column, True)])
        far = crossed(near, False)
        near_before = near
        if planes > 4:
            done_before = expert_group(place, near, far, weights, experts, cores)
            held.append(done_before)
        else:
            held.append((near, far))
    if planes <= 4:
        held = [expert_group(place, near, far, weights, experts, cores) for near, far in held]
    for group, summed in zip(groups, held, strict=True):
        for i, ahead in enumerate(group):
            results[ahead] = jnp.concatenate(
                [total[i * part_rows : (i + 1) * part_rows] for total in summed]
            )
    moe = results[0]
    for ahead in range(1, planes):
        moe = moe + wide(to_plane(narrow(results[ahead]), ahead))
    moe = jnp.roll(moe.reshape(cores, part_rows, col_width), tok_index, axis=0)
    moe = moe.reshape(tok_rows, col_width)
    layer_out = (own_share.astype(jnp.float32) + moe).astype(jnp.bfloat16)
    return (layer_out, kv_pages)


def solution(mesh):
    placed = (
        P("blk", "tok"),
        P("blk", "tok"),
        P("blk", "tok"),
        P("blk", "tok"),
        P(),
        P("blk", None),
        P("blk", None),
        P("blk"),
        P("tok", None),
        P(),
        P("blk", None, "tok"),
        P("blk", None, "tok"),
        P("blk", "tok", None),
    )
    return jax.shard_map(
        on_device,
        mesh=mesh,
        in_specs=placed,
        out_specs=(P("blk", "tok"), P("blk", None, None, "tok")),
        check_vma=False,
    )
```

```python
import functools

import jax
import jax.numpy as jnp
from jax import lax
from jax.experimental import pallas as pl
from jax.experimental.pallas import tpu as pltpu
from jax.sharding import PartitionSpec as P

HEAD_DIM = 128
REACH = 4
PAGE = 16
PLANE = 4
EPSILON = 1e-06


def after(value, *others):
    return lax.optimization_barrier((value, *others))[0]


def flipped(block, mask):
    return lax.ppermute(block, "blk", [(i, i ^ mask) for i in range(lax.axis_size("blk"))])


def next_plane(block):
    count = lax.axis_size("blk")
    return lax.ppermute(block, "blk", [(i, i + PLANE) for i in range(count - PLANE)])


def from_plane(block, ahead):
    count = lax.axis_size("blk")
    return lax.ppermute(
        block, "blk", [((i + PLANE * ahead) % count, i) for i in range(count)]
    )


def to_plane(block, ahead):
    count = lax.axis_size("blk")
    return lax.ppermute(
        block, "blk", [(i, (i + PLANE * ahead) % count) for i in range(count)]
    )


def from_core(block, ahead):
    count = lax.axis_size("tok")
    return lax.ppermute(block, "tok", [((i + ahead) % count, i) for i in range(count)])


def segment_starts(place_ref, lengths_ref, shape):
    token = place_ref[0] * shape[0] + lax.broadcasted_iota(jnp.int32, shape, 0)
    start = jnp.zeros(shape, jnp.int32)
    end = jnp.int32(0)
    for i in range(lengths_ref.shape[0]):
        end = end + lengths_ref[i]
        start = jnp.where(token >= end, end, start)
    return token, start


def rope_kernel(place_ref, lengths_ref, freq_ref, q_ref, k_ref, q_out, k_out):
    rows, width = q_ref.shape
    shape = (rows, HEAD_DIM)
    token, start = segment_starts(place_ref, lengths_ref, shape)
    angle = (token - start).astype(jnp.float32) * freq_ref[...]
    cosine, sine = jnp.cos(angle), jnp.sin(angle)
    lane = lax.broadcasted_iota(jnp.int32, shape, 1)
    sine = jnp.where(lane < HEAD_DIM // 2, -sine, sine)
    for source, target in ((k_ref, k_out), (q_ref, q_out)):
        for head in range(width // HEAD_DIM):
            columns = slice(head * HEAD_DIM, (head + 1) * HEAD_DIM)
            x = source[:, columns].astype(jnp.float32)
            turned = x * cosine + pltpu.roll(x, HEAD_DIM // 2, 1) * sine
            target[:, columns] = turned.astype(jnp.bfloat16)


def score_kernel(place_ref, lengths_ref, q_ref, *rest):
    *keys, out_ref = rest
    rows, width = q_ref.shape
    shape = (rows, rows)
    token, start = segment_starts(place_ref, lengths_ref, shape)
    blk = place_ref[0]
    column = lax.rem(blk, PLANE)
    bases = [blk, blk - PLANE]
    for mask in range(1, PLANE):
        other = column ^ mask
        bases.append(blk - column + other - jnp.where(other > column, PLANE, 0))
    lane = lax.broadcasted_iota(jnp.int32, shape, 1)
    ids = jnp.concatenate([base * rows + lane for base in bases], axis=1)
    token = jnp.concatenate([token] * len(keys), axis=1)
    start = jnp.concatenate([start] * len(keys), axis=1)
    allowed = (ids >= start) & (ids <= token)
    for head in range(width // HEAD_DIM):
        columns = slice(head * HEAD_DIM, (head + 1) * HEAD_DIM)
        key = jnp.concatenate([ref[:, columns] for ref in keys], axis=0)
        scores = lax.dot_general(
            q_ref[:, columns],
            key,
            (((1,), (1,)), ((), ())),
            preferred_element_type=jnp.float32,
        )
        scores = jnp.where(allowed, scores * HEAD_DIM ** (-0.5), -1e30)
        terms = jnp.exp(scores - jnp.max(scores, axis=1, keepdims=True))
        share = 1.0 / jnp.sum(terms, axis=1, keepdims=True)
        out_ref[head] = (terms * share).astype(jnp.bfloat16)


def mix_kernel(place_ref, prob_ref, weight_ref, residual_ref, *rest):
    *values, out_ref = rest
    heads = prob_ref.shape[0]
    mixed = []
    for head in range(heads):
        columns = slice(head * HEAD_DIM, (head + 1) * HEAD_DIM)
        value = jnp.concatenate([ref[:, columns] for ref in values], axis=0)
        product = jnp.dot(prob_ref[head], value, preferred_element_type=jnp.float32)
        mixed.append(product.astype(jnp.bfloat16))
    attention = jnp.concatenate(mixed, axis=1)
    out_ref[...] = jnp.dot(attention, weight_ref[...], preferred_element_type=jnp.float32)
    width = residual_ref.shape[1]
    own = pl.ds(pl.multiple_of(place_ref[1] * width, 128), width)
    out_ref[:, own] = out_ref[:, own] + residual_ref[...].astype(jnp.float32)


def norm_kernel(place_ref, gain_ref, lanes_ref, *rest):
    *addends, rows_out, share_out = rest
    rows, width = addends[0].shape
    part_rows = rows_out.shape[0]
    part_width = share_out.shape[1]
    own = pl.ds(pl.multiple_of(place_ref[1] * part_width, 128), part_width)
    share_out[...] = sum(ref[:, own] for ref in addends).astype(jnp.bfloat16)
    part = pl.ds(pl.multiple_of(place_ref[1] * part_rows, 16), part_rows)
    stream = sum(ref[part, :] for ref in addends).astype(jnp.bfloat16).astype(jnp.float32)
    scale = lax.rsqrt(jnp.mean(stream * stream, axis=1, keepdims=True) + EPSILON)
    rows_out[:, :width] = (stream * scale * gain_ref[...]).astype(jnp.bfloat16)
    rows_out[:, width:] = lanes_ref[part, :]


def local_call(body, out_shapes, scalars, arrays, flops=0, limit=16):
    whole = pl.BlockSpec(memory_space=pltpu.VMEM)
    scalar = pl.BlockSpec(memory_space=pltpu.SMEM)
    moved = sum(x.size * x.dtype.itemsize for x in (*arrays, *out_shapes))
    return pl.pallas_call(
        body,
        in_specs=[scalar] * len(scalars) + [whole] * len(arrays),
        out_specs=[whole] * len(out_shapes),
        out_shape=out_shapes,
        cost_estimate=pl.CostEstimate(flops=flops, bytes_accessed=moved, transcendentals=0),
        compiler_params=pltpu.CompilerParams(vmem_limit_bytes=limit << 20),
    )(*scalars, *arrays)


def gate_lanes(expert_ids, gate_weights, experts):
    hits = expert_ids[:, :, None] == jnp.arange(experts, dtype=jnp.int32)[None, None, :]
    gates = jnp.sum(jnp.where(hits, gate_weights[:, :, None], 0.0), axis=1)
    pieces = []
    for _ in range(3):
        piece = lax.reduce_precision(gates, 8, 7)
        pieces.append(piece.astype(jnp.bfloat16))
        gates = gates - piece
    lanes = jnp.concatenate(pieces, axis=1)
    return jnp.pad(lanes, ((0, 0), (0, -lanes.shape[1] % 128)))


def crossed(block, first):
    cores, count = lax.axis_size("tok"), lax.axis_size("blk")
    route = []
    for core in range(cores):
        mask = 1 if (core % 2 == 0) == first else 2
        route += [(core * count + i, core * count + (i ^ mask)) for i in range(count)]
    return lax.ppermute(block, ("tok", "blk"), route)


def expert_kernel(experts, ahead, place_ref, near_ref, far_ref, gate_ref, up_ref, down_ref, *outs):
    width = gate_ref.shape[1]
    parts = len(outs)
    blocks, part_rows, part_width = outs[0].shape
    held = jnp.concatenate([near_ref[...], far_ref[...]], axis=0)
    rows = held[:, :width]
    lanes = held[:, width:].astype(jnp.float32)
    lane_ids = lax.broadcasted_iota(jnp.int32, lanes.shape, 1)
    named = (lane_ids < 3 * experts) & (lane_ids % experts == place_ref[0])
    weight = jnp.sum(jnp.where(named, lanes, 0.0), axis=1, keepdims=True)
    turned = (((1,), (1,)), ((), ()))
    gate_act = lax.dot_general(rows, gate_ref[...], turned, preferred_element_type=jnp.float32)
    up_act = lax.dot_general(rows, up_ref[...], turned, preferred_element_type=jnp.float32)
    hidden = (gate_act / (1.0 + jnp.exp(-gate_act)) * up_act).astype(jnp.bfloat16)
    for part in range(parts):
        start = lax.rem(place_ref[1] + part, parts) * part_width
        columns = pl.ds(pl.multiple_of(start, 128), part_width)
        product = jnp.dot(hidden, down_ref[:, columns], preferred_element_type=jnp.float32)
        product = (weight * product).astype(jnp.bfloat16)
        order = (0, 2, 1, 3) if (part - ahead) % 2 else (0, 1, 2, 3)
        for block in range(blocks):
            outs[part][order[block]] = product[block * part_rows : (block + 1) * part_rows]


def run_expert(place, near, far, w_gate, w_up, w_down, experts, parts, ahead):
    count = 2 * near.shape[0]
    units, width = w_gate.shape
    out_shape = jax.ShapeDtypeStruct((PLANE, count // PLANE, width // parts), jnp.bfloat16)
    return local_call(
        functools.partial(expert_kernel, experts, ahead),
        [out_shape] * parts,
        [place],
        [near, far, w_gate, w_up, w_down],
        flops=6 * count * width * units,
    )


def wide(block):
    return block.astype(jnp.float32)


def narrow(block):
    return block.astype(jnp.bfloat16)


def second_share(totals):
    return narrow(jnp.stack([total[2:4] for total in totals]))


def first_share(totals):
    return narrow(jnp.stack([total[1] for total in totals]))


def merged(totals, got, count):
    return [total[0:count] + wide(got[i]) for i, total in enumerate(totals)]


def expert_outputs(place, near, far, weights, experts, cores, waits):
    outs = []
    for ahead in range(cores):
        near_rows = from_core(near, ahead) if ahead else near
        far_rows = from_core(far, ahead) if ahead else far
        near_rows = after(near_rows, *outs[-1:], *waits.get(ahead, []))
        outs.append(run_expert(place, near_rows, far_rows, *weights, experts, cores, ahead))
    return outs


def core_totals(outs, cores):
    totals = []
    for rows_of in range(cores):
        total = wide(outs[rows_of][0])
        for ahead in range(1, cores):
            sent = outs[(rows_of + ahead) % cores][ahead]
            total = total + wide(from_core(sent, cores - ahead))
        totals.append(total)
    return totals


def on_device(
    q_proj,
    k_proj,
    v_proj,
    residual,
    prompt_lengths,
    expert_ids,
    gate_weights,
    page_table,
    out_weight,
    norm_gain,
    w_gate,
    w_up,
    w_down,
):
    tok_rows = q_proj.shape[0]
    col_width = residual.shape[1]
    model_width = norm_gain.shape[0]
    blk_index = lax.axis_index("blk")
    tok_index = lax.axis_index("tok")
    cores = lax.axis_size("tok")
    experts = lax.axis_size("blk")
    planes = experts // PLANE
    place = jnp.stack([blk_index, tok_index]).astype(jnp.int32)
    part_rows = tok_rows // cores
    half_dim = HEAD_DIM // 2
    inv_freq = 10000.0 ** (-jnp.arange(half_dim, dtype=jnp.float32) / half_dim)
    freq = jnp.concatenate([inv_freq, inv_freq])[None, :]
    rotated = jax.ShapeDtypeStruct(q_proj.shape, jnp.bfloat16)
    rot_query, rot_keys = local_call(
        rope_kernel, [rotated] * 2, [place, prompt_lengths], [freq, q_proj, k_proj]
    )
    column = blk_index % PLANE
    key_blocks, value_blocks = [
        [block, next_plane(block)] for block in (rot_keys, after(v_proj, rot_keys))
    ]
    for blocks in (key_blocks, value_blocks):
        own, below = blocks
        for mask in range(1, PLANE):
            blocks.append(flipped(jnp.where(column < column ^ mask, own, below), mask))
    heads = q_proj.shape[1] // HEAD_DIM
    probs_shape = (heads, tok_rows, len(key_blocks) * tok_rows)
    probs = local_call(
        score_kernel,
        [jax.ShapeDtypeStruct(probs_shape, jnp.bfloat16)],
        [place, prompt_lengths],
        [rot_query, *key_blocks],
        flops=2 * tok_rows * probs_shape[2] * heads * HEAD_DIM,
    )[0]
    page_count = tok_rows // PAGE
    local_page = page_table - blk_index * page_count
    kv_rows = jnp.stack([rot_keys, v_proj], axis=1).reshape(page_count, PAGE, 2, -1)
    kv_pages = jnp.zeros_like(kv_rows).at[local_page].set(kv_rows)
    lanes = gate_lanes(expert_ids, gate_weights, experts)
    probs = after(probs, kv_pages, lanes)
    mixed = local_call(
        mix_kernel,
        [jax.ShapeDtypeStruct((tok_rows, model_width), jnp.float32)],
        [place],
        [probs, out_weight, residual, *value_blocks],
        flops=2 * tok_rows * (probs_shape[2] + model_width) * heads * HEAD_DIM,
    )[0]
    if cores == 2:
        addends = [mixed, from_core(mixed, 1)]
    else:
        addends = [lax.psum(mixed, "tok")]
    payload, own_share = local_call(
        norm_kernel,
        [
            jax.ShapeDtypeStruct((part_rows, model_width + lanes.shape[1]), jnp.bfloat16),
            jax.ShapeDtypeStruct((tok_rows, col_width), jnp.bfloat16),
        ],
        [place],
        [norm_gain[None, :], lanes, *addends],
    )
    weights = (w_gate[0].T, w_up[0].T, w_down[0])
    if planes <= 4:
        groups = [[0]] + [sorted({i, planes - i}) for i in range(1, planes // 2 + 1)]
    else:
        groups = [[0]] + [list(range(i, min(i + 8, planes))) for i in range(1, planes, 8)]
    nears, fars = [], []
    for number, group in enumerate(groups):
        sent = after(payload, nears[0]) if number > 1 else payload
        column = jnp.concatenate([from_plane(sent, ahead) if ahead else sent for ahead in group])
        if number > 1:
            column = after(column, nears[-1])
        nears.append(jnp.concatenate([column, crossed(column, True)]))
        fars.append(crossed(nears[-1], False))
    weights = (w_gate[0].T, w_up[0].T, w_down[0])
    run = functools.partial(
        expert_outputs, place, weights=weights, experts=experts, cores=cores
    )
    outs = run(nears[0], fars[0], waits={})
    own_totals = core_totals(outs, cores)
    got = crossed(after(second_share(own_totals), nears[-1]), False)
    own_totals = merged(own_totals, got, 2)
    own_got = crossed(first_share(own_totals), True)
    totals, sents = [], []
    for number in range(1, len(groups)):
        waits = {0: [outs]}
        if number == len(groups) - 1:
            waits = {0: [outs, got], cores - 1: [own_got, *sents]}
        outs = run(nears[number], fars[number], waits=waits)
        totals.append(core_totals(outs, cores))
        sents.append(second_share(totals[-1]))
    gots = [crossed(sent, False) for sent in sents]
    totals = [merged(*pair, 2) for pair in zip(totals, gots, strict=True)]
    gots = [crossed(first_share(pair), True) for pair in totals]
    results = {}
    for group, pair, came in zip(
        groups, [own_totals, *totals], [own_got, *gots], strict=True
    ):
        rows_of = merged([total[0] for total in pair], came, None)
        for i, ahead in enumerate(group):
            results[ahead] = jnp.concatenate(
                [rows[i * part_rows : (i + 1) * part_rows] for rows in rows_of]
            )
    moe = results[0]
    for ahead in range(1, planes):
        moe = moe + wide(to_plane(narrow(results[ahead]), ahead))
    moe = jnp.roll(moe.reshape(cores, part_rows, col_width), tok_index, axis=0)
    moe = moe.reshape(tok_rows, col_width)
    layer_out = (own_share.astype(jnp.float32) + moe).astype(jnp.bfloat16)
    return (layer_out, kv_pages)


def solution(mesh):
    placed = (
        P("blk", "tok"),
        P("blk", "tok"),
        P("blk", "tok"),
        P("blk", "tok"),
        P(),
        P("blk", None),
        P("blk", None),
        P("blk"),
        P("tok", None),
        P(),
        P("blk", None, "tok"),
        P("blk", None, "tok"),
        P("blk", "tok", None),
    )
    return jax.shard_map(
        on_device,
        mesh=mesh,
        in_specs=placed,
        out_specs=(P("blk", "tok"), P("blk", None, None, "tok")),
        check_vma=False,
    )
```

```python
import functools

import jax
import jax.numpy as jnp
from jax import lax
from jax.experimental import pallas as pl
from jax.experimental.pallas import tpu as pltpu
from jax.sharding import PartitionSpec as P

HEAD_DIM = 128
REACH = 4
PAGE = 16
PLANE = 4
EPSILON = 1e-06


def after(value, *others):
    return lax.optimization_barrier((value, *others))[0]


def flipped(block, mask):
    return lax.ppermute(block, "blk", [(i, i ^ mask) for i in range(lax.axis_size("blk"))])


def next_plane(block):
    count = lax.axis_size("blk")
    return lax.ppermute(block, "blk", [(i, i + PLANE) for i in range(count - PLANE)])


def from_plane(block, ahead):
    count = lax.axis_size("blk")
    return lax.ppermute(
        block, "blk", [((i + PLANE * ahead) % count, i) for i in range(count)]
    )


def to_plane(block, ahead):
    count = lax.axis_size("blk")
    return lax.ppermute(
        block, "blk", [(i, (i + PLANE * ahead) % count) for i in range(count)]
    )


def from_core(block, ahead):
    count = lax.axis_size("tok")
    return lax.ppermute(block, "tok", [((i + ahead) % count, i) for i in range(count)])


def segment_starts(place_ref, lengths_ref, shape):
    token = place_ref[0] * shape[0] + lax.broadcasted_iota(jnp.int32, shape, 0)
    start = jnp.zeros(shape, jnp.int32)
    end = jnp.int32(0)
    for i in range(lengths_ref.shape[0]):
        end = end + lengths_ref[i]
        start = jnp.where(token >= end, end, start)
    return token, start


def rope_kernel(place_ref, lengths_ref, freq_ref, q_ref, k_ref, q_out, k_out):
    rows, width = q_ref.shape
    shape = (rows, HEAD_DIM)
    token, start = segment_starts(place_ref, lengths_ref, shape)
    angle = (token - start).astype(jnp.float32) * freq_ref[...]
    cosine, sine = jnp.cos(angle), jnp.sin(angle)
    lane = lax.broadcasted_iota(jnp.int32, shape, 1)
    sine = jnp.where(lane < HEAD_DIM // 2, -sine, sine)
    for source, target in ((k_ref, k_out), (q_ref, q_out)):
        for head in range(width // HEAD_DIM):
            columns = slice(head * HEAD_DIM, (head + 1) * HEAD_DIM)
            x = source[:, columns].astype(jnp.float32)
            turned = x * cosine + pltpu.roll(x, HEAD_DIM // 2, 1) * sine
            target[:, columns] = turned.astype(jnp.bfloat16)


def score_kernel(place_ref, lengths_ref, q_ref, *rest):
    *keys, out_ref = rest
    rows, width = q_ref.shape
    shape = (rows, rows)
    token, start = segment_starts(place_ref, lengths_ref, shape)
    blk = place_ref[0]
    column = lax.rem(blk, PLANE)
    bases = [blk, blk - PLANE]
    for mask in range(1, PLANE):
        other = column ^ mask
        bases.append(blk - column + other - jnp.where(other > column, PLANE, 0))
    lane = lax.broadcasted_iota(jnp.int32, shape, 1)
    ids = jnp.concatenate([base * rows + lane for base in bases], axis=1)
    token = jnp.concatenate([token] * len(keys), axis=1)
    start = jnp.concatenate([start] * len(keys), axis=1)
    allowed = (ids >= start) & (ids <= token)
    for head in range(width // HEAD_DIM):
        columns = slice(head * HEAD_DIM, (head + 1) * HEAD_DIM)
        key = jnp.concatenate([ref[:, columns] for ref in keys], axis=0)
        scores = lax.dot_general(
            q_ref[:, columns],
            key,
            (((1,), (1,)), ((), ())),
            preferred_element_type=jnp.float32,
        )
        scores = jnp.where(allowed, scores * HEAD_DIM ** (-0.5), -1e30)
        terms = jnp.exp(scores - jnp.max(scores, axis=1, keepdims=True))
        share = 1.0 / jnp.sum(terms, axis=1, keepdims=True)
        out_ref[head] = (terms * share).astype(jnp.bfloat16)


def mix_kernel(place_ref, prob_ref, weight_ref, residual_ref, *rest):
    *values, out_ref = rest
    heads = prob_ref.shape[0]
    mixed = []
    for head in range(heads):
        columns = slice(head * HEAD_DIM, (head + 1) * HEAD_DIM)
        value = jnp.concatenate([ref[:, columns] for ref in values], axis=0)
        product = jnp.dot(prob_ref[head], value, preferred_element_type=jnp.float32)
        mixed.append(product.astype(jnp.bfloat16))
    attention = jnp.concatenate(mixed, axis=1)
    out_ref[...] = jnp.dot(attention, weight_ref[...], preferred_element_type=jnp.float32)
    width = residual_ref.shape[1]
    own = pl.ds(pl.multiple_of(place_ref[1] * width, 128), width)
    out_ref[:, own] = out_ref[:, own] + residual_ref[...].astype(jnp.float32)


def norm_kernel(place_ref, gain_ref, lanes_ref, *rest):
    *addends, rows_out, share_out = rest
    rows, width = addends[0].shape
    part_rows = rows_out.shape[0]
    part_width = share_out.shape[1]
    own = pl.ds(pl.multiple_of(place_ref[1] * part_width, 128), part_width)
    share_out[...] = sum(ref[:, own] for ref in addends).astype(jnp.bfloat16)
    part = pl.ds(pl.multiple_of(place_ref[1] * part_rows, 16), part_rows)
    stream = sum(ref[part, :] for ref in addends).astype(jnp.bfloat16).astype(jnp.float32)
    scale = lax.rsqrt(jnp.mean(stream * stream, axis=1, keepdims=True) + EPSILON)
    rows_out[:, :width] = (stream * scale * gain_ref[...]).astype(jnp.bfloat16)
    rows_out[:, width:] = lanes_ref[part, :]


def local_call(body, out_shapes, scalars, arrays, flops=0, moved=0, limit=16):
    whole = pl.BlockSpec(memory_space=pltpu.VMEM)
    scalar = pl.BlockSpec(memory_space=pltpu.SMEM)
    moved = moved or sum(x.size * x.dtype.itemsize for x in (*arrays, *out_shapes))
    return pl.pallas_call(
        body,
        in_specs=[scalar] * len(scalars) + [whole] * len(arrays),
        out_specs=[whole] * len(out_shapes),
        out_shape=out_shapes,
        cost_estimate=pl.CostEstimate(flops=flops, bytes_accessed=moved, transcendentals=0),
        compiler_params=pltpu.CompilerParams(vmem_limit_bytes=limit << 20),
    )(*scalars, *arrays)


def gate_lanes(expert_ids, gate_weights, experts):
    hits = expert_ids[:, :, None] == jnp.arange(experts, dtype=jnp.int32)[None, None, :]
    gates = jnp.sum(jnp.where(hits, gate_weights[:, :, None], 0.0), axis=1)
    pieces = []
    for _ in range(3):
        piece = lax.reduce_precision(gates, 8, 7)
        pieces.append(piece.astype(jnp.bfloat16))
        gates = gates - piece
    lanes = jnp.concatenate(pieces, axis=1)
    return jnp.pad(lanes, ((0, 0), (0, -lanes.shape[1] % 128)))


def crossed(block, first):
    cores, count = lax.axis_size("tok"), lax.axis_size("blk")
    route = []
    for core in range(cores):
        mask = 1 if (core % 2 == 0) == first else 2
        route += [(core * count + i, core * count + (i ^ mask)) for i in range(count)]
    return lax.ppermute(block, ("tok", "blk"), route)


def expert_kernel(experts, ahead, place_ref, near_ref, far_ref, gate_ref, up_ref, down_ref, *outs):
    width = gate_ref.shape[1]
    parts = len(outs)
    blocks, part_rows, part_width = outs[0].shape
    held = jnp.concatenate([near_ref[...], far_ref[...]], axis=0)
    rows = held[:, :width]
    lanes = held[:, width:].astype(jnp.float32)
    lane_ids = lax.broadcasted_iota(jnp.int32, lanes.shape, 1)
    named = (lane_ids < 3 * experts) & (lane_ids % experts == place_ref[0])
    weight = jnp.sum(jnp.where(named, lanes, 0.0), axis=1, keepdims=True)
    turned = (((1,), (1,)), ((), ()))
    gate_act = lax.dot_general(rows, gate_ref[...], turned, preferred_element_type=jnp.float32)
    up_act = lax.dot_general(rows, up_ref[...], turned, preferred_element_type=jnp.float32)
    hidden = (gate_act / (1.0 + jnp.exp(-gate_act)) * up_act).astype(jnp.bfloat16)
    for part in range(parts):
        start = lax.rem(place_ref[1] + part, parts) * part_width
        columns = pl.ds(pl.multiple_of(start, 128), part_width)
        product = jnp.dot(hidden, down_ref[:, columns], preferred_element_type=jnp.float32)
        product = (weight * product).astype(jnp.bfloat16)
        order = (0, 2, 1, 3) if (part - ahead) % 2 else (0, 1, 2, 3)
        for block in range(blocks):
            outs[part][order[block]] = product[block * part_rows : (block + 1) * part_rows]


def run_expert(place, near, far, w_gate, w_up, w_down, experts, parts, ahead):
    count = 2 * near.shape[0]
    units, width = w_gate.shape
    out_shape = jax.ShapeDtypeStruct((PLANE, count // PLANE, width // parts), jnp.bfloat16)
    return local_call(
        functools.partial(expert_kernel, experts, ahead),
        [out_shape] * parts,
        [place],
        [near, far, w_gate, w_up, w_down],
        flops=count,
        moved=count,
    )


def wide(block):
    return block.astype(jnp.float32)


def narrow(block):
    return block.astype(jnp.bfloat16)


def second_share(totals):
    return narrow(jnp.stack([total[2:4] for total in totals]))


def first_share(totals):
    return narrow(jnp.stack([total[1] for total in totals]))


def merged(totals, got, count):
    return [total[0:count] + wide(got[i]) for i, total in enumerate(totals)]


def expert_outputs(place, near, far, weights, experts, cores, waits):
    outs = []
    for ahead in range(cores):
        near_rows = from_core(near, ahead) if ahead else near
        far_rows = from_core(far, ahead) if ahead else far
        near_rows = after(near_rows, *outs[-1:], *waits.get(ahead, []))
        outs.append(run_expert(place, near_rows, far_rows, *weights, experts, cores, ahead))
    return outs


def core_totals(outs, cores):
    totals = []
    for rows_of in range(cores):
        total = wide(outs[rows_of][0])
        for ahead in range(1, cores):
            sent = outs[(rows_of + ahead) % cores][ahead]
            total = total + wide(from_core(sent, cores - ahead))
        totals.append(total)
    return totals


def on_device(
    q_proj,
    k_proj,
    v_proj,
    residual,
    prompt_lengths,
    expert_ids,
    gate_weights,
    page_table,
    out_weight,
    norm_gain,
    w_gate,
    w_up,
    w_down,
):
    tok_rows = q_proj.shape[0]
    col_width = residual.shape[1]
    model_width = norm_gain.shape[0]
    blk_index = lax.axis_index("blk")
    tok_index = lax.axis_index("tok")
    cores = lax.axis_size("tok")
    experts = lax.axis_size("blk")
    planes = experts // PLANE
    place = jnp.stack([blk_index, tok_index]).astype(jnp.int32)
    part_rows = tok_rows // cores
    half_dim = HEAD_DIM // 2
    inv_freq = 10000.0 ** (-jnp.arange(half_dim, dtype=jnp.float32) / half_dim)
    freq = jnp.concatenate([inv_freq, inv_freq])[None, :]
    rotated = jax.ShapeDtypeStruct(q_proj.shape, jnp.bfloat16)
    rot_query, rot_keys = local_call(
        rope_kernel, [rotated] * 2, [place, prompt_lengths], [freq, q_proj, k_proj]
    )
    column = blk_index % PLANE
    key_blocks, value_blocks = [
        [block, next_plane(block)] for block in (rot_keys, after(v_proj, rot_keys))
    ]
    for blocks in (key_blocks, value_blocks):
        own, below = blocks
        for mask in range(1, PLANE):
            blocks.append(flipped(jnp.where(column < column ^ mask, own, below), mask))
    heads = q_proj.shape[1] // HEAD_DIM
    probs_shape = (heads, tok_rows, len(key_blocks) * tok_rows)
    probs = local_call(
        score_kernel,
        [jax.ShapeDtypeStruct(probs_shape, jnp.bfloat16)],
        [place, prompt_lengths],
        [rot_query, *key_blocks],
        flops=2 * tok_rows * probs_shape[2] * heads * HEAD_DIM,
    )[0]
    page_count = tok_rows // PAGE
    local_page = page_table - blk_index * page_count
    kv_rows = jnp.stack([rot_keys, v_proj], axis=1).reshape(page_count, PAGE, 2, -1)
    kv_pages = jnp.zeros_like(kv_rows).at[local_page].set(kv_rows)
    lanes = gate_lanes(expert_ids, gate_weights, experts)
    probs = after(probs, kv_pages, lanes)
    mixed = local_call(
        mix_kernel,
        [jax.ShapeDtypeStruct((tok_rows, model_width), jnp.float32)],
        [place],
        [probs, out_weight, residual, *value_blocks],
        flops=2 * tok_rows * (probs_shape[2] + model_width) * heads * HEAD_DIM,
    )[0]
    if cores == 2:
        addends = [mixed, from_core(mixed, 1)]
    else:
        addends = [lax.psum(mixed, "tok")]
    payload, own_share = local_call(
        norm_kernel,
        [
            jax.ShapeDtypeStruct((part_rows, model_width + lanes.shape[1]), jnp.bfloat16),
            jax.ShapeDtypeStruct((tok_rows, col_width), jnp.bfloat16),
        ],
        [place],
        [norm_gain[None, :], lanes, *addends],
    )
    weights = (w_gate[0].T, w_up[0].T, w_down[0])
    if planes <= 4:
        groups = [[0]] + [sorted({i, planes - i}) for i in range(planes // 2, 0, -1)]
    else:
        groups = [[0]] + [list(range(i, min(i + 8, planes))) for i in range(1, planes, 8)]
    nears, fars = [], []
    for number, group in enumerate(groups):
        sent = after(payload, nears[0]) if number > 1 else payload
        column = jnp.concatenate([from_plane(sent, ahead) if ahead else sent for ahead in group])
        if number > 1:
            column = after(column, nears[-1])
        nears.append(jnp.concatenate([column, crossed(column, True)]))
        fars.append(crossed(after(nears[-1], *fars[-1:]), False))
    weights = (w_gate[0].T, w_up[0].T, w_down[0])
    run = functools.partial(
        expert_outputs, place, weights=weights, experts=experts, cores=cores
    )
    outs = run(nears[0], fars[0], waits={})
    own_totals = core_totals(outs, cores)
    own_sent = sent = second_share(own_totals)
    partial = {}
    shared = None
    for number in range(1, len(groups)):
        outs = run(nears[number], fars[number], waits={0: [outs], cores - 1: [sent]})
        totals = core_totals(outs, cores)
        if shared is not None:
            totals = [after(total, shared) for total in totals]
        sent = second_share(totals)
        totals = merged(totals, crossed(sent, False), 2)
        shared = first_share(totals)
        partial[number] = (totals, crossed(shared, True))
    totals = merged(own_totals, crossed(after(own_sent, shared), False), 2)
    partial[0] = (totals, crossed(first_share(totals), True))
    results = {}
    for number, group in enumerate(groups):
        totals, came = partial[number]
        rows_of = merged([total[0] for total in totals], came, None)
        for i, ahead in enumerate(group):
            results[ahead] = jnp.concatenate(
                [rows[i * part_rows : (i + 1) * part_rows] for rows in rows_of]
            )
    moe = results[0]
    for ahead in range(1, planes):
        moe = moe + wide(to_plane(narrow(results[ahead]), ahead))
    moe = jnp.roll(moe.reshape(cores, part_rows, col_width), tok_index, axis=0)
    moe = moe.reshape(tok_rows, col_width)
    layer_out = (own_share.astype(jnp.float32) + moe).astype(jnp.bfloat16)
    return (layer_out, kv_pages)


def solution(mesh):
    placed = (
        P("blk", "tok"),
        P("blk", "tok"),
        P("blk", "tok"),
        P("blk", "tok"),
        P(),
        P("blk", None),
        P("blk", None),
        P("blk"),
        P("tok", None),
        P(),
        P("blk", None, "tok"),
        P("blk", None, "tok"),
        P("blk", "tok", None),
    )
    return jax.shard_map(
        on_device,
        mesh=mesh,
        in_specs=placed,
        out_specs=(P("blk", "tok"), P("blk", None, None, "tok")),
        check_vma=False,
    )
```

```python
import functools

import jax
import jax.numpy as jnp
from jax import lax
from jax.experimental import pallas as pl
from jax.experimental.pallas import tpu as pltpu
from jax.sharding import PartitionSpec as P

HEAD_DIM = 128
REACH = 4
PAGE = 16
PLANE = 4
EPSILON = 1e-06


def after(value, *others):
    return lax.optimization_barrier((value, *others))[0]


def flipped(block, mask):
    return lax.ppermute(block, "blk", [(i, i ^ mask) for i in range(lax.axis_size("blk"))])


def next_plane(block):
    count = lax.axis_size("blk")
    return lax.ppermute(block, "blk", [(i, i + PLANE) for i in range(count - PLANE)])


def from_plane(block, ahead):
    count = lax.axis_size("blk")
    return lax.ppermute(
        block, "blk", [((i + PLANE * ahead) % count, i) for i in range(count)]
    )


def to_plane(block, ahead):
    count = lax.axis_size("blk")
    return lax.ppermute(
        block, "blk", [(i, (i + PLANE * ahead) % count) for i in range(count)]
    )


def from_core(block, ahead):
    count = lax.axis_size("tok")
    return lax.ppermute(block, "tok", [((i + ahead) % count, i) for i in range(count)])


def segment_starts(place_ref, lengths_ref, shape):
    token = place_ref[0] * shape[0] + lax.broadcasted_iota(jnp.int32, shape, 0)
    start = jnp.zeros(shape, jnp.int32)
    end = jnp.int32(0)
    for i in range(lengths_ref.shape[0]):
        end = end + lengths_ref[i]
        start = jnp.where(token >= end, end, start)
    return token, start


def rope_kernel(place_ref, lengths_ref, freq_ref, q_ref, k_ref, q_out, k_out):
    rows, width = q_ref.shape
    shape = (rows, HEAD_DIM)
    token, start = segment_starts(place_ref, lengths_ref, shape)
    angle = (token - start).astype(jnp.float32) * freq_ref[...]
    cosine, sine = jnp.cos(angle), jnp.sin(angle)
    lane = lax.broadcasted_iota(jnp.int32, shape, 1)
    sine = jnp.where(lane < HEAD_DIM // 2, -sine, sine)
    for source, target in ((k_ref, k_out), (q_ref, q_out)):
        for head in range(width // HEAD_DIM):
            columns = slice(head * HEAD_DIM, (head + 1) * HEAD_DIM)
            x = source[:, columns].astype(jnp.float32)
            turned = x * cosine + pltpu.roll(x, HEAD_DIM // 2, 1) * sine
            target[:, columns] = turned.astype(jnp.bfloat16)


def score_kernel(place_ref, lengths_ref, q_ref, *rest):
    *keys, out_ref = rest
    rows, width = q_ref.shape
    shape = (rows, rows)
    token, start = segment_starts(place_ref, lengths_ref, shape)
    blk = place_ref[0]
    column = lax.rem(blk, PLANE)
    bases = [blk, blk - PLANE]
    for mask in range(1, PLANE):
        other = column ^ mask
        bases.append(blk - column + other - jnp.where(other > column, PLANE, 0))
    lane = lax.broadcasted_iota(jnp.int32, shape, 1)
    ids = jnp.concatenate([base * rows + lane for base in bases], axis=1)
    token = jnp.concatenate([token] * len(keys), axis=1)
    start = jnp.concatenate([start] * len(keys), axis=1)
    allowed = (ids >= start) & (ids <= token)
    for head in range(width // HEAD_DIM):
        columns = slice(head * HEAD_DIM, (head + 1) * HEAD_DIM)
        key = jnp.concatenate([ref[:, columns] for ref in keys], axis=0)
        scores = lax.dot_general(
            q_ref[:, columns],
            key,
            (((1,), (1,)), ((), ())),
            preferred_element_type=jnp.float32,
        )
        scores = jnp.where(allowed, scores * HEAD_DIM ** (-0.5), -1e30)
        terms = jnp.exp(scores - jnp.max(scores, axis=1, keepdims=True))
        share = 1.0 / jnp.sum(terms, axis=1, keepdims=True)
        out_ref[head] = (terms * share).astype(jnp.bfloat16)


def mix_kernel(place_ref, prob_ref, weight_ref, residual_ref, *rest):
    *values, out_ref = rest
    heads = prob_ref.shape[0]
    mixed = []
    for head in range(heads):
        columns = slice(head * HEAD_DIM, (head + 1) * HEAD_DIM)
        value = jnp.concatenate([ref[:, columns] for ref in values], axis=0)
        product = jnp.dot(prob_ref[head], value, preferred_element_type=jnp.float32)
        mixed.append(product.astype(jnp.bfloat16))
    attention = jnp.concatenate(mixed, axis=1)
    out_ref[...] = jnp.dot(attention, weight_ref[...], preferred_element_type=jnp.float32)
    width = residual_ref.shape[1]
    own = pl.ds(pl.multiple_of(place_ref[1] * width, 128), width)
    out_ref[:, own] = out_ref[:, own] + residual_ref[...].astype(jnp.float32)


def norm_kernel(place_ref, gain_ref, lanes_ref, *rest):
    *addends, rows_out, share_out = rest
    rows, width = addends[0].shape
    part_rows = rows_out.shape[0]
    part_width = share_out.shape[1]
    own = pl.ds(pl.multiple_of(place_ref[1] * part_width, 128), part_width)
    share_out[...] = sum(ref[:, own] for ref in addends).astype(jnp.bfloat16)
    part = pl.ds(pl.multiple_of(place_ref[1] * part_rows, 16), part_rows)
    stream = sum(ref[part, :] for ref in addends).astype(jnp.bfloat16).astype(jnp.float32)
    scale = lax.rsqrt(jnp.mean(stream * stream, axis=1, keepdims=True) + EPSILON)
    rows_out[:, :width] = (stream * scale * gain_ref[...]).astype(jnp.bfloat16)
    rows_out[:, width:] = lanes_ref[part, :]


def local_call(body, out_shapes, scalars, arrays, flops=0, moved=0, limit=16):
    whole = pl.BlockSpec(memory_space=pltpu.VMEM)
    scalar = pl.BlockSpec(memory_space=pltpu.SMEM)
    moved = moved or sum(x.size * x.dtype.itemsize for x in (*arrays, *out_shapes))
    return pl.pallas_call(
        body,
        in_specs=[scalar] * len(scalars) + [whole] * len(arrays),
        out_specs=[whole] * len(out_shapes),
        out_shape=out_shapes,
        cost_estimate=pl.CostEstimate(flops=flops, bytes_accessed=moved, transcendentals=0),
        compiler_params=pltpu.CompilerParams(vmem_limit_bytes=limit << 20),
    )(*scalars, *arrays)


def gate_lanes(expert_ids, gate_weights, experts):
    hits = expert_ids[:, :, None] == jnp.arange(experts, dtype=jnp.int32)[None, None, :]
    gates = jnp.sum(jnp.where(hits, gate_weights[:, :, None], 0.0), axis=1)
    pieces = []
    for _ in range(3):
        piece = lax.reduce_precision(gates, 8, 7)
        pieces.append(piece.astype(jnp.bfloat16))
        gates = gates - piece
    lanes = jnp.concatenate(pieces, axis=1)
    return jnp.pad(lanes, ((0, 0), (0, -lanes.shape[1] % 128)))


def crossed(block, first):
    cores, count = lax.axis_size("tok"), lax.axis_size("blk")
    route = []
    for core in range(cores):
        mask = 1 if (core % 2 == 0) == first else 2
        route += [(core * count + i, core * count + (i ^ mask)) for i in range(count)]
    return lax.ppermute(block, ("tok", "blk"), route)


def expert_kernel(experts, ahead, place_ref, near_ref, far_ref, gate_ref, up_ref, down_ref, *outs):
    width = gate_ref.shape[1]
    parts = len(outs)
    blocks, part_rows, part_width = outs[0].shape
    held = jnp.concatenate([near_ref[...], far_ref[...]], axis=0)
    rows = held[:, :width]
    lanes = held[:, width:].astype(jnp.float32)
    lane_ids = lax.broadcasted_iota(jnp.int32, lanes.shape, 1)
    named = (lane_ids < 3 * experts) & (lane_ids % experts == place_ref[0])
    weight = jnp.sum(jnp.where(named, lanes, 0.0), axis=1, keepdims=True)
    turned = (((1,), (1,)), ((), ()))
    gate_act = lax.dot_general(rows, gate_ref[...], turned, preferred_element_type=jnp.float32)
    up_act = lax.dot_general(rows, up_ref[...], turned, preferred_element_type=jnp.float32)
    hidden = (gate_act / (1.0 + jnp.exp(-gate_act)) * up_act).astype(jnp.bfloat16)
    for part in range(parts):
        start = lax.rem(place_ref[1] + part, parts) * part_width
        columns = pl.ds(pl.multiple_of(start, 128), part_width)
        product = jnp.dot(hidden, down_ref[:, columns], preferred_element_type=jnp.float32)
        product = (weight * product).astype(jnp.bfloat16)
        order = (0, 2, 1, 3) if (part - ahead) % 2 else (0, 1, 2, 3)
        for block in range(blocks):
            outs[part][order[block]] = product[block * part_rows : (block + 1) * part_rows]


def run_expert(place, near, far, w_gate, w_up, w_down, experts, parts, ahead):
    count = 2 * near.shape[0]
    units, width = w_gate.shape
    out_shape = jax.ShapeDtypeStruct((PLANE, count // PLANE, width // parts), jnp.bfloat16)
    return local_call(
        functools.partial(expert_kernel, experts, ahead),
        [out_shape] * parts,
        [place],
        [near, far, w_gate, w_up, w_down],
        flops=count,
        moved=count,
    )


def wide(block):
    return block.astype(jnp.float32)


def narrow(block):
    return block.astype(jnp.bfloat16)


def second_share(totals):
    return narrow(jnp.stack([total[2:4] for total in totals]))


def first_share(totals):
    return narrow(jnp.stack([total[1] for total in totals]))


def merged(totals, got, count):
    return [total[0:count] + wide(got[i]) for i, total in enumerate(totals)]


def expert_outputs(place, near, far, weights, experts, cores, waits):
    outs = []
    for ahead in range(cores):
        near_rows = from_core(near, ahead) if ahead else near
        far_rows = from_core(far, ahead) if ahead else far
        near_rows = after(near_rows, *outs[-1:], *waits.get(ahead, []))
        outs.append(run_expert(place, near_rows, far_rows, *weights, experts, cores, ahead))
    return outs


def core_totals(outs, cores):
    totals = []
    for rows_of in range(cores):
        total = wide(outs[rows_of][0])
        for ahead in range(1, cores):
            sent = outs[(rows_of + ahead) % cores][ahead]
            total = total + wide(from_core(sent, cores - ahead))
        totals.append(total)
    return totals


def on_device(
    q_proj,
    k_proj,
    v_proj,
    residual,
    prompt_lengths,
    expert_ids,
    gate_weights,
    page_table,
    out_weight,
    norm_gain,
    w_gate,
    w_up,
    w_down,
):
    tok_rows = q_proj.shape[0]
    col_width = residual.shape[1]
    model_width = norm_gain.shape[0]
    blk_index = lax.axis_index("blk")
    tok_index = lax.axis_index("tok")
    cores = lax.axis_size("tok")
    experts = lax.axis_size("blk")
    planes = experts // PLANE
    place = jnp.stack([blk_index, tok_index]).astype(jnp.int32)
    part_rows = tok_rows // cores
    half_dim = HEAD_DIM // 2
    inv_freq = 10000.0 ** (-jnp.arange(half_dim, dtype=jnp.float32) / half_dim)
    freq = jnp.concatenate([inv_freq, inv_freq])[None, :]
    rotated = jax.ShapeDtypeStruct(q_proj.shape, jnp.bfloat16)
    rot_query, rot_keys = local_call(
        rope_kernel, [rotated] * 2, [place, prompt_lengths], [freq, q_proj, k_proj]
    )
    column = blk_index % PLANE
    key_blocks, value_blocks = [
        [block, next_plane(block)] for block in (rot_keys, after(v_proj, rot_keys))
    ]
    for blocks in (key_blocks, value_blocks):
        own, below = blocks
        for mask in range(1, PLANE):
            blocks.append(flipped(jnp.where(column < column ^ mask, own, below), mask))
    heads = q_proj.shape[1] // HEAD_DIM
    probs_shape = (heads, tok_rows, len(key_blocks) * tok_rows)
    probs = local_call(
        score_kernel,
        [jax.ShapeDtypeStruct(probs_shape, jnp.bfloat16)],
        [place, prompt_lengths],
        [rot_query, *key_blocks],
        flops=2 * tok_rows * probs_shape[2] * heads * HEAD_DIM,
    )[0]
    page_count = tok_rows // PAGE
    local_page = page_table - blk_index * page_count
    kv_rows = jnp.stack([rot_keys, v_proj], axis=1).reshape(page_count, PAGE, 2, -1)
    kv_pages = jnp.zeros_like(kv_rows).at[local_page].set(kv_rows)
    lanes = gate_lanes(expert_ids, gate_weights, experts)
    probs = after(probs, kv_pages, lanes)
    mixed = local_call(
        mix_kernel,
        [jax.ShapeDtypeStruct((tok_rows, model_width), jnp.float32)],
        [place],
        [probs, out_weight, residual, *value_blocks],
        flops=2 * tok_rows * (probs_shape[2] + model_width) * heads * HEAD_DIM,
    )[0]
    if cores == 2:
        addends = [mixed, from_core(mixed, 1)]
    else:
        addends = [lax.psum(mixed, "tok")]
    payload, own_share = local_call(
        norm_kernel,
        [
            jax.ShapeDtypeStruct((part_rows, model_width + lanes.shape[1]), jnp.bfloat16),
            jax.ShapeDtypeStruct((tok_rows, col_width), jnp.bfloat16),
        ],
        [place],
        [norm_gain[None, :], lanes, *addends],
    )
    weights = (w_gate[0].T, w_up[0].T, w_down[0])
    if planes <= 4:
        groups = [[0]] + [sorted({i, planes - i}) for i in range(1, planes // 2 + 1)]
    else:
        groups = [[0]] + [list(range(i, min(i + 8, planes))) for i in range(1, planes, 8)]
    nears, fars = [], []
    weights = (w_gate[0].T, w_up[0].T, w_down[0])
    run = functools.partial(
        expert_outputs, place, weights=weights, experts=experts, cores=cores
    )
    for number, group in enumerate(groups):
        sent = after(payload, nears[0]) if number > 1 else payload
        column = jnp.concatenate([from_plane(sent, ahead) if ahead else sent for ahead in group])
        if number > 1:
            column = after(column, nears[-1])
        nears.append(jnp.concatenate([column, crossed(column, True)]))
        if number > 1 and number == len(groups) - 1:
            outs = run(nears[0], fars[0], waits={})
            nears[-1] = after(nears[-1], *outs)
        fars.append(crossed(after(nears[-1], *fars[-1:]), False))
    totals = core_totals(outs, cores)
    sent = second_share(totals)
    totals = merged(totals, crossed(after(sent, fars[-1]), False), 2)
    shared = first_share(totals)
    partial = {0: (totals, crossed(shared, True))}
    for number in reversed(range(1, len(groups))):
        waits = {0: [outs], cores - 1: [sent]}
        if number < len(groups) - 1:
            waits[cores - 1] = [sent, shared]
        outs = run(nears[number], fars[number], waits=waits)
        totals = core_totals(outs, cores)
        if number < len(groups) - 1:
            totals = [after(total, late) for total in totals]
        sent = second_share(totals)
        totals = merged(totals, crossed(sent, False), 2)
        late = first_share(totals)
        partial[number] = (totals, crossed(late, True))
    results = {}
    for number, group in enumerate(groups):
        totals, came = partial[number]
        rows_of = merged([total[0] for total in totals], came, None)
        for i, ahead in enumerate(group):
            results[ahead] = jnp.concatenate(
                [rows[i * part_rows : (i + 1) * part_rows] for rows in rows_of]
            )
    moe = results[0]
    for ahead in range(1, planes):
        moe = moe + wide(to_plane(narrow(results[ahead]), ahead))
    moe = jnp.roll(moe.reshape(cores, part_rows, col_width), tok_index, axis=0)
    moe = moe.reshape(tok_rows, col_width)
    layer_out = (own_share.astype(jnp.float32) + moe).astype(jnp.bfloat16)
    return (layer_out, kv_pages)


def solution(mesh):
    placed = (
        P("blk", "tok"),
        P("blk", "tok"),
        P("blk", "tok"),
        P("blk", "tok"),
        P(),
        P("blk", None),
        P("blk", None),
        P("blk"),
        P("tok", None),
        P(),
        P("blk", None, "tok"),
        P("blk", None, "tok"),
        P("blk", "tok", None),
    )
    return jax.shard_map(
        on_device,
        mesh=mesh,
        in_specs=placed,
        out_specs=(P("blk", "tok"), P("blk", None, None, "tok")),
        check_vma=False,
    )
```

```python
import functools

import jax
import jax.numpy as jnp
from jax import lax
from jax.experimental import pallas as pl
from jax.experimental.pallas import tpu as pltpu
from jax.sharding import PartitionSpec as P

HEAD_DIM = 128
REACH = 4
PAGE = 16
PLANE = 4
EPSILON = 1e-06


def after(value, *others):
    return lax.optimization_barrier((value, *others))[0]


def flipped(block, mask):
    return lax.ppermute(block, "blk", [(i, i ^ mask) for i in range(lax.axis_size("blk"))])


def next_plane(block):
    count = lax.axis_size("blk")
    return lax.ppermute(block, "blk", [(i, i + PLANE) for i in range(count - PLANE)])


def from_plane(block, ahead):
    count = lax.axis_size("blk")
    with jax.named_scope(f"from_plane_{ahead}"):
        return lax.ppermute(
            block, "blk", [((i + PLANE * ahead) % count, i) for i in range(count)]
        )


def to_plane(block, ahead):
    count = lax.axis_size("blk")
    with jax.named_scope(f"to_plane_{ahead}"):
        return lax.ppermute(
            block, "blk", [(i, (i + PLANE * ahead) % count) for i in range(count)]
        )


def from_core(block, ahead):
    count = lax.axis_size("tok")
    return lax.ppermute(block, "tok", [((i + ahead) % count, i) for i in range(count)])


def segment_starts(place_ref, lengths_ref, shape):
    token = place_ref[0] * shape[0] + lax.broadcasted_iota(jnp.int32, shape, 0)
    start = jnp.zeros(shape, jnp.int32)
    end = jnp.int32(0)
    for i in range(lengths_ref.shape[0]):
        end = end + lengths_ref[i]
        start = jnp.where(token >= end, end, start)
    return token, start


def rope_kernel(place_ref, lengths_ref, freq_ref, q_ref, k_ref, q_out, k_out):
    rows, width = q_ref.shape
    shape = (rows, HEAD_DIM)
    token, start = segment_starts(place_ref, lengths_ref, shape)
    angle = (token - start).astype(jnp.float32) * freq_ref[...]
    cosine, sine = jnp.cos(angle), jnp.sin(angle)
    lane = lax.broadcasted_iota(jnp.int32, shape, 1)
    sine = jnp.where(lane < HEAD_DIM // 2, -sine, sine)
    for source, target in ((k_ref, k_out), (q_ref, q_out)):
        for head in range(width // HEAD_DIM):
            columns = slice(head * HEAD_DIM, (head + 1) * HEAD_DIM)
            x = source[:, columns].astype(jnp.float32)
            turned = x * cosine + pltpu.roll(x, HEAD_DIM // 2, 1) * sine
            target[:, columns] = turned.astype(jnp.bfloat16)


def score_kernel(place_ref, lengths_ref, q_ref, *rest):
    *keys, out_ref = rest
    rows, width = q_ref.shape
    shape = (rows, rows)
    token, start = segment_starts(place_ref, lengths_ref, shape)
    blk = place_ref[0]
    column = lax.rem(blk, PLANE)
    bases = [blk, blk - PLANE]
    for mask in range(1, PLANE):
        other = column ^ mask
        bases.append(blk - column + other - jnp.where(other > column, PLANE, 0))
    lane = lax.broadcasted_iota(jnp.int32, shape, 1)
    ids = jnp.concatenate([base * rows + lane for base in bases], axis=1)
    token = jnp.concatenate([token] * len(keys), axis=1)
    start = jnp.concatenate([start] * len(keys), axis=1)
    allowed = (ids >= start) & (ids <= token)
    for head in range(width // HEAD_DIM):
        columns = slice(head * HEAD_DIM, (head + 1) * HEAD_DIM)
        key = jnp.concatenate([ref[:, columns] for ref in keys], axis=0)
        scores = lax.dot_general(
            q_ref[:, columns],
            key,
            (((1,), (1,)), ((), ())),
            preferred_element_type=jnp.float32,
        )
        scores = jnp.where(allowed, scores * HEAD_DIM ** (-0.5), -1e30)
        terms = jnp.exp(scores - jnp.max(scores, axis=1, keepdims=True))
        share = 1.0 / jnp.sum(terms, axis=1, keepdims=True)
        out_ref[head] = (terms * share).astype(jnp.bfloat16)


def mix_kernel(place_ref, prob_ref, weight_ref, residual_ref, *rest):
    *values, out_ref = rest
    heads = prob_ref.shape[0]
    mixed = []
    for head in range(heads):
        columns = slice(head * HEAD_DIM, (head + 1) * HEAD_DIM)
        value = jnp.concatenate([ref[:, columns] for ref in values], axis=0)
        product = jnp.dot(prob_ref[head], value, preferred_element_type=jnp.float32)
        mixed.append(product.astype(jnp.bfloat16))
    attention = jnp.concatenate(mixed, axis=1)
    out_ref[...] = jnp.dot(attention, weight_ref[...], preferred_element_type=jnp.float32)
    width = residual_ref.shape[1]
    own = pl.ds(pl.multiple_of(place_ref[1] * width, 128), width)
    out_ref[:, own] = out_ref[:, own] + residual_ref[...].astype(jnp.float32)


def norm_kernel(place_ref, gain_ref, lanes_ref, *rest):
    *addends, rows_out, share_out = rest
    rows, width = addends[0].shape
    part_rows = rows_out.shape[0]
    part_width = share_out.shape[1]
    own = pl.ds(pl.multiple_of(place_ref[1] * part_width, 128), part_width)
    share_out[...] = sum(ref[:, own] for ref in addends).astype(jnp.bfloat16)
    part = pl.ds(pl.multiple_of(place_ref[1] * part_rows, 16), part_rows)
    stream = sum(ref[part, :] for ref in addends).astype(jnp.bfloat16).astype(jnp.float32)
    scale = lax.rsqrt(jnp.mean(stream * stream, axis=1, keepdims=True) + EPSILON)
    rows_out[:, :width] = (stream * scale * gain_ref[...]).astype(jnp.bfloat16)
    rows_out[:, width:] = lanes_ref[part, :]


def local_call(body, out_shapes, scalars, arrays, flops=0, moved=0, limit=16):
    whole = pl.BlockSpec(memory_space=pltpu.VMEM)
    scalar = pl.BlockSpec(memory_space=pltpu.SMEM)
    moved = moved or sum(x.size * x.dtype.itemsize for x in (*arrays, *out_shapes))
    return pl.pallas_call(
        body,
        in_specs=[scalar] * len(scalars) + [whole] * len(arrays),
        out_specs=[whole] * len(out_shapes),
        out_shape=out_shapes,
        cost_estimate=pl.CostEstimate(flops=flops, bytes_accessed=moved, transcendentals=0),
        compiler_params=pltpu.CompilerParams(vmem_limit_bytes=limit << 20),
    )(*scalars, *arrays)


def gate_lanes(expert_ids, gate_weights, experts):
    hits = expert_ids[:, :, None] == jnp.arange(experts, dtype=jnp.int32)[None, None, :]
    gates = jnp.sum(jnp.where(hits, gate_weights[:, :, None], 0.0), axis=1)
    pieces = []
    for _ in range(3):
        piece = lax.reduce_precision(gates, 8, 7)
        pieces.append(piece.astype(jnp.bfloat16))
        gates = gates - piece
    lanes = jnp.concatenate(pieces, axis=1)
    return jnp.pad(lanes, ((0, 0), (0, -lanes.shape[1] % 128)))


def crossed(block, first, name="flip"):
    cores, count = lax.axis_size("tok"), lax.axis_size("blk")
    route = []
    for core in range(cores):
        mask = 1 if (core % 2 == 0) == first else 2
        route += [(core * count + i, core * count + (i ^ mask)) for i in range(count)]
    with jax.named_scope(name):
        return lax.ppermute(block, ("tok", "blk"), route)


def expert_kernel(experts, ahead, place_ref, near_ref, far_ref, gate_ref, up_ref, down_ref, *outs):
    width = gate_ref.shape[1]
    parts = len(outs)
    blocks, part_rows, part_width = outs[0].shape
    held = jnp.concatenate([near_ref[...], far_ref[...]], axis=0)
    rows = held[:, :width]
    lanes = held[:, width:].astype(jnp.float32)
    lane_ids = lax.broadcasted_iota(jnp.int32, lanes.shape, 1)
    named = (lane_ids < 3 * experts) & (lane_ids % experts == place_ref[0])
    weight = jnp.sum(jnp.where(named, lanes, 0.0), axis=1, keepdims=True)
    turned = (((1,), (1,)), ((), ()))
    gate_act = lax.dot_general(rows, gate_ref[...], turned, preferred_element_type=jnp.float32)
    up_act = lax.dot_general(rows, up_ref[...], turned, preferred_element_type=jnp.float32)
    hidden = (gate_act / (1.0 + jnp.exp(-gate_act)) * up_act).astype(jnp.bfloat16)
    for part in range(parts):
        start = lax.rem(place_ref[1] + part, parts) * part_width
        columns = pl.ds(pl.multiple_of(start, 128), part_width)
        product = jnp.dot(hidden, down_ref[:, columns], preferred_element_type=jnp.float32)
        product = (weight * product).astype(jnp.bfloat16)
        order = (0, 2, 1, 3) if (part - ahead) % 2 else (0, 1, 2, 3)
        for block in range(blocks):
            outs[part][order[block]] = product[block * part_rows : (block + 1) * part_rows]


def run_expert(place, near, far, w_gate, w_up, w_down, experts, parts, ahead):
    count = 2 * near.shape[0]
    units, width = w_gate.shape
    out_shape = jax.ShapeDtypeStruct((PLANE, count // PLANE, width // parts), jnp.bfloat16)
    return local_call(
        functools.partial(expert_kernel, experts, ahead),
        [out_shape] * parts,
        [place],
        [near, far, w_gate, w_up, w_down],
        flops=6 * count * width * units,
        moved=count,
    )


def wide(block):
    return block.astype(jnp.float32)


def narrow(block):
    return block.astype(jnp.bfloat16)


def second_share(totals):
    return narrow(jnp.stack([total[2:4] for total in totals]))


def first_share(totals):
    return narrow(jnp.stack([total[1] for total in totals]))


def merged(totals, got, count):
    return [total[0:count] + wide(got[i]) for i, total in enumerate(totals)]


def expert_outputs(place, near, far, weights, experts, cores, waits):
    outs = []
    for ahead in range(cores):
        near_rows = from_core(near, ahead) if ahead else near
        far_rows = from_core(far, ahead) if ahead else far
        near_rows = after(near_rows, *outs[-1:], *waits.get(ahead, []))
        outs.append(run_expert(place, near_rows, far_rows, *weights, experts, cores, ahead))
    return outs


def core_totals(outs, cores):
    totals = []
    for rows_of in range(cores):
        total = wide(outs[rows_of][0])
        for ahead in range(1, cores):
            sent = outs[(rows_of + ahead) % cores][ahead]
            total = total + wide(from_core(sent, cores - ahead))
        totals.append(total)
    return totals


def on_device(
    q_proj,
    k_proj,
    v_proj,
    residual,
    prompt_lengths,
    expert_ids,
    gate_weights,
    page_table,
    out_weight,
    norm_gain,
    w_gate,
    w_up,
    w_down,
):
    tok_rows = q_proj.shape[0]
    col_width = residual.shape[1]
    model_width = norm_gain.shape[0]
    blk_index = lax.axis_index("blk")
    tok_index = lax.axis_index("tok")
    cores = lax.axis_size("tok")
    experts = lax.axis_size("blk")
    planes = experts // PLANE
    place = jnp.stack([blk_index, tok_index]).astype(jnp.int32)
    part_rows = tok_rows // cores
    half_dim = HEAD_DIM // 2
    inv_freq = 10000.0 ** (-jnp.arange(half_dim, dtype=jnp.float32) / half_dim)
    freq = jnp.concatenate([inv_freq, inv_freq])[None, :]
    rotated = jax.ShapeDtypeStruct(q_proj.shape, jnp.bfloat16)
    rot_query, rot_keys = local_call(
        rope_kernel, [rotated] * 2, [place, prompt_lengths], [freq, q_proj, k_proj]
    )
    column = blk_index % PLANE
    key_blocks, value_blocks = [
        [block, next_plane(block)] for block in (rot_keys, after(v_proj, rot_keys))
    ]
    for blocks in (key_blocks, value_blocks):
        own, below = blocks
        for mask in range(1, PLANE):
            blocks.append(flipped(jnp.where(column < column ^ mask, own, below), mask))
    heads = q_proj.shape[1] // HEAD_DIM
    probs_shape = (heads, tok_rows, len(key_blocks) * tok_rows)
    probs = local_call(
        score_kernel,
        [jax.ShapeDtypeStruct(probs_shape, jnp.bfloat16)],
        [place, prompt_lengths],
        [rot_query, *key_blocks],
        flops=2 * tok_rows * probs_shape[2] * heads * HEAD_DIM,
    )[0]
    page_count = tok_rows // PAGE
    local_page = page_table - blk_index * page_count
    kv_rows = jnp.stack([rot_keys, v_proj], axis=1).reshape(page_count, PAGE, 2, -1)
    kv_pages = jnp.zeros_like(kv_rows).at[local_page].set(kv_rows)
    lanes = gate_lanes(expert_ids, gate_weights, experts)
    probs = after(probs, kv_pages, lanes)
    mixed = local_call(
        mix_kernel,
        [jax.ShapeDtypeStruct((tok_rows, model_width), jnp.float32)],
        [place],
        [probs, out_weight, residual, *value_blocks],
        flops=2 * tok_rows * (probs_shape[2] + model_width) * heads * HEAD_DIM,
    )[0]
    if cores == 2:
        addends = [mixed, from_core(mixed, 1)]
    else:
        addends = [lax.psum(mixed, "tok")]
    payload, own_share = local_call(
        norm_kernel,
        [
            jax.ShapeDtypeStruct((part_rows, model_width + lanes.shape[1]), jnp.bfloat16),
            jax.ShapeDtypeStruct((tok_rows, col_width), jnp.bfloat16),
        ],
        [place],
        [norm_gain[None, :], lanes, *addends],
    )
    weights = (w_gate[0].T, w_up[0].T, w_down[0])
    if planes <= 4:
        groups = [[0]] + [sorted({i, planes - i}) for i in range(1, planes // 2 + 1)]
    else:
        groups = [[0]] + [list(range(i, min(i + 8, planes))) for i in range(1, planes, 8)]
    nears, fars = [], []
    weights = (w_gate[0].T, w_up[0].T, w_down[0])
    run = functools.partial(
        expert_outputs, place, weights=weights, experts=experts, cores=cores
    )
    for number, group in enumerate(groups):
        sent = after(payload, nears[0]) if number > 1 else payload
        column = jnp.concatenate([from_plane(sent, ahead) if ahead else sent for ahead in group])
        if number > 1:
            column = after(column, nears[-1])
        nears.append(jnp.concatenate([column, crossed(column, True, f"gather_first_{number}")]))
        if number > 1 and number == len(groups) - 1:
            outs = run(nears[0], fars[0], waits={})
            nears[-1] = after(nears[-1], *outs)
        fars.append(crossed(after(nears[-1], *fars[-1:]), False, f"gather_second_{number}"))
    totals = core_totals(outs, cores)
    sent = second_share(totals)
    totals = merged(totals, crossed(after(sent, fars[-1]), False, "scatter_second_0"), 2)
    shared = first_share(totals)
    partial = (totals, crossed(shared, True, "scatter_first_0"))
    results = {}
    returned = []
    for number in reversed(range(1, len(groups))):
        waits = {0: [outs], cores - 1: [sent]}
        if number < len(groups) - 1:
            waits[cores - 1] = [sent, shared]
        outs = run(nears[number], fars[number], waits=waits)
        totals = core_totals(outs, cores)
        if number < len(groups) - 1:
            totals = [after(total, late) for total in totals]
        sent = second_share(totals)
        totals = merged(totals, crossed(sent, False, f"scatter_second_{number}"), 2)
        late = after(first_share(totals), *results.values())
        came = crossed(late, True, f"scatter_first_{number}")
        rows_of = merged([total[0] for total in totals], came, None)
        results = {}
        for i, ahead in enumerate(groups[number]):
            piece = [rows[i * part_rows : (i + 1) * part_rows] for rows in rows_of]
            results[ahead] = after(narrow(jnp.concatenate(piece)), *returned[-1:])
        for ahead, block in results.items():
            returned.append(to_plane(block, ahead))
    totals, came = partial
    moe = jnp.concatenate(merged([total[0] for total in totals], came, None))
    moe = moe + sum(wide(block) for block in returned)
    moe = jnp.roll(moe.reshape(cores, part_rows, col_width), tok_index, axis=0)
    moe = moe.reshape(tok_rows, col_width)
    layer_out = (own_share.astype(jnp.float32) + moe).astype(jnp.bfloat16)
    return (layer_out, kv_pages)


def solution(mesh):
    placed = (
        P("blk", "tok"),
        P("blk", "tok"),
        P("blk", "tok"),
        P("blk", "tok"),
        P(),
        P("blk", None),
        P("blk", None),
        P("blk"),
        P("tok", None),
        P(),
        P("blk", None, "tok"),
        P("blk", None, "tok"),
        P("blk", "tok", None),
    )
    return jax.shard_map(
        on_device,
        mesh=mesh,
        in_specs=placed,
        out_specs=(P("blk", "tok"), P("blk", None, None, "tok")),
        check_vma=False,
    )
```

```python
import functools

import jax
import jax.numpy as jnp
from jax import lax
from jax.experimental import pallas as pl
from jax.experimental.pallas import tpu as pltpu
from jax.sharding import PartitionSpec as P

HEAD_DIM = 128
REACH = 4
PAGE = 16
PLANE = 4
EPSILON = 1e-06
LIGHT = 100


def after(value, *others):
    return lax.optimization_barrier((value, *others))[0]


def flipped(block, mask):
    return lax.ppermute(block, "blk", [(i, i ^ mask) for i in range(lax.axis_size("blk"))])


def next_plane(block):
    count = lax.axis_size("blk")
    return lax.ppermute(block, "blk", [(i, i + PLANE) for i in range(count - PLANE)])


def from_plane(block, ahead):
    count = lax.axis_size("blk")
    with jax.named_scope(f"from_plane_{ahead}"):
        return lax.ppermute(
            block, "blk", [((i + PLANE * ahead) % count, i) for i in range(count)]
        )


def to_plane(block, ahead):
    count = lax.axis_size("blk")
    with jax.named_scope(f"to_plane_{ahead}"):
        return lax.ppermute(
            block, "blk", [(i, (i + PLANE * ahead) % count) for i in range(count)]
        )


def from_core(block, ahead):
    count = lax.axis_size("tok")
    return lax.ppermute(block, "tok", [((i + ahead) % count, i) for i in range(count)])


def segment_starts(place_ref, lengths_ref, shape):
    token = place_ref[0] * shape[0] + lax.broadcasted_iota(jnp.int32, shape, 0)
    start = jnp.zeros(shape, jnp.int32)
    end = jnp.int32(0)
    for i in range(lengths_ref.shape[0]):
        end = end + lengths_ref[i]
        start = jnp.where(token >= end, end, start)
    return token, start


def rope_kernel(place_ref, lengths_ref, freq_ref, q_ref, k_ref, q_out, k_out):
    rows, width = q_ref.shape
    shape = (rows, HEAD_DIM)
    token, start = segment_starts(place_ref, lengths_ref, shape)
    angle = (token - start).astype(jnp.float32) * freq_ref[...]
    cosine, sine = jnp.cos(angle), jnp.sin(angle)
    lane = lax.broadcasted_iota(jnp.int32, shape, 1)
    sine = jnp.where(lane < HEAD_DIM // 2, -sine, sine)
    for source, target in ((k_ref, k_out), (q_ref, q_out)):
        for head in range(width // HEAD_DIM):
            columns = slice(head * HEAD_DIM, (head + 1) * HEAD_DIM)
            x = source[:, columns].astype(jnp.float32)
            turned = x * cosine + pltpu.roll(x, HEAD_DIM // 2, 1) * sine
            target[:, columns] = turned.astype(jnp.bfloat16)


def score_kernel(place_ref, lengths_ref, q_ref, *rest):
    *keys, out_ref = rest
    rows, width = q_ref.shape
    shape = (rows, rows)
    token, start = segment_starts(place_ref, lengths_ref, shape)
    blk = place_ref[0]
    column = lax.rem(blk, PLANE)
    bases = [blk, blk - PLANE]
    for mask in range(1, PLANE):
        other = column ^ mask
        bases.append(blk - column + other - jnp.where(other > column, PLANE, 0))
    lane = lax.broadcasted_iota(jnp.int32, shape, 1)
    ids = jnp.concatenate([base * rows + lane for base in bases], axis=1)
    token = jnp.concatenate([token] * len(keys), axis=1)
    start = jnp.concatenate([start] * len(keys), axis=1)
    allowed = (ids >= start) & (ids <= token)
    for head in range(width // HEAD_DIM):
        columns = slice(head * HEAD_DIM, (head + 1) * HEAD_DIM)
        key = jnp.concatenate([ref[:, columns] for ref in keys], axis=0)
        scores = lax.dot_general(
            q_ref[:, columns],
            key,
            (((1,), (1,)), ((), ())),
            preferred_element_type=jnp.float32,
        )
        scores = jnp.where(allowed, scores * HEAD_DIM ** (-0.5), -1e30)
        terms = jnp.exp(scores - jnp.max(scores, axis=1, keepdims=True))
        share = 1.0 / jnp.sum(terms, axis=1, keepdims=True)
        out_ref[head] = (terms * share).astype(jnp.bfloat16)


def mix_kernel(place_ref, prob_ref, weight_ref, residual_ref, *rest):
    *values, out_ref = rest
    heads = prob_ref.shape[0]
    mixed = []
    for head in range(heads):
        columns = slice(head * HEAD_DIM, (head + 1) * HEAD_DIM)
        value = jnp.concatenate([ref[:, columns] for ref in values], axis=0)
        product = jnp.dot(prob_ref[head], value, preferred_element_type=jnp.float32)
        mixed.append(product.astype(jnp.bfloat16))
    attention = jnp.concatenate(mixed, axis=1)
    out_ref[...] = jnp.dot(attention, weight_ref[...], preferred_element_type=jnp.float32)
    width = residual_ref.shape[1]
    own = pl.ds(pl.multiple_of(place_ref[1] * width, 128), width)
    out_ref[:, own] = out_ref[:, own] + residual_ref[...].astype(jnp.float32)


def norm_kernel(place_ref, gain_ref, lanes_ref, *rest):
    *addends, rows_out, share_out = rest
    rows, width = addends[0].shape
    part_rows = rows_out.shape[0]
    part_width = share_out.shape[1]
    own = pl.ds(pl.multiple_of(place_ref[1] * part_width, 128), part_width)
    share_out[...] = sum(ref[:, own] for ref in addends).astype(jnp.bfloat16)
    part = pl.ds(pl.multiple_of(place_ref[1] * part_rows, 16), part_rows)
    stream = sum(ref[part, :] for ref in addends).astype(jnp.bfloat16).astype(jnp.float32)
    scale = lax.rsqrt(jnp.mean(stream * stream, axis=1, keepdims=True) + EPSILON)
    rows_out[:, :width] = (stream * scale * gain_ref[...]).astype(jnp.bfloat16)
    rows_out[:, width:] = lanes_ref[part, :]


def local_call(body, out_shapes, scalars, arrays, flops=0, moved=0, limit=16):
    whole = pl.BlockSpec(memory_space=pltpu.VMEM)
    scalar = pl.BlockSpec(memory_space=pltpu.SMEM)
    moved = moved or sum(x.size * x.dtype.itemsize for x in (*arrays, *out_shapes))
    return pl.pallas_call(
        body,
        in_specs=[scalar] * len(scalars) + [whole] * len(arrays),
        out_specs=[whole] * len(out_shapes),
        out_shape=out_shapes,
        cost_estimate=pl.CostEstimate(flops=flops, bytes_accessed=moved, transcendentals=0),
        compiler_params=pltpu.CompilerParams(vmem_limit_bytes=limit << 20),
    )(*scalars, *arrays)


def gate_lanes(expert_ids, gate_weights, experts):
    hits = expert_ids[:, :, None] == jnp.arange(experts, dtype=jnp.int32)[None, None, :]
    gates = jnp.sum(jnp.where(hits, gate_weights[:, :, None], 0.0), axis=1)
    pieces = []
    for _ in range(3):
        piece = lax.reduce_precision(gates, 8, 7)
        pieces.append(piece.astype(jnp.bfloat16))
        gates = gates - piece
    lanes = jnp.concatenate(pieces, axis=1)
    return jnp.pad(lanes, ((0, 0), (0, -lanes.shape[1] % 128)))


def crossed(block, first, name="flip"):
    cores, count = lax.axis_size("tok"), lax.axis_size("blk")
    route = []
    for core in range(cores):
        mask = 1 if (core % 2 == 0) == first else 2
        route += [(core * count + i, core * count + (i ^ mask)) for i in range(count)]
    with jax.named_scope(name):
        return lax.ppermute(block, ("tok", "blk"), route)


def expert_kernel(experts, ahead, place_ref, near_ref, far_ref, gate_ref, up_ref, down_ref, *outs):
    width = gate_ref.shape[1]
    parts = len(outs)
    blocks, part_rows, part_width = outs[0].shape
    held = jnp.concatenate([near_ref[...], far_ref[...]], axis=0)
    rows = held[:, :width]
    lanes = held[:, width:].astype(jnp.float32)
    lane_ids = lax.broadcasted_iota(jnp.int32, lanes.shape, 1)
    named = (lane_ids < 3 * experts) & (lane_ids % experts == place_ref[0])
    weight = jnp.sum(jnp.where(named, lanes, 0.0), axis=1, keepdims=True)
    turned = (((1,), (1,)), ((), ()))
    gate_act = lax.dot_general(rows, gate_ref[...], turned, preferred_element_type=jnp.float32)
    up_act = lax.dot_general(rows, up_ref[...], turned, preferred_element_type=jnp.float32)
    hidden = (gate_act / (1.0 + jnp.exp(-gate_act)) * up_act).astype(jnp.bfloat16)
    for part in range(parts):
        start = lax.rem(place_ref[1] + part, parts) * part_width
        columns = pl.ds(pl.multiple_of(start, 128), part_width)
        product = jnp.dot(hidden, down_ref[:, columns], preferred_element_type=jnp.float32)
        product = (weight * product).astype(jnp.bfloat16)
        order = (0, 2, 1, 3) if (part - ahead) % 2 else (0, 1, 2, 3)
        for block in range(blocks):
            outs[part][order[block]] = product[block * part_rows : (block + 1) * part_rows]


def run_expert(place, near, far, w_gate, w_up, w_down, experts, parts, ahead, weight):
    count = 2 * near.shape[0]
    units, width = w_gate.shape
    out_shape = jax.ShapeDtypeStruct((PLANE, count // PLANE, width // parts), jnp.bfloat16)
    return local_call(
        functools.partial(expert_kernel, experts, ahead),
        [out_shape] * parts,
        [place],
        [near, far, w_gate, w_up, w_down],
        flops=6 * count * width * units // weight,
        moved=count,
    )


def wide(block):
    return block.astype(jnp.float32)


def narrow(block):
    return block.astype(jnp.bfloat16)


def second_share(totals):
    return narrow(jnp.stack([total[2:4] for total in totals]))


def first_share(totals):
    return narrow(jnp.stack([total[1] for total in totals]))


def merged(totals, got, count):
    return [total[0:count] + wide(got[i]) for i, total in enumerate(totals)]


def expert_outputs(place, near, far, weights, experts, cores, waits, weight=1):
    outs = []
    for ahead in range(cores):
        near_rows = from_core(near, ahead) if ahead else near
        far_rows = from_core(far, ahead) if ahead else far
        near_rows = after(near_rows, *outs[-1:], *waits.get(ahead, []))
        outs.append(run_expert(place, near_rows, far_rows, *weights, experts, cores, ahead, weight))
    return outs


def core_totals(outs, cores):
    totals = []
    for rows_of in range(cores):
        total = wide(outs[rows_of][0])
        for ahead in range(1, cores):
            sent = outs[(rows_of + ahead) % cores][ahead]
            total = total + wide(from_core(sent, cores - ahead))
        totals.append(total)
    return totals


def on_device(
    q_proj,
    k_proj,
    v_proj,
    residual,
    prompt_lengths,
    expert_ids,
    gate_weights,
    page_table,
    out_weight,
    norm_gain,
    w_gate,
    w_up,
    w_down,
):
    tok_rows = q_proj.shape[0]
    col_width = residual.shape[1]
    model_width = norm_gain.shape[0]
    blk_index = lax.axis_index("blk")
    tok_index = lax.axis_index("tok")
    cores = lax.axis_size("tok")
    experts = lax.axis_size("blk")
    planes = experts // PLANE
    place = jnp.stack([blk_index, tok_index]).astype(jnp.int32)
    part_rows = tok_rows // cores
    half_dim = HEAD_DIM // 2
    inv_freq = 10000.0 ** (-jnp.arange(half_dim, dtype=jnp.float32) / half_dim)
    freq = jnp.concatenate([inv_freq, inv_freq])[None, :]
    rotated = jax.ShapeDtypeStruct(q_proj.shape, jnp.bfloat16)
    rot_query, rot_keys = local_call(
        rope_kernel, [rotated] * 2, [place, prompt_lengths], [freq, q_proj, k_proj]
    )
    column = blk_index % PLANE
    key_blocks, value_blocks = [
        [block, next_plane(block)] for block in (rot_keys, after(v_proj, rot_keys))
    ]
    for blocks in (key_blocks, value_blocks):
        own, below = blocks
        for mask in range(1, PLANE):
            blocks.append(flipped(jnp.where(column < column ^ mask, own, below), mask))
    heads = q_proj.shape[1] // HEAD_DIM
    probs_shape = (heads, tok_rows, len(key_blocks) * tok_rows)
    probs = local_call(
        score_kernel,
        [jax.ShapeDtypeStruct(probs_shape, jnp.bfloat16)],
        [place, prompt_lengths],
        [rot_query, *key_blocks],
        flops=2 * tok_rows * probs_shape[2] * heads * HEAD_DIM,
    )[0]
    page_count = tok_rows // PAGE
    local_page = page_table - blk_index * page_count
    kv_rows = jnp.stack([rot_keys, v_proj], axis=1).reshape(page_count, PAGE, 2, -1)
    kv_pages = jnp.zeros_like(kv_rows).at[local_page].set(kv_rows)
    lanes = gate_lanes(expert_ids, gate_weights, experts)
    probs = after(probs, kv_pages, lanes)
    mixed = local_call(
        mix_kernel,
        [jax.ShapeDtypeStruct((tok_rows, model_width), jnp.float32)],
        [place],
        [probs, out_weight, residual, *value_blocks],
        flops=2 * tok_rows * (probs_shape[2] + model_width) * heads * HEAD_DIM,
    )[0]
    if cores == 2:
        addends = [mixed, from_core(mixed, 1)]
    else:
        addends = [lax.psum(mixed, "tok")]
    payload, own_share = local_call(
        norm_kernel,
        [
            jax.ShapeDtypeStruct((part_rows, model_width + lanes.shape[1]), jnp.bfloat16),
            jax.ShapeDtypeStruct((tok_rows, col_width), jnp.bfloat16),
        ],
        [place],
        [norm_gain[None, :], lanes, *addends],
    )
    weights = (w_gate[0].T, w_up[0].T, w_down[0])
    if planes <= 4:
        groups = [[0]] + [sorted({i, planes - i}) for i in range(1, planes // 2 + 1)]
    else:
        groups = [[0]] + [list(range(i, min(i + 8, planes))) for i in range(1, planes, 8)]
    nears, fars = [], []
    weights = (w_gate[0].T, w_up[0].T, w_down[0])
    run = functools.partial(
        expert_outputs, place, weights=weights, experts=experts, cores=cores
    )
    for number, group in enumerate(groups):
        sent = after(payload, nears[0]) if number > 1 else payload
        column = jnp.concatenate([from_plane(sent, ahead) if ahead else sent for ahead in group])
        if number > 1:
            column = after(column, nears[-1])
        nears.append(jnp.concatenate([column, crossed(column, True, f"gather_first_{number}")]))
        fars.append(crossed(nears[-1], False, f"gather_second_{number}"))
    outs = run(nears[0], fars[0], waits={})
    totals = core_totals(outs, cores)
    sent = second_share(totals)
    totals = merged(totals, crossed(after(sent, fars[-1]), False, "scatter_second_0"), 2)
    shared = first_share(totals)
    partial = (totals, crossed(shared, True, "scatter_first_0"))
    results = {}
    returned = []
    for number in reversed(range(1, len(groups))):
        waits = {0: [outs, fars], cores - 1: [sent]}
        if number < len(groups) - 1:
            waits = {0: [outs], cores - 1: [sent, shared]}
        outs = run(nears[number], fars[number], waits=waits, weight=LIGHT)
        totals = core_totals(outs, cores)
        if number < len(groups) - 1:
            totals = [after(total, late) for total in totals]
        sent = second_share(totals)
        totals = merged(totals, crossed(sent, False, f"scatter_second_{number}"), 2)
        late = after(first_share(totals), *results.values())
        came = crossed(late, True, f"scatter_first_{number}")
        rows_of = merged([total[0] for total in totals], came, None)
        results = {}
        for i, ahead in enumerate(groups[number]):
            piece = [rows[i * part_rows : (i + 1) * part_rows] for rows in rows_of]
            results[ahead] = after(narrow(jnp.concatenate(piece)), *returned[-1:])
        for ahead, block in results.items():
            returned.append(to_plane(block, ahead))
    totals, came = partial
    moe = jnp.concatenate(merged([total[0] for total in totals], came, None))
    moe = moe + sum(wide(block) for block in returned)
    moe = jnp.roll(moe.reshape(cores, part_rows, col_width), tok_index, axis=0)
    moe = moe.reshape(tok_rows, col_width)
    layer_out = (own_share.astype(jnp.float32) + moe).astype(jnp.bfloat16)
    return (layer_out, kv_pages)


def solution(mesh):
    placed = (
        P("blk", "tok"),
        P("blk", "tok"),
        P("blk", "tok"),
        P("blk", "tok"),
        P(),
        P("blk", None),
        P("blk", None),
        P("blk"),
        P("tok", None),
        P(),
        P("blk", None, "tok"),
        P("blk", None, "tok"),
        P("blk", "tok", None),
    )
    return jax.shard_map(
        on_device,
        mesh=mesh,
        in_specs=placed,
        out_specs=(P("blk", "tok"), P("blk", None, None, "tok")),
        check_vma=False,
    )
```

```python
import functools

import jax
import jax.numpy as jnp
from jax import lax
from jax.experimental import pallas as pl
from jax.experimental.pallas import tpu as pltpu
from jax.sharding import PartitionSpec as P

HEAD_DIM = 128
REACH = 4
PAGE = 16
PLANE = 4
EPSILON = 1e-06


def after(value, *others):
    return lax.optimization_barrier((value, *others))[0]


def flipped(block, mask):
    return lax.ppermute(block, "blk", [(i, i ^ mask) for i in range(lax.axis_size("blk"))])


def next_plane(block):
    count = lax.axis_size("blk")
    return lax.ppermute(block, "blk", [(i, i + PLANE) for i in range(count - PLANE)])


def from_plane(block, ahead):
    count = lax.axis_size("blk")
    with jax.named_scope(f"from_plane_{ahead}"):
        return lax.ppermute(
            block, "blk", [((i + PLANE * ahead) % count, i) for i in range(count)]
        )


def to_plane(block, ahead):
    count = lax.axis_size("blk")
    with jax.named_scope(f"to_plane_{ahead}"):
        return lax.ppermute(
            block, "blk", [(i, (i + PLANE * ahead) % count) for i in range(count)]
        )


def from_core(block, ahead):
    count = lax.axis_size("tok")
    return lax.ppermute(block, "tok", [((i + ahead) % count, i) for i in range(count)])


def segment_starts(place_ref, lengths_ref, shape):
    token = place_ref[0] * shape[0] + lax.broadcasted_iota(jnp.int32, shape, 0)
    start = jnp.zeros(shape, jnp.int32)
    end = jnp.int32(0)
    for i in range(lengths_ref.shape[0]):
        end = end + lengths_ref[i]
        start = jnp.where(token >= end, end, start)
    return token, start


def rope_kernel(place_ref, lengths_ref, freq_ref, q_ref, k_ref, q_out, k_out):
    rows, width = q_ref.shape
    shape = (rows, HEAD_DIM)
    token, start = segment_starts(place_ref, lengths_ref, shape)
    angle = (token - start).astype(jnp.float32) * freq_ref[...]
    cosine, sine = jnp.cos(angle), jnp.sin(angle)
    lane = lax.broadcasted_iota(jnp.int32, shape, 1)
    sine = jnp.where(lane < HEAD_DIM // 2, -sine, sine)
    for source, target in ((k_ref, k_out), (q_ref, q_out)):
        for head in range(width // HEAD_DIM):
            columns = slice(head * HEAD_DIM, (head + 1) * HEAD_DIM)
            x = source[:, columns].astype(jnp.float32)
            turned = x * cosine + pltpu.roll(x, HEAD_DIM // 2, 1) * sine
            target[:, columns] = turned.astype(jnp.bfloat16)


def score_kernel(place_ref, lengths_ref, q_ref, *rest):
    *keys, out_ref = rest
    rows, width = q_ref.shape
    shape = (rows, rows)
    token, start = segment_starts(place_ref, lengths_ref, shape)
    blk = place_ref[0]
    column = lax.rem(blk, PLANE)
    bases = [blk, blk - PLANE]
    for mask in range(1, PLANE):
        other = column ^ mask
        bases.append(blk - column + other - jnp.where(other > column, PLANE, 0))
    lane = lax.broadcasted_iota(jnp.int32, shape, 1)
    ids = jnp.concatenate([base * rows + lane for base in bases], axis=1)
    token = jnp.concatenate([token] * len(keys), axis=1)
    start = jnp.concatenate([start] * len(keys), axis=1)
    allowed = (ids >= start) & (ids <= token)
    for head in range(width // HEAD_DIM):
        columns = slice(head * HEAD_DIM, (head + 1) * HEAD_DIM)
        key = jnp.concatenate([ref[:, columns] for ref in keys], axis=0)
        scores = lax.dot_general(
            q_ref[:, columns],
            key,
            (((1,), (1,)), ((), ())),
            preferred_element_type=jnp.float32,
        )
        scores = jnp.where(allowed, scores * HEAD_DIM ** (-0.5), -1e30)
        terms = jnp.exp(scores - jnp.max(scores, axis=1, keepdims=True))
        share = 1.0 / jnp.sum(terms, axis=1, keepdims=True)
        out_ref[head] = (terms * share).astype(jnp.bfloat16)


def mix_kernel(place_ref, prob_ref, weight_ref, residual_ref, *rest):
    *values, out_ref = rest
    heads = prob_ref.shape[0]
    mixed = []
    for head in range(heads):
        columns = slice(head * HEAD_DIM, (head + 1) * HEAD_DIM)
        value = jnp.concatenate([ref[:, columns] for ref in values], axis=0)
        product = jnp.dot(prob_ref[head], value, preferred_element_type=jnp.float32)
        mixed.append(product.astype(jnp.bfloat16))
    attention = jnp.concatenate(mixed, axis=1)
    out_ref[...] = jnp.dot(attention, weight_ref[...], preferred_element_type=jnp.float32)
    width = residual_ref.shape[1]
    own = pl.ds(pl.multiple_of(place_ref[1] * width, 128), width)
    out_ref[:, own] = out_ref[:, own] + residual_ref[...].astype(jnp.float32)


def norm_kernel(place_ref, gain_ref, lanes_ref, *rest):
    *addends, rows_out, share_out = rest
    rows, width = addends[0].shape
    part_rows = rows_out.shape[0]
    part_width = share_out.shape[1]
    own = pl.ds(pl.multiple_of(place_ref[1] * part_width, 128), part_width)
    share_out[...] = sum(ref[:, own] for ref in addends).astype(jnp.bfloat16)
    part = pl.ds(pl.multiple_of(place_ref[1] * part_rows, 16), part_rows)
    stream = sum(ref[part, :] for ref in addends).astype(jnp.bfloat16).astype(jnp.float32)
    scale = lax.rsqrt(jnp.mean(stream * stream, axis=1, keepdims=True) + EPSILON)
    rows_out[:, :width] = (stream * scale * gain_ref[...]).astype(jnp.bfloat16)
    rows_out[:, width:] = lanes_ref[part, :]


def local_call(body, out_shapes, scalars, arrays, flops=0, moved=0, limit=16):
    whole = pl.BlockSpec(memory_space=pltpu.VMEM)
    scalar = pl.BlockSpec(memory_space=pltpu.SMEM)
    moved = moved or sum(x.size * x.dtype.itemsize for x in (*arrays, *out_shapes))
    return pl.pallas_call(
        body,
        in_specs=[scalar] * len(scalars) + [whole] * len(arrays),
        out_specs=[whole] * len(out_shapes),
        out_shape=out_shapes,
        cost_estimate=pl.CostEstimate(flops=flops, bytes_accessed=moved, transcendentals=0),
        compiler_params=pltpu.CompilerParams(vmem_limit_bytes=limit << 20),
    )(*scalars, *arrays)


def gate_lanes(expert_ids, gate_weights, experts):
    hits = expert_ids[:, :, None] == jnp.arange(experts, dtype=jnp.int32)[None, None, :]
    gates = jnp.sum(jnp.where(hits, gate_weights[:, :, None], 0.0), axis=1)
    pieces = []
    for _ in range(3):
        piece = lax.reduce_precision(gates, 8, 7)
        pieces.append(piece.astype(jnp.bfloat16))
        gates = gates - piece
    lanes = jnp.concatenate(pieces, axis=1)
    return jnp.pad(lanes, ((0, 0), (0, -lanes.shape[1] % 128)))


def crossed(block, first, name="flip"):
    cores, count = lax.axis_size("tok"), lax.axis_size("blk")
    route = []
    for core in range(cores):
        mask = 1 if (core % 2 == 0) == first else 2
        route += [(core * count + i, core * count + (i ^ mask)) for i in range(count)]
    with jax.named_scope(name):
        return lax.ppermute(block, ("tok", "blk"), route)


def expert_kernel(experts, ahead, place_ref, near_ref, far_ref, gate_ref, up_ref, down_ref, *outs):
    width = gate_ref.shape[1]
    parts = len(outs)
    blocks, part_rows, part_width = outs[0].shape
    held = jnp.concatenate([near_ref[...], far_ref[...]], axis=0)
    rows = held[:, :width]
    lanes = held[:, width:].astype(jnp.float32)
    lane_ids = lax.broadcasted_iota(jnp.int32, lanes.shape, 1)
    named = (lane_ids < 3 * experts) & (lane_ids % experts == place_ref[0])
    weight = jnp.sum(jnp.where(named, lanes, 0.0), axis=1, keepdims=True)
    turned = (((1,), (1,)), ((), ()))
    gate_act = lax.dot_general(rows, gate_ref[...], turned, preferred_element_type=jnp.float32)
    up_act = lax.dot_general(rows, up_ref[...], turned, preferred_element_type=jnp.float32)
    hidden = (gate_act / (1.0 + jnp.exp(-gate_act)) * up_act).astype(jnp.bfloat16)
    for part in range(parts):
        start = lax.rem(place_ref[1] + part, parts) * part_width
        columns = pl.ds(pl.multiple_of(start, 128), part_width)
        product = jnp.dot(hidden, down_ref[:, columns], preferred_element_type=jnp.float32)
        product = (weight * product).astype(jnp.bfloat16)
        order = (0, 2, 1, 3) if (part - ahead) % 2 else (0, 1, 2, 3)
        for block in range(blocks):
            outs[part][order[block]] = product[block * part_rows : (block + 1) * part_rows]


def run_expert(place, near, far, w_gate, w_up, w_down, experts, parts, ahead):
    count = 2 * near.shape[0]
    units, width = w_gate.shape
    out_shape = jax.ShapeDtypeStruct((PLANE, count // PLANE, width // parts), jnp.bfloat16)
    return local_call(
        functools.partial(expert_kernel, experts, ahead),
        [out_shape] * parts,
        [place],
        [near, far, w_gate, w_up, w_down],
        flops=6 * count * width * units,
        moved=count,
    )


def wide(block):
    return block.astype(jnp.float32)


def narrow(block):
    return block.astype(jnp.bfloat16)


def second_share(totals):
    return narrow(jnp.stack([total[2:4] for total in totals]))


def first_share(totals):
    return narrow(jnp.stack([total[1] for total in totals]))


def merged(totals, got, count):
    return [total[0:count] + wide(got[i]) for i, total in enumerate(totals)]


def expert_outputs(place, near, far, weights, experts, cores, waits):
    outs = []
    for ahead in range(cores):
        near_rows = from_core(near, ahead) if ahead else near
        far_rows = from_core(far, ahead) if ahead else far
        near_rows = after(near_rows, *outs[-1:], *waits.get(ahead, []))
        outs.append(run_expert(place, near_rows, far_rows, *weights, experts, cores, ahead))
    return outs


def core_totals(outs, cores):
    totals = []
    for rows_of in range(cores):
        total = wide(outs[rows_of][0])
        for ahead in range(1, cores):
            sent = outs[(rows_of + ahead) % cores][ahead]
            total = total + wide(from_core(sent, cores - ahead))
        totals.append(total)
    return totals


def on_device(
    q_proj,
    k_proj,
    v_proj,
    residual,
    prompt_lengths,
    expert_ids,
    gate_weights,
    page_table,
    out_weight,
    norm_gain,
    w_gate,
    w_up,
    w_down,
):
    tok_rows = q_proj.shape[0]
    col_width = residual.shape[1]
    model_width = norm_gain.shape[0]
    blk_index = lax.axis_index("blk")
    tok_index = lax.axis_index("tok")
    cores = lax.axis_size("tok")
    experts = lax.axis_size("blk")
    planes = experts // PLANE
    place = jnp.stack([blk_index, tok_index]).astype(jnp.int32)
    part_rows = tok_rows // cores
    half_dim = HEAD_DIM // 2
    inv_freq = 10000.0 ** (-jnp.arange(half_dim, dtype=jnp.float32) / half_dim)
    freq = jnp.concatenate([inv_freq, inv_freq])[None, :]
    rotated = jax.ShapeDtypeStruct(q_proj.shape, jnp.bfloat16)
    rot_query, rot_keys = local_call(
        rope_kernel, [rotated] * 2, [place, prompt_lengths], [freq, q_proj, k_proj]
    )
    column = blk_index % PLANE
    key_blocks, value_blocks = [
        [block, next_plane(block)] for block in (rot_keys, after(v_proj, rot_keys))
    ]
    for blocks in (key_blocks, value_blocks):
        own, below = blocks
        for mask in range(1, PLANE):
            blocks.append(flipped(jnp.where(column < column ^ mask, own, below), mask))
    heads = q_proj.shape[1] // HEAD_DIM
    probs_shape = (heads, tok_rows, len(key_blocks) * tok_rows)
    probs = local_call(
        score_kernel,
        [jax.ShapeDtypeStruct(probs_shape, jnp.bfloat16)],
        [place, prompt_lengths],
        [rot_query, *key_blocks],
        flops=2 * tok_rows * probs_shape[2] * heads * HEAD_DIM,
    )[0]
    page_count = tok_rows // PAGE
    local_page = page_table - blk_index * page_count
    kv_rows = jnp.stack([rot_keys, v_proj], axis=1).reshape(page_count, PAGE, 2, -1)
    kv_pages = jnp.zeros_like(kv_rows).at[local_page].set(kv_rows)
    lanes = gate_lanes(expert_ids, gate_weights, experts)
    probs = after(probs, kv_pages, lanes)
    mixed = local_call(
        mix_kernel,
        [jax.ShapeDtypeStruct((tok_rows, model_width), jnp.float32)],
        [place],
        [probs, out_weight, residual, *value_blocks],
        flops=2 * tok_rows * (probs_shape[2] + model_width) * heads * HEAD_DIM,
    )[0]
    if cores == 2:
        addends = [mixed, from_core(mixed, 1)]
    else:
        addends = [lax.psum(mixed, "tok")]
    payload, own_share = local_call(
        norm_kernel,
        [
            jax.ShapeDtypeStruct((part_rows, model_width + lanes.shape[1]), jnp.bfloat16),
            jax.ShapeDtypeStruct((tok_rows, col_width), jnp.bfloat16),
        ],
        [place],
        [norm_gain[None, :], lanes, *addends],
    )
    weights = (w_gate[0].T, w_up[0].T, w_down[0])
    size = 1 if planes <= 4 else 4
    groups = [[0]] + [
        list(range(i, min(i + size, planes))) for i in range(1, planes, size)
    ]
    weights = (w_gate[0].T, w_up[0].T, w_down[0])
    columns, nears, fars = [], [], []
    every, seconds, firsts, ready, returned = [], [], [], [], []
    for step in range(len(groups) + 1):
        if step < len(groups):
            source = after(payload, nears[step - 2]) if step > 1 else payload
            column = jnp.concatenate(
                [from_plane(source, ahead) if ahead else source for ahead in groups[step]]
            )
            waits = [*nears[-1:]]
            if step > 1:
                waits.append(fars[step - 2])
            if step > 2:
                waits.append(every[step - 3])
            columns.append(after(column, *waits))
            got = crossed(columns[-1], True, f"gather_first_{step}")
            nears.append(jnp.concatenate([columns[-1], got]))
        if step == 0:
            continue
        number, group = step - 1, groups[step - 1]
        fars.append(crossed(nears[number], False, f"gather_second_{number}"))
        waits = {0: [*every[-1:], *nears[step : step + 1]], cores - 1: []}
        if number > 0:
            waits[cores - 1].append(seconds[-1])
        if number > 1:
            waits[0].append(firsts[-2])
            waits[cores - 1].append(ready[-2])
        far = after(fars[number], *[outs[0] for outs in every[-1:]])
        outs = expert_outputs(place, nears[number], far, weights, experts, cores, waits)
        every.append(outs)
        totals = core_totals(outs, cores)
        seconds.append(second_share(totals))
        totals = merged(totals, crossed(seconds[-1], False, f"scatter_second_{number}"), 2)
        firsts.append(first_share(totals))
        came = crossed(firsts[-1], True, f"scatter_first_{number}")
        rows_of = merged([total[0] for total in totals], came, None)
        if group == [0]:
            moe = jnp.concatenate(rows_of)
            ready.append(moe)
            continue
        blocks = []
        for i in range(len(group)):
            piece = [rows[i * part_rows : (i + 1) * part_rows] for rows in rows_of]
            blocks.append(narrow(jnp.concatenate(piece)))
        ready.append(blocks)
        returned += [to_plane(block, ahead) for block, ahead in zip(blocks, group, strict=True)]
    moe = moe + sum(wide(block) for block in returned)
    moe = jnp.roll(moe.reshape(cores, part_rows, col_width), tok_index, axis=0)
    moe = moe.reshape(tok_rows, col_width)
    layer_out = (own_share.astype(jnp.float32) + moe).astype(jnp.bfloat16)
    return (layer_out, kv_pages)


def solution(mesh):
    placed = (
        P("blk", "tok"),
        P("blk", "tok"),
        P("blk", "tok"),
        P("blk", "tok"),
        P(),
        P("blk", None),
        P("blk", None),
        P("blk"),
        P("tok", None),
        P(),
        P("blk", None, "tok"),
        P("blk", None, "tok"),
        P("blk", "tok", None),
    )
    return jax.shard_map(
        on_device,
        mesh=mesh,
        in_specs=placed,
        out_specs=(P("blk", "tok"), P("blk", None, None, "tok")),
        check_vma=False,
    )
```

```python
import functools

import jax
import jax.numpy as jnp
from jax import lax
from jax.experimental import pallas as pl
from jax.experimental.pallas import tpu as pltpu
from jax.sharding import PartitionSpec as P

HEAD_DIM = 128
REACH = 4
PAGE = 16
PLANE = 4
EPSILON = 1e-06


def after(value, *others):
    return lax.optimization_barrier((value, *others))[0]


def flipped(block, mask):
    return lax.ppermute(block, "blk", [(i, i ^ mask) for i in range(lax.axis_size("blk"))])


def next_plane(block):
    count = lax.axis_size("blk")
    return lax.ppermute(block, "blk", [(i, i + PLANE) for i in range(count - PLANE)])


def from_plane(block, ahead):
    count = lax.axis_size("blk")
    with jax.named_scope(f"from_plane_{ahead}"):
        return lax.ppermute(
            block, "blk", [((i + PLANE * ahead) % count, i) for i in range(count)]
        )


def to_plane(block, ahead):
    count = lax.axis_size("blk")
    with jax.named_scope(f"to_plane_{ahead}"):
        return lax.ppermute(
            block, "blk", [(i, (i + PLANE * ahead) % count) for i in range(count)]
        )


def from_core(block, ahead):
    count = lax.axis_size("tok")
    return lax.ppermute(block, "tok", [((i + ahead) % count, i) for i in range(count)])


def segment_starts(place_ref, lengths_ref, shape):
    token = place_ref[0] * shape[0] + lax.broadcasted_iota(jnp.int32, shape, 0)
    start = jnp.zeros(shape, jnp.int32)
    end = jnp.int32(0)
    for i in range(lengths_ref.shape[0]):
        end = end + lengths_ref[i]
        start = jnp.where(token >= end, end, start)
    return token, start


def rope_kernel(place_ref, lengths_ref, freq_ref, q_ref, k_ref, q_out, k_out):
    rows, width = q_ref.shape
    shape = (rows, HEAD_DIM)
    token, start = segment_starts(place_ref, lengths_ref, shape)
    angle = (token - start).astype(jnp.float32) * freq_ref[...]
    cosine, sine = jnp.cos(angle), jnp.sin(angle)
    lane = lax.broadcasted_iota(jnp.int32, shape, 1)
    sine = jnp.where(lane < HEAD_DIM // 2, -sine, sine)
    for source, target in ((k_ref, k_out), (q_ref, q_out)):
        for head in range(width // HEAD_DIM):
            columns = slice(head * HEAD_DIM, (head + 1) * HEAD_DIM)
            x = source[:, columns].astype(jnp.float32)
            turned = x * cosine + pltpu.roll(x, HEAD_DIM // 2, 1) * sine
            target[:, columns] = turned.astype(jnp.bfloat16)


def score_kernel(place_ref, lengths_ref, q_ref, *rest):
    *keys, out_ref = rest
    rows, width = q_ref.shape
    shape = (rows, rows)
    token, start = segment_starts(place_ref, lengths_ref, shape)
    blk = place_ref[0]
    column = lax.rem(blk, PLANE)
    bases = [blk, blk - PLANE]
    for mask in range(1, PLANE):
        other = column ^ mask
        bases.append(blk - column + other - jnp.where(other > column, PLANE, 0))
    lane = lax.broadcasted_iota(jnp.int32, shape, 1)
    ids = jnp.concatenate([base * rows + lane for base in bases], axis=1)
    token = jnp.concatenate([token] * len(keys), axis=1)
    start = jnp.concatenate([start] * len(keys), axis=1)
    allowed = (ids >= start) & (ids <= token)
    for head in range(width // HEAD_DIM):
        columns = slice(head * HEAD_DIM, (head + 1) * HEAD_DIM)
        key = jnp.concatenate([ref[:, columns] for ref in keys], axis=0)
        scores = lax.dot_general(
            q_ref[:, columns],
            key,
            (((1,), (1,)), ((), ())),
            preferred_element_type=jnp.float32,
        )
        scores = jnp.where(allowed, scores * HEAD_DIM ** (-0.5), -1e30)
        terms = jnp.exp(scores - jnp.max(scores, axis=1, keepdims=True))
        share = 1.0 / jnp.sum(terms, axis=1, keepdims=True)
        out_ref[head] = (terms * share).astype(jnp.bfloat16)


def mix_kernel(place_ref, prob_ref, weight_ref, residual_ref, *rest):
    *values, out_ref = rest
    heads = prob_ref.shape[0]
    mixed = []
    for head in range(heads):
        columns = slice(head * HEAD_DIM, (head + 1) * HEAD_DIM)
        value = jnp.concatenate([ref[:, columns] for ref in values], axis=0)
        product = jnp.dot(prob_ref[head], value, preferred_element_type=jnp.float32)
        mixed.append(product.astype(jnp.bfloat16))
    attention = jnp.concatenate(mixed, axis=1)
    out_ref[...] = jnp.dot(attention, weight_ref[...], preferred_element_type=jnp.float32)
    width = residual_ref.shape[1]
    own = pl.ds(pl.multiple_of(place_ref[1] * width, 128), width)
    out_ref[:, own] = out_ref[:, own] + residual_ref[...].astype(jnp.float32)


def norm_kernel(place_ref, gain_ref, lanes_ref, *rest):
    *addends, rows_out, share_out = rest
    rows, width = addends[0].shape
    part_rows = rows_out.shape[0]
    part_width = share_out.shape[1]
    own = pl.ds(pl.multiple_of(place_ref[1] * part_width, 128), part_width)
    share_out[...] = sum(ref[:, own] for ref in addends).astype(jnp.bfloat16)
    part = pl.ds(pl.multiple_of(place_ref[1] * part_rows, 16), part_rows)
    stream = sum(ref[part, :] for ref in addends).astype(jnp.bfloat16).astype(jnp.float32)
    scale = lax.rsqrt(jnp.mean(stream * stream, axis=1, keepdims=True) + EPSILON)
    rows_out[:, :width] = (stream * scale * gain_ref[...]).astype(jnp.bfloat16)
    rows_out[:, width:] = lanes_ref[part, :]


def local_call(body, out_shapes, scalars, arrays, flops=0, moved=0, limit=16):
    whole = pl.BlockSpec(memory_space=pltpu.VMEM)
    scalar = pl.BlockSpec(memory_space=pltpu.SMEM)
    moved = moved or sum(x.size * x.dtype.itemsize for x in (*arrays, *out_shapes))
    return pl.pallas_call(
        body,
        in_specs=[scalar] * len(scalars) + [whole] * len(arrays),
        out_specs=[whole] * len(out_shapes),
        out_shape=out_shapes,
        cost_estimate=pl.CostEstimate(flops=flops, bytes_accessed=moved, transcendentals=0),
        compiler_params=pltpu.CompilerParams(vmem_limit_bytes=limit << 20),
    )(*scalars, *arrays)


def gate_lanes(expert_ids, gate_weights, experts):
    hits = expert_ids[:, :, None] == jnp.arange(experts, dtype=jnp.int32)[None, None, :]
    gates = jnp.sum(jnp.where(hits, gate_weights[:, :, None], 0.0), axis=1)
    pieces = []
    for _ in range(3):
        piece = lax.reduce_precision(gates, 8, 7)
        pieces.append(piece.astype(jnp.bfloat16))
        gates = gates - piece
    lanes = jnp.concatenate(pieces, axis=1)
    return jnp.pad(lanes, ((0, 0), (0, -lanes.shape[1] % 128)))


def crossed(block, first, name="flip"):
    cores, count = lax.axis_size("tok"), lax.axis_size("blk")
    route = []
    for core in range(cores):
        mask = 1 if (core % 2 == 0) == first else 2
        route += [(core * count + i, core * count + (i ^ mask)) for i in range(count)]
    with jax.named_scope(name):
        return lax.ppermute(block, ("tok", "blk"), route)


def expert_kernel(experts, ahead, place_ref, near_ref, far_ref, gate_ref, up_ref, down_ref, *outs):
    width = gate_ref.shape[1]
    parts = len(outs)
    blocks, part_rows, part_width = outs[0].shape
    held = jnp.concatenate([near_ref[...], far_ref[...]], axis=0)
    rows = held[:, :width]
    lanes = held[:, width:].astype(jnp.float32)
    lane_ids = lax.broadcasted_iota(jnp.int32, lanes.shape, 1)
    named = (lane_ids < 3 * experts) & (lane_ids % experts == place_ref[0])
    weight = jnp.sum(jnp.where(named, lanes, 0.0), axis=1, keepdims=True)
    turned = (((1,), (1,)), ((), ()))
    gate_act = lax.dot_general(rows, gate_ref[...], turned, preferred_element_type=jnp.float32)
    up_act = lax.dot_general(rows, up_ref[...], turned, preferred_element_type=jnp.float32)
    hidden = (gate_act / (1.0 + jnp.exp(-gate_act)) * up_act).astype(jnp.bfloat16)
    for part in range(parts):
        start = lax.rem(place_ref[1] + part, parts) * part_width
        columns = pl.ds(pl.multiple_of(start, 128), part_width)
        product = jnp.dot(hidden, down_ref[:, columns], preferred_element_type=jnp.float32)
        product = (weight * product).astype(jnp.bfloat16)
        order = (0, 2, 1, 3) if (part - ahead) % 2 else (0, 1, 2, 3)
        for block in range(blocks):
            outs[part][order[block]] = product[block * part_rows : (block + 1) * part_rows]


def run_expert(place, near, far, w_gate, w_up, w_down, experts, parts, ahead, light):
    count = 2 * near.shape[0]
    units, width = w_gate.shape
    out_shape = jax.ShapeDtypeStruct((PLANE, count // PLANE, width // parts), jnp.bfloat16)
    return local_call(
        functools.partial(expert_kernel, experts, ahead),
        [out_shape] * parts,
        [place],
        [near, far, w_gate, w_up, w_down],
        flops=count if light else 6 * count * width * units,
        moved=count,
    )


def wide(block):
    return block.astype(jnp.float32)


def narrow(block):
    return block.astype(jnp.bfloat16)


def second_share(totals):
    return narrow(jnp.stack([total[2:4] for total in totals]))


def first_share(totals):
    return narrow(jnp.stack([total[1] for total in totals]))


def merged(totals, got, count):
    return [total[0:count] + wide(got[i]) for i, total in enumerate(totals)]


def expert_outputs(place, near, far, weights, experts, cores, waits, light):
    outs = []
    for ahead in range(cores):
        near_rows = from_core(near, ahead) if ahead else near
        far_rows = from_core(far, ahead) if ahead else far
        near_rows = after(near_rows, *outs[-1:], *waits.get(ahead, []))
        outs.append(run_expert(place, near_rows, far_rows, *weights, experts, cores, ahead, light))
    return outs


def core_totals(outs, cores):
    totals = []
    for rows_of in range(cores):
        total = wide(outs[rows_of][0])
        for ahead in range(1, cores):
            sent = outs[(rows_of + ahead) % cores][ahead]
            total = total + wide(from_core(sent, cores - ahead))
        totals.append(total)
    return totals


def on_device(
    q_proj,
    k_proj,
    v_proj,
    residual,
    prompt_lengths,
    expert_ids,
    gate_weights,
    page_table,
    out_weight,
    norm_gain,
    w_gate,
    w_up,
    w_down,
):
    tok_rows = q_proj.shape[0]
    col_width = residual.shape[1]
    model_width = norm_gain.shape[0]
    blk_index = lax.axis_index("blk")
    tok_index = lax.axis_index("tok")
    cores = lax.axis_size("tok")
    experts = lax.axis_size("blk")
    planes = experts // PLANE
    place = jnp.stack([blk_index, tok_index]).astype(jnp.int32)
    part_rows = tok_rows // cores
    half_dim = HEAD_DIM // 2
    inv_freq = 10000.0 ** (-jnp.arange(half_dim, dtype=jnp.float32) / half_dim)
    freq = jnp.concatenate([inv_freq, inv_freq])[None, :]
    rotated = jax.ShapeDtypeStruct(q_proj.shape, jnp.bfloat16)
    rot_query, rot_keys = local_call(
        rope_kernel, [rotated] * 2, [place, prompt_lengths], [freq, q_proj, k_proj]
    )
    column = blk_index % PLANE
    key_blocks, value_blocks = [
        [block, next_plane(block)] for block in (rot_keys, after(v_proj, rot_keys))
    ]
    for blocks in (key_blocks, value_blocks):
        own, below = blocks
        for mask in range(1, PLANE):
            blocks.append(flipped(jnp.where(column < column ^ mask, own, below), mask))
    heads = q_proj.shape[1] // HEAD_DIM
    probs_shape = (heads, tok_rows, len(key_blocks) * tok_rows)
    probs = local_call(
        score_kernel,
        [jax.ShapeDtypeStruct(probs_shape, jnp.bfloat16)],
        [place, prompt_lengths],
        [rot_query, *key_blocks],
        flops=2 * tok_rows * probs_shape[2] * heads * HEAD_DIM,
    )[0]
    page_count = tok_rows // PAGE
    local_page = page_table - blk_index * page_count
    kv_rows = jnp.stack([rot_keys, v_proj], axis=1).reshape(page_count, PAGE, 2, -1)
    kv_pages = jnp.zeros_like(kv_rows).at[local_page].set(kv_rows)
    lanes = gate_lanes(expert_ids, gate_weights, experts)
    probs = after(probs, kv_pages, lanes)
    mixed = local_call(
        mix_kernel,
        [jax.ShapeDtypeStruct((tok_rows, model_width), jnp.float32)],
        [place],
        [probs, out_weight, residual, *value_blocks],
        flops=2 * tok_rows * (probs_shape[2] + model_width) * heads * HEAD_DIM,
    )[0]
    if cores == 2:
        addends = [mixed, from_core(mixed, 1)]
    else:
        addends = [lax.psum(mixed, "tok")]
    payload, own_share = local_call(
        norm_kernel,
        [
            jax.ShapeDtypeStruct((part_rows, model_width + lanes.shape[1]), jnp.bfloat16),
            jax.ShapeDtypeStruct((tok_rows, col_width), jnp.bfloat16),
        ],
        [place],
        [norm_gain[None, :], lanes, *addends],
    )
    weights = (w_gate[0].T, w_up[0].T, w_down[0])
    size = 1 if planes <= 4 else 4
    groups = [[0]] + [
        list(range(i, min(i + size, planes))) for i in range(1, planes, size)
    ]
    weights = (w_gate[0].T, w_up[0].T, w_down[0])
    columns, nears, fars = [], [], []
    every, seconds, firsts, ready, returned = [], [], [], [], []
    for step in range(len(groups) + 1):
        if step < len(groups):
            blocks = []
            for ahead in groups[step]:
                source = from_plane(source, 1) if ahead else payload
                blocks.append(source)
            column = jnp.concatenate(blocks)
            waits = [*nears[-1:]]
            if step > 1:
                waits.append(fars[step - 2])
                waits.append(every[step - 2][0])
            columns.append(after(column, *waits))
            got = crossed(columns[-1], True, f"gather_first_{step}")
            nears.append(jnp.concatenate([columns[-1], got]))
        if step == 0:
            continue
        number, group = step - 1, groups[step - 1]
        fars.append(crossed(nears[number], False, f"gather_second_{number}"))
        waits = {0: [*every[-1:], *nears[step : step + 1]], cores - 1: []}
        if number > 0:
            waits[cores - 1].append(seconds[-1])
        if number > 2:
            waits[0].append(firsts[-2])
            waits[cores - 1].append(ready[-2])
        far = after(fars[number], *[outs[0] for outs in every[-1:]])
        light = number == len(groups) - 1
        outs = expert_outputs(place, nears[number], far, weights, experts, cores, waits, light)
        every.append(outs)
        totals = core_totals(outs, cores)
        seconds.append(after(second_share(totals), *firsts[-1:]))
        if number == 0:
            own_totals = totals
            continue
        totals = merged(totals, crossed(seconds[-1], False, f"scatter_second_{number}"), 2)
        firsts.append(first_share(totals))
        came = crossed(firsts[-1], True, f"scatter_first_{number}")
        rows_of = merged([total[0] for total in totals], came, None)
        blocks = []
        for i in range(len(group)):
            piece = [rows[i * part_rows : (i + 1) * part_rows] for rows in rows_of]
            blocks.append(narrow(jnp.concatenate(piece)))
        ready.append(blocks)
        returned += [to_plane(block, ahead) for block, ahead in zip(blocks, group, strict=True)]
    got = crossed(after(seconds[0], firsts[-1]), False, "scatter_second_0")
    totals = merged(own_totals, got, 2)
    got = crossed(first_share(totals), True, "scatter_first_0")
    moe = jnp.concatenate(merged([total[0] for total in totals], got, None))
    moe = moe + sum(wide(block) for block in returned)
    moe = jnp.roll(moe.reshape(cores, part_rows, col_width), tok_index, axis=0)
    moe = moe.reshape(tok_rows, col_width)
    layer_out = (own_share.astype(jnp.float32) + moe).astype(jnp.bfloat16)
    return (layer_out, kv_pages)


def solution(mesh):
    placed = (
        P("blk", "tok"),
        P("blk", "tok"),
        P("blk", "tok"),
        P("blk", "tok"),
        P(),
        P("blk", None),
        P("blk", None),
        P("blk"),
        P("tok", None),
        P(),
        P("blk", None, "tok"),
        P("blk", None, "tok"),
        P("blk", "tok", None),
    )
    return jax.shard_map(
        on_device,
        mesh=mesh,
        in_specs=placed,
        out_specs=(P("blk", "tok"), P("blk", None, None, "tok")),
        check_vma=False,
    )
```

```python
import functools

import jax
import jax.numpy as jnp
from jax import lax
from jax.experimental import pallas as pl
from jax.experimental.pallas import tpu as pltpu
from jax.sharding import PartitionSpec as P

HEAD_DIM = 128
REACH = 4
PAGE = 16
PLANE = 4
EPSILON = 1e-06


def after(value, *others):
    return lax.optimization_barrier((value, *others))[0]


def flipped(block, mask):
    return lax.ppermute(block, "blk", [(i, i ^ mask) for i in range(lax.axis_size("blk"))])


def next_plane(block):
    count = lax.axis_size("blk")
    return lax.ppermute(block, "blk", [(i, i + PLANE) for i in range(count - PLANE)])


def from_plane(block, ahead):
    count = lax.axis_size("blk")
    with jax.named_scope(f"from_plane_{ahead}"):
        return lax.ppermute(
            block, "blk", [((i + PLANE * ahead) % count, i) for i in range(count)]
        )


def to_plane(block, ahead):
    count = lax.axis_size("blk")
    with jax.named_scope(f"to_plane_{ahead}"):
        return lax.ppermute(
            block, "blk", [(i, (i + PLANE * ahead) % count) for i in range(count)]
        )


def from_core(block, ahead):
    count = lax.axis_size("tok")
    return lax.ppermute(block, "tok", [((i + ahead) % count, i) for i in range(count)])


def segment_starts(place_ref, lengths_ref, shape):
    token = place_ref[0] * shape[0] + lax.broadcasted_iota(jnp.int32, shape, 0)
    start = jnp.zeros(shape, jnp.int32)
    end = jnp.int32(0)
    for i in range(lengths_ref.shape[0]):
        end = end + lengths_ref[i]
        start = jnp.where(token >= end, end, start)
    return token, start


def rope_kernel(place_ref, lengths_ref, freq_ref, q_ref, k_ref, q_out, k_out):
    rows, width = q_ref.shape
    shape = (rows, HEAD_DIM)
    token, start = segment_starts(place_ref, lengths_ref, shape)
    angle = (token - start).astype(jnp.float32) * freq_ref[...]
    cosine, sine = jnp.cos(angle), jnp.sin(angle)
    lane = lax.broadcasted_iota(jnp.int32, shape, 1)
    sine = jnp.where(lane < HEAD_DIM // 2, -sine, sine)
    for source, target in ((k_ref, k_out), (q_ref, q_out)):
        for head in range(width // HEAD_DIM):
            columns = slice(head * HEAD_DIM, (head + 1) * HEAD_DIM)
            x = source[:, columns].astype(jnp.float32)
            turned = x * cosine + pltpu.roll(x, HEAD_DIM // 2, 1) * sine
            target[:, columns] = turned.astype(jnp.bfloat16)


def score_kernel(place_ref, lengths_ref, q_ref, *rest):
    *keys, out_ref = rest
    rows, width = q_ref.shape
    shape = (rows, rows)
    token, start = segment_starts(place_ref, lengths_ref, shape)
    blk = place_ref[0]
    column = lax.rem(blk, PLANE)
    bases = [blk, blk - PLANE]
    for mask in range(1, PLANE):
        other = column ^ mask
        bases.append(blk - column + other - jnp.where(other > column, PLANE, 0))
    lane = lax.broadcasted_iota(jnp.int32, shape, 1)
    ids = jnp.concatenate([base * rows + lane for base in bases], axis=1)
    token = jnp.concatenate([token] * len(keys), axis=1)
    start = jnp.concatenate([start] * len(keys), axis=1)
    allowed = (ids >= start) & (ids <= token)
    for head in range(width // HEAD_DIM):
        columns = slice(head * HEAD_DIM, (head + 1) * HEAD_DIM)
        key = jnp.concatenate([ref[:, columns] for ref in keys], axis=0)
        scores = lax.dot_general(
            q_ref[:, columns],
            key,
            (((1,), (1,)), ((), ())),
            preferred_element_type=jnp.float32,
        )
        scores = jnp.where(allowed, scores * HEAD_DIM ** (-0.5), -1e30)
        terms = jnp.exp(scores - jnp.max(scores, axis=1, keepdims=True))
        share = 1.0 / jnp.sum(terms, axis=1, keepdims=True)
        out_ref[head] = (terms * share).astype(jnp.bfloat16)


def mix_kernel(place_ref, prob_ref, weight_ref, residual_ref, *rest):
    *values, out_ref = rest
    heads = prob_ref.shape[0]
    mixed = []
    for head in range(heads):
        columns = slice(head * HEAD_DIM, (head + 1) * HEAD_DIM)
        value = jnp.concatenate([ref[:, columns] for ref in values], axis=0)
        product = jnp.dot(prob_ref[head], value, preferred_element_type=jnp.float32)
        mixed.append(product.astype(jnp.bfloat16))
    attention = jnp.concatenate(mixed, axis=1)
    out_ref[...] = jnp.dot(attention, weight_ref[...], preferred_element_type=jnp.float32)
    width = residual_ref.shape[1]
    own = pl.ds(pl.multiple_of(place_ref[1] * width, 128), width)
    out_ref[:, own] = out_ref[:, own] + residual_ref[...].astype(jnp.float32)


def norm_kernel(place_ref, gain_ref, lanes_ref, *rest):
    *addends, rows_out, share_out = rest
    rows, width = addends[0].shape
    part_rows = rows_out.shape[0]
    part_width = share_out.shape[1]
    own = pl.ds(pl.multiple_of(place_ref[1] * part_width, 128), part_width)
    share_out[...] = sum(ref[:, own] for ref in addends).astype(jnp.bfloat16)
    part = pl.ds(pl.multiple_of(place_ref[1] * part_rows, 16), part_rows)
    stream = sum(ref[part, :] for ref in addends).astype(jnp.bfloat16).astype(jnp.float32)
    scale = lax.rsqrt(jnp.mean(stream * stream, axis=1, keepdims=True) + EPSILON)
    rows_out[:, :width] = (stream * scale * gain_ref[...]).astype(jnp.bfloat16)
    rows_out[:, width:] = lanes_ref[part, :]


def local_call(body, out_shapes, scalars, arrays, flops=0, moved=0, limit=16):
    whole = pl.BlockSpec(memory_space=pltpu.VMEM)
    scalar = pl.BlockSpec(memory_space=pltpu.SMEM)
    moved = moved or sum(x.size * x.dtype.itemsize for x in (*arrays, *out_shapes))
    return pl.pallas_call(
        body,
        in_specs=[scalar] * len(scalars) + [whole] * len(arrays),
        out_specs=[whole] * len(out_shapes),
        out_shape=out_shapes,
        cost_estimate=pl.CostEstimate(flops=flops, bytes_accessed=moved, transcendentals=0),
        compiler_params=pltpu.CompilerParams(vmem_limit_bytes=limit << 20),
    )(*scalars, *arrays)


def gate_lanes(expert_ids, gate_weights, experts):
    hits = expert_ids[:, :, None] == jnp.arange(experts, dtype=jnp.int32)[None, None, :]
    gates = jnp.sum(jnp.where(hits, gate_weights[:, :, None], 0.0), axis=1)
    pieces = []
    for _ in range(3):
        piece = lax.reduce_precision(gates, 8, 7)
        pieces.append(piece.astype(jnp.bfloat16))
        gates = gates - piece
    lanes = jnp.concatenate(pieces, axis=1)
    return jnp.pad(lanes, ((0, 0), (0, -lanes.shape[1] % 128)))


def crossed(block, first, name="flip"):
    cores, count = lax.axis_size("tok"), lax.axis_size("blk")
    route = []
    for core in range(cores):
        mask = 1 if (core % 2 == 0) == first else 2
        route += [(core * count + i, core * count + (i ^ mask)) for i in range(count)]
    with jax.named_scope(name):
        return lax.ppermute(block, ("tok", "blk"), route)


def expert_kernel(experts, ahead, place_ref, near_ref, far_ref, gate_ref, up_ref, down_ref, *outs):
    width = gate_ref.shape[1]
    parts = len(outs)
    blocks, part_rows, part_width = outs[0].shape
    held = jnp.concatenate([near_ref[...], far_ref[...]], axis=0)
    rows = held[:, :width]
    lanes = held[:, width:].astype(jnp.float32)
    lane_ids = lax.broadcasted_iota(jnp.int32, lanes.shape, 1)
    named = (lane_ids < 3 * experts) & (lane_ids % experts == place_ref[0])
    weight = jnp.sum(jnp.where(named, lanes, 0.0), axis=1, keepdims=True)
    turned = (((1,), (1,)), ((), ()))
    gate_act = lax.dot_general(rows, gate_ref[...], turned, preferred_element_type=jnp.float32)
    up_act = lax.dot_general(rows, up_ref[...], turned, preferred_element_type=jnp.float32)
    hidden = (gate_act / (1.0 + jnp.exp(-gate_act)) * up_act).astype(jnp.bfloat16)
    for part in range(parts):
        start = lax.rem(place_ref[1] + part, parts) * part_width
        columns = pl.ds(pl.multiple_of(start, 128), part_width)
        product = jnp.dot(hidden, down_ref[:, columns], preferred_element_type=jnp.float32)
        product = (weight * product).astype(jnp.bfloat16)
        order = (0, 2, 1, 3) if (part - ahead) % 2 else (0, 1, 2, 3)
        for block in range(blocks):
            outs[part][order[block]] = product[block * part_rows : (block + 1) * part_rows]


def run_expert(place, near, far, w_gate, w_up, w_down, experts, parts, ahead):
    count = 2 * near.shape[0]
    units, width = w_gate.shape
    out_shape = jax.ShapeDtypeStruct((PLANE, count // PLANE, width // parts), jnp.bfloat16)
    return local_call(
        functools.partial(expert_kernel, experts, ahead),
        [out_shape] * parts,
        [place],
        [near, far, w_gate, w_up, w_down],
        flops=6 * count * width * units,
    )


def wide(block):
    return block.astype(jnp.float32)


def narrow(block):
    return block.astype(jnp.bfloat16)


def second_share(totals):
    return narrow(jnp.stack([total[2:4] for total in totals]))


def first_share(totals):
    return narrow(jnp.stack([total[1] for total in totals]))


def merged(totals, got, count):
    return [total[0:count] + wide(got[i]) for i, total in enumerate(totals)]


def expert_outputs(place, near, far, weights, experts, cores, waits):
    outs = []
    for ahead in range(cores):
        near_rows = from_core(near, ahead) if ahead else near
        far_rows = from_core(far, ahead) if ahead else far
        near_rows = after(near_rows, *outs[-1:], *waits.get(ahead, []))
        outs.append(run_expert(place, near_rows, far_rows, *weights, experts, cores, ahead))
    return outs


def core_totals(outs, cores, *waits):
    totals = []
    for rows_of in range(cores):
        total = wide(outs[rows_of][0])
        for ahead in range(1, cores):
            sent = outs[(rows_of + ahead) % cores][ahead]
            total = total + wide(after(from_core(sent, cores - ahead), *waits))
        totals.append(total)
    return totals


def on_device(
    q_proj,
    k_proj,
    v_proj,
    residual,
    prompt_lengths,
    expert_ids,
    gate_weights,
    page_table,
    out_weight,
    norm_gain,
    w_gate,
    w_up,
    w_down,
):
    tok_rows = q_proj.shape[0]
    col_width = residual.shape[1]
    model_width = norm_gain.shape[0]
    blk_index = lax.axis_index("blk")
    tok_index = lax.axis_index("tok")
    cores = lax.axis_size("tok")
    experts = lax.axis_size("blk")
    planes = experts // PLANE
    place = jnp.stack([blk_index, tok_index]).astype(jnp.int32)
    part_rows = tok_rows // cores
    half_dim = HEAD_DIM // 2
    inv_freq = 10000.0 ** (-jnp.arange(half_dim, dtype=jnp.float32) / half_dim)
    freq = jnp.concatenate([inv_freq, inv_freq])[None, :]
    rotated = jax.ShapeDtypeStruct(q_proj.shape, jnp.bfloat16)
    rot_query, rot_keys = local_call(
        rope_kernel, [rotated] * 2, [place, prompt_lengths], [freq, q_proj, k_proj]
    )
    column = blk_index % PLANE
    key_blocks, value_blocks = [
        [block, next_plane(block)] for block in (rot_keys, after(v_proj, rot_keys))
    ]
    for blocks in (key_blocks, value_blocks):
        own, below = blocks
        for mask in range(1, PLANE):
            blocks.append(flipped(jnp.where(column < column ^ mask, own, below), mask))
    heads = q_proj.shape[1] // HEAD_DIM
    probs_shape = (heads, tok_rows, len(key_blocks) * tok_rows)
    probs = local_call(
        score_kernel,
        [jax.ShapeDtypeStruct(probs_shape, jnp.bfloat16)],
        [place, prompt_lengths],
        [rot_query, *key_blocks],
        flops=2 * tok_rows * probs_shape[2] * heads * HEAD_DIM,
    )[0]
    page_count = tok_rows // PAGE
    local_page = page_table - blk_index * page_count
    kv_rows = jnp.stack([rot_keys, v_proj], axis=1).reshape(page_count, PAGE, 2, -1)
    kv_pages = jnp.zeros_like(kv_rows).at[local_page].set(kv_rows)
    lanes = gate_lanes(expert_ids, gate_weights, experts)
    probs = after(probs, kv_pages, lanes)
    mixed = local_call(
        mix_kernel,
        [jax.ShapeDtypeStruct((tok_rows, model_width), jnp.float32)],
        [place],
        [probs, out_weight, residual, *value_blocks],
        flops=2 * tok_rows * (probs_shape[2] + model_width) * heads * HEAD_DIM,
    )[0]
    if cores == 2:
        addends = [mixed, from_core(mixed, 1)]
    else:
        addends = [lax.psum(mixed, "tok")]
    payload, own_share = local_call(
        norm_kernel,
        [
            jax.ShapeDtypeStruct((part_rows, model_width + lanes.shape[1]), jnp.bfloat16),
            jax.ShapeDtypeStruct((tok_rows, col_width), jnp.bfloat16),
        ],
        [place],
        [norm_gain[None, :], lanes, *addends],
    )
    weights = (w_gate[0].T, w_up[0].T, w_down[0])
    if planes <= 4:
        groups = [[0]] + [sorted({i, planes - i}) for i in range(1, planes // 2 + 1)]
    else:
        groups = [[0]] + [list(range(i, min(i + 8, planes))) for i in range(1, planes, 8)]
    nears, fars = [], []
    for number, group in enumerate(groups):
        sent = after(payload, nears[0]) if number > 1 else payload
        column = jnp.concatenate([from_plane(sent, ahead) if ahead else sent for ahead in group])
        if number > 1:
            column = after(column, nears[-1])
        nears.append(jnp.concatenate([column, crossed(column, True, f"gather_first_{number}")]))
        fars.append(crossed(nears[-1], False, f"gather_second_{number}"))
    weights = (w_gate[0].T, w_up[0].T, w_down[0])
    run = functools.partial(
        expert_outputs, place, weights=weights, experts=experts, cores=cores
    )
    outs = run(nears[0], fars[0], waits={})
    own_totals = core_totals(outs, cores)
    sent = after(second_share(own_totals), nears[-1])
    got = crossed(sent, False, "scatter_second_0")
    own_totals = merged(own_totals, got, 2)
    own_got = crossed(first_share(own_totals), True, "scatter_first_0")
    seconds, firsts, returned = [], [], []
    for number in range(1, len(groups)):
        waits = {0: [outs], cores - 1: [got]}
        if number > 1:
            waits = {0: [outs], cores - 1: [own_got, *seconds]}
        outs = run(nears[number], fars[number], waits=waits)
        totals = core_totals(outs, cores, *firsts[-1:])
        seconds.append(second_share(totals))
        totals = merged(totals, crossed(seconds[-1], False, f"scatter_second_{number}"), 2)
        firsts.append(first_share(totals))
        came = crossed(firsts[-1], True, f"scatter_first_{number}")
        rows_of = merged([total[0] for total in totals], came, None)
        for i, ahead in enumerate(groups[number]):
            piece = [rows[i * part_rows : (i + 1) * part_rows] for rows in rows_of]
            returned.append(to_plane(narrow(jnp.concatenate(piece)), ahead))
    moe = jnp.concatenate(merged([total[0] for total in own_totals], own_got, None))
    moe = moe + sum(wide(block) for block in returned)
    moe = jnp.roll(moe.reshape(cores, part_rows, col_width), tok_index, axis=0)
    moe = moe.reshape(tok_rows, col_width)
    layer_out = (own_share.astype(jnp.float32) + moe).astype(jnp.bfloat16)
    return (layer_out, kv_pages)


def solution(mesh):
    placed = (
        P("blk", "tok"),
        P("blk", "tok"),
        P("blk", "tok"),
        P("blk", "tok"),
        P(),
        P("blk", None),
        P("blk", None),
        P("blk"),
        P("tok", None),
        P(),
        P("blk", None, "tok"),
        P("blk", None, "tok"),
        P("blk", "tok", None),
    )
    return jax.shard_map(
        on_device,
        mesh=mesh,
        in_specs=placed,
        out_specs=(P("blk", "tok"), P("blk", None, None, "tok")),
        check_vma=False,
    )
```

```python
import functools

import jax
import jax.numpy as jnp
from jax import lax
from jax.experimental import pallas as pl
from jax.experimental.pallas import tpu as pltpu
from jax.sharding import PartitionSpec as P

HEAD_DIM = 128
REACH = 4
PAGE = 16
PLANE = 4
EPSILON = 1e-06


def after(value, *others):
    return lax.optimization_barrier((value, *others))[0]


def flipped(block, mask):
    return lax.ppermute(block, "blk", [(i, i ^ mask) for i in range(lax.axis_size("blk"))])


def next_plane(block):
    count = lax.axis_size("blk")
    return lax.ppermute(block, "blk", [(i, i + PLANE) for i in range(count - PLANE)])


def from_plane(block, ahead):
    count = lax.axis_size("blk")
    with jax.named_scope(f"from_plane_{ahead}"):
        return lax.ppermute(
            block, "blk", [((i + PLANE * ahead) % count, i) for i in range(count)]
        )


def to_plane(block, ahead):
    count = lax.axis_size("blk")
    with jax.named_scope(f"to_plane_{ahead}"):
        return lax.ppermute(
            block, "blk", [(i, (i + PLANE * ahead) % count) for i in range(count)]
        )


def from_core(block, ahead):
    count = lax.axis_size("tok")
    return lax.ppermute(block, "tok", [((i + ahead) % count, i) for i in range(count)])


def segment_starts(place_ref, lengths_ref, shape):
    token = place_ref[0] * shape[0] + lax.broadcasted_iota(jnp.int32, shape, 0)
    start = jnp.zeros(shape, jnp.int32)
    end = jnp.int32(0)
    for i in range(lengths_ref.shape[0]):
        end = end + lengths_ref[i]
        start = jnp.where(token >= end, end, start)
    return token, start


def rope_kernel(place_ref, lengths_ref, freq_ref, q_ref, k_ref, q_out, k_out):
    rows, width = q_ref.shape
    shape = (rows, HEAD_DIM)
    token, start = segment_starts(place_ref, lengths_ref, shape)
    angle = (token - start).astype(jnp.float32) * freq_ref[...]
    cosine, sine = jnp.cos(angle), jnp.sin(angle)
    lane = lax.broadcasted_iota(jnp.int32, shape, 1)
    sine = jnp.where(lane < HEAD_DIM // 2, -sine, sine)
    for source, target in ((k_ref, k_out), (q_ref, q_out)):
        for head in range(width // HEAD_DIM):
            columns = slice(head * HEAD_DIM, (head + 1) * HEAD_DIM)
            x = source[:, columns].astype(jnp.float32)
            turned = x * cosine + pltpu.roll(x, HEAD_DIM // 2, 1) * sine
            target[:, columns] = turned.astype(jnp.bfloat16)


def score_kernel(place_ref, lengths_ref, q_ref, *rest):
    *keys, out_ref = rest
    rows, width = q_ref.shape
    shape = (rows, rows)
    token, start = segment_starts(place_ref, lengths_ref, shape)
    blk = place_ref[0]
    column = lax.rem(blk, PLANE)
    bases = [blk, blk - PLANE]
    for mask in range(1, PLANE):
        other = column ^ mask
        bases.append(blk - column + other - jnp.where(other > column, PLANE, 0))
    lane = lax.broadcasted_iota(jnp.int32, shape, 1)
    ids = jnp.concatenate([base * rows + lane for base in bases], axis=1)
    token = jnp.concatenate([token] * len(keys), axis=1)
    start = jnp.concatenate([start] * len(keys), axis=1)
    allowed = (ids >= start) & (ids <= token)
    for head in range(width // HEAD_DIM):
        columns = slice(head * HEAD_DIM, (head + 1) * HEAD_DIM)
        key = jnp.concatenate([ref[:, columns] for ref in keys], axis=0)
        scores = lax.dot_general(
            q_ref[:, columns],
            key,
            (((1,), (1,)), ((), ())),
            preferred_element_type=jnp.float32,
        )
        scores = jnp.where(allowed, scores * HEAD_DIM ** (-0.5), -1e30)
        terms = jnp.exp(scores - jnp.max(scores, axis=1, keepdims=True))
        share = 1.0 / jnp.sum(terms, axis=1, keepdims=True)
        out_ref[head] = (terms * share).astype(jnp.bfloat16)


def mix_kernel(place_ref, prob_ref, weight_ref, residual_ref, *rest):
    *values, out_ref = rest
    heads = prob_ref.shape[0]
    mixed = []
    for head in range(heads):
        columns = slice(head * HEAD_DIM, (head + 1) * HEAD_DIM)
        value = jnp.concatenate([ref[:, columns] for ref in values], axis=0)
        product = jnp.dot(prob_ref[head], value, preferred_element_type=jnp.float32)
        mixed.append(product.astype(jnp.bfloat16))
    attention = jnp.concatenate(mixed, axis=1)
    out_ref[...] = jnp.dot(attention, weight_ref[...], preferred_element_type=jnp.float32)
    width = residual_ref.shape[1]
    own = pl.ds(pl.multiple_of(place_ref[1] * width, 128), width)
    out_ref[:, own] = out_ref[:, own] + residual_ref[...].astype(jnp.float32)


def norm_kernel(place_ref, gain_ref, lanes_ref, *rest):
    *addends, rows_out, share_out = rest
    rows, width = addends[0].shape
    part_rows = rows_out.shape[0]
    part_width = share_out.shape[1]
    own = pl.ds(pl.multiple_of(place_ref[1] * part_width, 128), part_width)
    share_out[...] = sum(ref[:, own] for ref in addends).astype(jnp.bfloat16)
    part = pl.ds(pl.multiple_of(place_ref[1] * part_rows, 16), part_rows)
    stream = sum(ref[part, :] for ref in addends).astype(jnp.bfloat16).astype(jnp.float32)
    scale = lax.rsqrt(jnp.mean(stream * stream, axis=1, keepdims=True) + EPSILON)
    rows_out[:, :width] = (stream * scale * gain_ref[...]).astype(jnp.bfloat16)
    rows_out[:, width:] = lanes_ref[part, :]


def local_call(body, out_shapes, scalars, arrays, flops=0, moved=0, limit=16):
    whole = pl.BlockSpec(memory_space=pltpu.VMEM)
    scalar = pl.BlockSpec(memory_space=pltpu.SMEM)
    moved = moved or sum(x.size * x.dtype.itemsize for x in (*arrays, *out_shapes))
    return pl.pallas_call(
        body,
        in_specs=[scalar] * len(scalars) + [whole] * len(arrays),
        out_specs=[whole] * len(out_shapes),
        out_shape=out_shapes,
        cost_estimate=pl.CostEstimate(flops=flops, bytes_accessed=moved, transcendentals=0),
        compiler_params=pltpu.CompilerParams(vmem_limit_bytes=limit << 20),
    )(*scalars, *arrays)


def gate_lanes(expert_ids, gate_weights, experts):
    hits = expert_ids[:, :, None] == jnp.arange(experts, dtype=jnp.int32)[None, None, :]
    gates = jnp.sum(jnp.where(hits, gate_weights[:, :, None], 0.0), axis=1)
    pieces = []
    for _ in range(3):
        piece = lax.reduce_precision(gates, 8, 7)
        pieces.append(piece.astype(jnp.bfloat16))
        gates = gates - piece
    lanes = jnp.concatenate(pieces, axis=1)
    return jnp.pad(lanes, ((0, 0), (0, -lanes.shape[1] % 128)))


def crossed(block, first, name="flip"):
    cores, count = lax.axis_size("tok"), lax.axis_size("blk")
    route = []
    for core in range(cores):
        mask = 1 if (core % 2 == 0) == first else 2
        route += [(core * count + i, core * count + (i ^ mask)) for i in range(count)]
    with jax.named_scope(name):
        return lax.ppermute(block, ("tok", "blk"), route)


def expert_kernel(experts, ahead, planes, plane, span, place_ref, near_ref, far_ref, gate_ref, up_ref, down_ref, *outs):
    width = gate_ref.shape[1]
    parts = len(outs)
    blocks, part_rows, part_width = outs[0].shape
    starts = [(i * planes + plane) * part_rows // span for i in range(2)]
    held = jnp.concatenate(
        [ref[start : start + part_rows] for ref in (near_ref, far_ref) for start in starts],
        axis=0,
    )
    rows = held[:, :width]
    lanes = held[:, width:].astype(jnp.float32)
    lane_ids = lax.broadcasted_iota(jnp.int32, lanes.shape, 1)
    named = (lane_ids < 3 * experts) & (lane_ids % experts == place_ref[0])
    weight = jnp.sum(jnp.where(named, lanes, 0.0), axis=1, keepdims=True)
    turned = (((1,), (1,)), ((), ()))
    gate_act = lax.dot_general(rows, gate_ref[...], turned, preferred_element_type=jnp.float32)
    up_act = lax.dot_general(rows, up_ref[...], turned, preferred_element_type=jnp.float32)
    hidden = (gate_act / (1.0 + jnp.exp(-gate_act)) * up_act).astype(jnp.bfloat16)
    for part in range(parts):
        start = lax.rem(place_ref[1] + part, parts) * part_width
        columns = pl.ds(pl.multiple_of(start, 128), part_width)
        product = jnp.dot(hidden, down_ref[:, columns], preferred_element_type=jnp.float32)
        product = (weight * product).astype(jnp.bfloat16)
        order = (0, 2, 1, 3) if (part - ahead) % 2 else (0, 1, 2, 3)
        for block in range(blocks):
            outs[part][order[block]] = product[block * part_rows : (block + 1) * part_rows]


def run_expert(place, near, far, w_gate, w_up, w_down, experts, parts, ahead, planes, plane, span):
    count = 2 * near.shape[0] // planes * span
    units, width = w_gate.shape
    out_shape = jax.ShapeDtypeStruct((PLANE, count // PLANE, width // parts), jnp.bfloat16)
    return local_call(
        functools.partial(expert_kernel, experts, ahead, planes, plane, span),
        [out_shape] * parts,
        [place],
        [near, far, w_gate, w_up, w_down],
        flops=6 * count * width * units,
    )


def wide(block):
    return block.astype(jnp.float32)


def narrow(block):
    return block.astype(jnp.bfloat16)


def second_share(totals):
    return narrow(jnp.stack([total[2:4] for total in totals]))


def first_share(totals):
    return narrow(jnp.stack([total[1] for total in totals]))


def merged(totals, got, count):
    return [total[0:count] + wide(got[i]) for i, total in enumerate(totals)]


def expert_outputs(place, rows, weights, experts, cores, planes, plane, span, waits):
    outs = []
    for ahead in range(cores):
        near, far = rows[ahead]
        near = after(near, *outs[-1:], *waits.get(ahead, []))
        outs.append(
            run_expert(
                place, near, far, *weights, experts, cores, ahead, planes, plane, span
            )
        )
    return outs


def core_totals(outs, cores, *waits):
    totals = []
    for rows_of in range(cores):
        total = wide(outs[rows_of][0])
        for ahead in range(1, cores):
            sent = outs[(rows_of + ahead) % cores][ahead]
            total = total + wide(after(from_core(sent, cores - ahead), *waits))
        totals.append(total)
    return totals


def on_device(
    q_proj,
    k_proj,
    v_proj,
    residual,
    prompt_lengths,
    expert_ids,
    gate_weights,
    page_table,
    out_weight,
    norm_gain,
    w_gate,
    w_up,
    w_down,
):
    tok_rows = q_proj.shape[0]
    col_width = residual.shape[1]
    model_width = norm_gain.shape[0]
    blk_index = lax.axis_index("blk")
    tok_index = lax.axis_index("tok")
    cores = lax.axis_size("tok")
    experts = lax.axis_size("blk")
    planes = experts // PLANE
    place = jnp.stack([blk_index, tok_index]).astype(jnp.int32)
    part_rows = tok_rows // cores
    half_dim = HEAD_DIM // 2
    inv_freq = 10000.0 ** (-jnp.arange(half_dim, dtype=jnp.float32) / half_dim)
    freq = jnp.concatenate([inv_freq, inv_freq])[None, :]
    rotated = jax.ShapeDtypeStruct(q_proj.shape, jnp.bfloat16)
    rot_query, rot_keys = local_call(
        rope_kernel, [rotated] * 2, [place, prompt_lengths], [freq, q_proj, k_proj]
    )
    column = blk_index % PLANE
    key_blocks, value_blocks = [
        [block, next_plane(block)] for block in (rot_keys, after(v_proj, rot_keys))
    ]
    for blocks in (key_blocks, value_blocks):
        own, below = blocks
        for mask in range(1, PLANE):
            blocks.append(flipped(jnp.where(column < column ^ mask, own, below), mask))
    heads = q_proj.shape[1] // HEAD_DIM
    probs_shape = (heads, tok_rows, len(key_blocks) * tok_rows)
    probs = local_call(
        score_kernel,
        [jax.ShapeDtypeStruct(probs_shape, jnp.bfloat16)],
        [place, prompt_lengths],
        [rot_query, *key_blocks],
        flops=2 * tok_rows * probs_shape[2] * heads * HEAD_DIM,
    )[0]
    page_count = tok_rows // PAGE
    local_page = page_table - blk_index * page_count
    kv_rows = jnp.stack([rot_keys, v_proj], axis=1).reshape(page_count, PAGE, 2, -1)
    kv_pages = jnp.zeros_like(kv_rows).at[local_page].set(kv_rows)
    lanes = gate_lanes(expert_ids, gate_weights, experts)
    probs = after(probs, kv_pages, lanes)
    mixed = local_call(
        mix_kernel,
        [jax.ShapeDtypeStruct((tok_rows, model_width), jnp.float32)],
        [place],
        [probs, out_weight, residual, *value_blocks],
        flops=2 * tok_rows * (probs_shape[2] + model_width) * heads * HEAD_DIM,
    )[0]
    if cores == 2:
        addends = [mixed, from_core(mixed, 1)]
    else:
        addends = [lax.psum(mixed, "tok")]
    payload, own_share = local_call(
        norm_kernel,
        [
            jax.ShapeDtypeStruct((part_rows, model_width + lanes.shape[1]), jnp.bfloat16),
            jax.ShapeDtypeStruct((tok_rows, col_width), jnp.bfloat16),
        ],
        [place],
        [norm_gain[None, :], lanes, *addends],
    )
    if planes <= 4:
        groups = [[0]] + [sorted({i, planes - i}) for i in range(1, planes // 2 + 1)]
    else:
        groups = [[0]] + [list(range(i, min(i + 8, planes))) for i in range(1, planes, 8)]
    weights = (w_gate[0].T, w_up[0].T, w_down[0])
    run = functools.partial(
        expert_outputs, place, weights=weights, experts=experts, cores=cores
    )
    columns, nears, fars, rows = [], [], [], []
    sent = payload
    for group in groups:
        columns.append(
            jnp.concatenate([from_plane(sent, ahead) if ahead else sent for ahead in group])
        )
        sent = after(payload, columns[-1])
    for number, column in enumerate(columns):
        if number > 0:
            column = after(column, nears[-1])
        if number == 2:
            outs = run(rows=rows[0], planes=1, plane=0, span=1, waits={})
            column = after(column, outs)
        nears.append(
            jnp.concatenate([column, crossed(column, True, f"gather_first_{number}")])
        )
        ready = after(nears[-1], fars[0], columns[2]) if number == 1 else nears[-1]
        fars.append(crossed(ready, False, f"gather_second_{number}"))
        rows.append(
            [
                (from_core(nears[-1], i), from_core(fars[-1], i)) if i else (nears[-1], fars[-1])
                for i in range(cores)
            ]
        )
    own_totals = core_totals(outs, cores)
    sent = after(second_share(own_totals), nears[-1])
    own_second = crossed(sent, False, "scatter_second_0")
    own_totals = merged(own_totals, own_second, 2)
    own_got = crossed(first_share(own_totals), True, "scatter_first_0")
    seconds, firsts, returned = [], [], []
    span_of = 1 if planes <= 4 else 8
    steps = [
        (number, plane, group[plane : plane + span_of])
        for number, group in enumerate(groups)
        for plane in range(0, len(group), span_of)
    ]
    for number, plane, aheads in steps[1:]:
        waits = {0: [outs], cores - 1: [*seconds[-1:]]}
        if len(seconds) == 2:
            waits[0].append(own_second)
        outs = run(
            rows=rows[number],
            planes=len(groups[number]),
            plane=plane,
            span=len(aheads),
            waits=waits,
        )
        totals = core_totals(outs, cores, *firsts[-1:])
        seconds.append(second_share(totals))
        got = crossed(seconds[-1], False, f"scatter_second_{aheads[0]}")
        totals = merged(totals, got, 2)
        firsts.append(first_share(totals))
        got = crossed(firsts[-1], True, f"scatter_first_{aheads[0]}")
        rows_of = merged([total[0] for total in totals], got, None)
        for i, ahead in enumerate(aheads):
            piece = [part[i * part_rows : (i + 1) * part_rows] for part in rows_of]
            returned.append(to_plane(narrow(jnp.concatenate(piece)), ahead))
    moe = jnp.concatenate(merged([total[0] for total in own_totals], own_got, None))
    moe = moe + sum(wide(block) for block in returned)
    moe = jnp.roll(moe.reshape(cores, part_rows, col_width), tok_index, axis=0)
    moe = moe.reshape(tok_rows, col_width)
    layer_out = (own_share.astype(jnp.float32) + moe).astype(jnp.bfloat16)
    return (layer_out, kv_pages)


def solution(mesh):
    placed = (
        P("blk", "tok"),
        P("blk", "tok"),
        P("blk", "tok"),
        P("blk", "tok"),
        P(),
        P("blk", None),
        P("blk", None),
        P("blk"),
        P("tok", None),
        P(),
        P("blk", None, "tok"),
        P("blk", None, "tok"),
        P("blk", "tok", None),
    )
    return jax.shard_map(
        on_device,
        mesh=mesh,
        in_specs=placed,
        out_specs=(P("blk", "tok"), P("blk", None, None, "tok")),
        check_vma=False,
    )
```

```python
import functools

import jax
import jax.numpy as jnp
from jax import lax
from jax.experimental import pallas as pl
from jax.experimental.pallas import tpu as pltpu
from jax.sharding import PartitionSpec as P

HEAD_DIM = 128
REACH = 4
PAGE = 16
PLANE = 4
EPSILON = 1e-06


def after(value, *others):
    return lax.optimization_barrier((value, *others))[0]


def flipped(block, mask):
    return lax.ppermute(block, "blk", [(i, i ^ mask) for i in range(lax.axis_size("blk"))])


def next_plane(block):
    count = lax.axis_size("blk")
    return lax.ppermute(block, "blk", [(i, i + PLANE) for i in range(count - PLANE)])


def from_plane(block, ahead):
    count = lax.axis_size("blk")
    with jax.named_scope(f"from_plane_{ahead}"):
        return lax.ppermute(
            block, "blk", [((i + PLANE * ahead) % count, i) for i in range(count)]
        )


def to_plane(block, ahead):
    count = lax.axis_size("blk")
    with jax.named_scope(f"to_plane_{ahead}"):
        return lax.ppermute(
            block, "blk", [(i, (i + PLANE * ahead) % count) for i in range(count)]
        )


def from_core(block, ahead):
    count = lax.axis_size("tok")
    return lax.ppermute(block, "tok", [((i + ahead) % count, i) for i in range(count)])


def segment_starts(place_ref, lengths_ref, shape):
    token = place_ref[0] * shape[0] + lax.broadcasted_iota(jnp.int32, shape, 0)
    start = jnp.zeros(shape, jnp.int32)
    end = jnp.int32(0)
    for i in range(lengths_ref.shape[0]):
        end = end + lengths_ref[i]
        start = jnp.where(token >= end, end, start)
    return token, start


def rope_kernel(place_ref, lengths_ref, freq_ref, q_ref, k_ref, q_out, k_out):
    rows, width = q_ref.shape
    shape = (rows, HEAD_DIM)
    token, start = segment_starts(place_ref, lengths_ref, shape)
    angle = (token - start).astype(jnp.float32) * freq_ref[...]
    cosine, sine = jnp.cos(angle), jnp.sin(angle)
    lane = lax.broadcasted_iota(jnp.int32, shape, 1)
    sine = jnp.where(lane < HEAD_DIM // 2, -sine, sine)
    for source, target in ((k_ref, k_out), (q_ref, q_out)):
        for head in range(width // HEAD_DIM):
            columns = slice(head * HEAD_DIM, (head + 1) * HEAD_DIM)
            x = source[:, columns].astype(jnp.float32)
            turned = x * cosine + pltpu.roll(x, HEAD_DIM // 2, 1) * sine
            target[:, columns] = turned.astype(jnp.bfloat16)


def score_kernel(place_ref, lengths_ref, q_ref, *rest):
    *keys, out_ref = rest
    rows, width = q_ref.shape
    shape = (rows, rows)
    token, start = segment_starts(place_ref, lengths_ref, shape)
    blk = place_ref[0]
    column = lax.rem(blk, PLANE)
    bases = [blk, blk - PLANE]
    for mask in range(1, PLANE):
        other = column ^ mask
        bases.append(blk - column + other - jnp.where(other > column, PLANE, 0))
    lane = lax.broadcasted_iota(jnp.int32, shape, 1)
    ids = jnp.concatenate([base * rows + lane for base in bases], axis=1)
    token = jnp.concatenate([token] * len(keys), axis=1)
    start = jnp.concatenate([start] * len(keys), axis=1)
    allowed = (ids >= start) & (ids <= token)
    for head in range(width // HEAD_DIM):
        columns = slice(head * HEAD_DIM, (head + 1) * HEAD_DIM)
        key = jnp.concatenate([ref[:, columns] for ref in keys], axis=0)
        scores = lax.dot_general(
            q_ref[:, columns],
            key,
            (((1,), (1,)), ((), ())),
            preferred_element_type=jnp.float32,
        )
        scores = jnp.where(allowed, scores * HEAD_DIM ** (-0.5), -1e30)
        terms = jnp.exp(scores - jnp.max(scores, axis=1, keepdims=True))
        share = 1.0 / jnp.sum(terms, axis=1, keepdims=True)
        out_ref[head] = (terms * share).astype(jnp.bfloat16)


def mix_kernel(place_ref, prob_ref, weight_ref, residual_ref, *rest):
    *values, out_ref = rest
    heads = prob_ref.shape[0]
    mixed = []
    for head in range(heads):
        columns = slice(head * HEAD_DIM, (head + 1) * HEAD_DIM)
        value = jnp.concatenate([ref[:, columns] for ref in values], axis=0)
        product = jnp.dot(prob_ref[head], value, preferred_element_type=jnp.float32)
        mixed.append(product.astype(jnp.bfloat16))
    attention = jnp.concatenate(mixed, axis=1)
    out_ref[...] = jnp.dot(attention, weight_ref[...], preferred_element_type=jnp.float32)
    width = residual_ref.shape[1]
    own = pl.ds(pl.multiple_of(place_ref[1] * width, 128), width)
    out_ref[:, own] = out_ref[:, own] + residual_ref[...].astype(jnp.float32)


def norm_kernel(place_ref, gain_ref, lanes_ref, *rest):
    *addends, rows_out, share_out = rest
    rows, width = addends[0].shape
    part_rows = rows_out.shape[0]
    part_width = share_out.shape[1]
    own = pl.ds(pl.multiple_of(place_ref[1] * part_width, 128), part_width)
    share_out[...] = sum(ref[:, own] for ref in addends).astype(jnp.bfloat16)
    part = pl.ds(pl.multiple_of(place_ref[1] * part_rows, 16), part_rows)
    stream = sum(ref[part, :] for ref in addends).astype(jnp.bfloat16).astype(jnp.float32)
    scale = lax.rsqrt(jnp.mean(stream * stream, axis=1, keepdims=True) + EPSILON)
    rows_out[:, :width] = (stream * scale * gain_ref[...]).astype(jnp.bfloat16)
    rows_out[:, width:] = lanes_ref[part, :]


def local_call(body, out_shapes, scalars, arrays, flops=0, moved=0, limit=16):
    whole = pl.BlockSpec(memory_space=pltpu.VMEM)
    scalar = pl.BlockSpec(memory_space=pltpu.SMEM)
    moved = moved or sum(x.size * x.dtype.itemsize for x in (*arrays, *out_shapes))
    return pl.pallas_call(
        body,
        in_specs=[scalar] * len(scalars) + [whole] * len(arrays),
        out_specs=[whole] * len(out_shapes),
        out_shape=out_shapes,
        cost_estimate=pl.CostEstimate(flops=flops, bytes_accessed=moved, transcendentals=0),
        compiler_params=pltpu.CompilerParams(vmem_limit_bytes=limit << 20),
    )(*scalars, *arrays)


def gate_lanes(expert_ids, gate_weights, experts):
    hits = expert_ids[:, :, None] == jnp.arange(experts, dtype=jnp.int32)[None, None, :]
    gates = jnp.sum(jnp.where(hits, gate_weights[:, :, None], 0.0), axis=1)
    pieces = []
    for _ in range(3):
        piece = lax.reduce_precision(gates, 8, 7)
        pieces.append(piece.astype(jnp.bfloat16))
        gates = gates - piece
    lanes = jnp.concatenate(pieces, axis=1)
    return jnp.pad(lanes, ((0, 0), (0, -lanes.shape[1] % 128)))


def crossed(block, first, name="flip"):
    cores, count = lax.axis_size("tok"), lax.axis_size("blk")
    route = []
    for core in range(cores):
        mask = 1 if (core % 2 == 0) == first else 2
        route += [(core * count + i, core * count + (i ^ mask)) for i in range(count)]
    with jax.named_scope(name):
        return lax.ppermute(block, ("tok", "blk"), route)


def expert_kernel(experts, ahead, planes, plane, span, place_ref, near_ref, far_ref, gate_ref, up_ref, down_ref, *outs):
    width = gate_ref.shape[1]
    parts = len(outs)
    blocks, part_rows, part_width = outs[0].shape
    starts = [(i * planes + plane) * part_rows // span for i in range(2)]
    held = jnp.concatenate(
        [ref[start : start + part_rows] for ref in (near_ref, far_ref) for start in starts],
        axis=0,
    )
    rows = held[:, :width]
    lanes = held[:, width:].astype(jnp.float32)
    lane_ids = lax.broadcasted_iota(jnp.int32, lanes.shape, 1)
    named = (lane_ids < 3 * experts) & (lane_ids % experts == place_ref[0])
    weight = jnp.sum(jnp.where(named, lanes, 0.0), axis=1, keepdims=True)
    turned = (((1,), (1,)), ((), ()))
    gate_act = lax.dot_general(rows, gate_ref[...], turned, preferred_element_type=jnp.float32)
    up_act = lax.dot_general(rows, up_ref[...], turned, preferred_element_type=jnp.float32)
    hidden = (gate_act / (1.0 + jnp.exp(-gate_act)) * up_act).astype(jnp.bfloat16)
    for part in range(parts):
        start = lax.rem(place_ref[1] + part, parts) * part_width
        columns = pl.ds(pl.multiple_of(start, 128), part_width)
        product = jnp.dot(hidden, down_ref[:, columns], preferred_element_type=jnp.float32)
        product = (weight * product).astype(jnp.bfloat16)
        order = (0, 2, 1, 3) if (part - ahead) % 2 else (0, 1, 2, 3)
        for block in range(blocks):
            outs[part][order[block]] = product[block * part_rows : (block + 1) * part_rows]


def run_expert(place, near, far, w_gate, w_up, w_down, experts, parts, ahead, planes, plane, span):
    count = 2 * near.shape[0] // planes * span
    units, width = w_gate.shape
    out_shape = jax.ShapeDtypeStruct((PLANE, count // PLANE, width // parts), jnp.bfloat16)
    return local_call(
        functools.partial(expert_kernel, experts, ahead, planes, plane, span),
        [out_shape] * parts,
        [place],
        [near, far, w_gate, w_up, w_down],
        flops=6 * count * width * units,
    )


def wide(block):
    return block.astype(jnp.float32)


def narrow(block):
    return block.astype(jnp.bfloat16)


def second_share(totals):
    return narrow(jnp.stack([total[2:4] for total in totals]))


def first_share(totals):
    return narrow(jnp.stack([total[1] for total in totals]))


def merged(totals, got, count):
    return [total[0:count] + wide(got[i]) for i, total in enumerate(totals)]


def expert_outputs(place, rows, weights, experts, cores, planes, plane, span, waits):
    outs = []
    for ahead in range(cores):
        near, far = rows[ahead]
        near = after(near, *outs[-1:], *waits.get(ahead, []))
        outs.append(
            run_expert(
                place, near, far, *weights, experts, cores, ahead, planes, plane, span
            )
        )
    return outs


def core_totals(outs, cores, *waits):
    totals = []
    for rows_of in range(cores):
        total = wide(outs[rows_of][0])
        for ahead in range(1, cores):
            sent = outs[(rows_of + ahead) % cores][ahead]
            total = total + wide(after(from_core(sent, cores - ahead), *waits))
        totals.append(total)
    return totals


def on_device(
    q_proj,
    k_proj,
    v_proj,
    residual,
    prompt_lengths,
    expert_ids,
    gate_weights,
    page_table,
    out_weight,
    norm_gain,
    w_gate,
    w_up,
    w_down,
):
    tok_rows = q_proj.shape[0]
    col_width = residual.shape[1]
    model_width = norm_gain.shape[0]
    blk_index = lax.axis_index("blk")
    tok_index = lax.axis_index("tok")
    cores = lax.axis_size("tok")
    experts = lax.axis_size("blk")
    planes = experts // PLANE
    place = jnp.stack([blk_index, tok_index]).astype(jnp.int32)
    part_rows = tok_rows // cores
    half_dim = HEAD_DIM // 2
    inv_freq = 10000.0 ** (-jnp.arange(half_dim, dtype=jnp.float32) / half_dim)
    freq = jnp.concatenate([inv_freq, inv_freq])[None, :]
    rotated = jax.ShapeDtypeStruct(q_proj.shape, jnp.bfloat16)
    rot_query, rot_keys = local_call(
        rope_kernel, [rotated] * 2, [place, prompt_lengths], [freq, q_proj, k_proj]
    )
    column = blk_index % PLANE
    key_blocks, value_blocks = [
        [block, next_plane(block)] for block in (rot_keys, after(v_proj, rot_keys))
    ]
    for blocks in (key_blocks, value_blocks):
        own, below = blocks
        for mask in range(1, PLANE):
            blocks.append(flipped(jnp.where(column < column ^ mask, own, below), mask))
    heads = q_proj.shape[1] // HEAD_DIM
    probs_shape = (heads, tok_rows, len(key_blocks) * tok_rows)
    probs = local_call(
        score_kernel,
        [jax.ShapeDtypeStruct(probs_shape, jnp.bfloat16)],
        [place, prompt_lengths],
        [rot_query, *key_blocks],
        flops=2 * tok_rows * probs_shape[2] * heads * HEAD_DIM,
    )[0]
    page_count = tok_rows // PAGE
    local_page = page_table - blk_index * page_count
    kv_rows = jnp.stack([rot_keys, v_proj], axis=1).reshape(page_count, PAGE, 2, -1)
    kv_pages = jnp.zeros_like(kv_rows).at[local_page].set(kv_rows)
    lanes = gate_lanes(expert_ids, gate_weights, experts)
    probs = after(probs, kv_pages, lanes)
    mixed = local_call(
        mix_kernel,
        [jax.ShapeDtypeStruct((tok_rows, model_width), jnp.float32)],
        [place],
        [probs, out_weight, residual, *value_blocks],
        flops=2 * tok_rows * (probs_shape[2] + model_width) * heads * HEAD_DIM,
    )[0]
    if cores == 2:
        addends = [mixed, from_core(mixed, 1)]
    else:
        addends = [lax.psum(mixed, "tok")]
    payload, own_share = local_call(
        norm_kernel,
        [
            jax.ShapeDtypeStruct((part_rows, model_width + lanes.shape[1]), jnp.bfloat16),
            jax.ShapeDtypeStruct((tok_rows, col_width), jnp.bfloat16),
        ],
        [place],
        [norm_gain[None, :], lanes, *addends],
    )
    if planes <= 4:
        groups = [[0]] + [sorted({i, planes - i}) for i in range(1, planes // 2 + 1)]
    else:
        groups = [[0]] + [list(range(i, min(i + 8, planes))) for i in range(1, planes, 8)]
    weights = (w_gate[0].T, w_up[0].T, w_down[0])
    run = functools.partial(
        expert_outputs, place, weights=weights, experts=experts, cores=cores
    )
    columns, nears, fars, rows = [], [], [], []
    sent = payload
    for group in groups:
        columns.append(
            jnp.concatenate([from_plane(sent, ahead) if ahead else sent for ahead in group])
        )
        sent = after(payload, columns[-1])
    for number, column in enumerate(columns):
        if number > 0:
            column = after(column, nears[-1], fars[0])
        if number == 2:
            outs = run(rows=rows[0], planes=1, plane=0, span=1, waits={})
            column = after(column, outs)
        nears.append(
            jnp.concatenate([column, crossed(column, True, f"gather_first_{number}")])
        )
        ready = after(nears[-1], columns[2]) if number == 1 else nears[-1]
        fars.append(crossed(ready, False, f"gather_second_{number}"))
        rows.append(
            [
                (from_core(nears[-1], i), from_core(fars[-1], i)) if i else (nears[-1], fars[-1])
                for i in range(cores)
            ]
        )
    own_totals = core_totals(outs, cores)
    sent = after(second_share(own_totals), nears[-1])
    own_second = crossed(sent, False, "scatter_second_0")
    own_totals = merged(own_totals, own_second, 2)
    seconds, firsts, flips, returned = [], [], [], []
    span_of = 1 if planes <= 4 else 8
    steps = [
        (number, plane, group[plane : plane + span_of])
        for number, group in enumerate(groups)
        for plane in range(0, len(group), span_of)
    ]
    for number, plane, aheads in steps[1:]:
        waits = {0: [outs], cores - 1: [*seconds[-1:]]}
        if len(seconds) > 1:
            waits[0].append(own_second)
        outs = run(
            rows=rows[number],
            planes=len(groups[number]),
            plane=plane,
            span=len(aheads),
            waits=waits,
        )
        totals = core_totals(outs, cores, *firsts[-1:], *flips[-2:-1])
        seconds.append(second_share(totals))
        got = crossed(seconds[-1], False, f"scatter_second_{aheads[0]}")
        totals = merged(totals, got, 2)
        firsts.append(first_share(totals))
        got = crossed(firsts[-1], True, f"scatter_first_{aheads[0]}")
        rows_of = merged([total[0] for total in totals], got, None)
        blocks = []
        for i, ahead in enumerate(aheads):
            piece = [part[i * part_rows : (i + 1) * part_rows] for part in rows_of]
            blocks.append(narrow(jnp.concatenate(piece)))
            returned.append(to_plane(blocks[-1], ahead))
        flips.append(blocks)
    own_first = after(first_share(own_totals), *flips[-2:-1])
    own_got = crossed(own_first, True, "scatter_first_0")
    moe = jnp.concatenate(merged([total[0] for total in own_totals], own_got, None))
    moe = moe + sum(wide(block) for block in returned)
    moe = jnp.roll(moe.reshape(cores, part_rows, col_width), tok_index, axis=0)
    moe = moe.reshape(tok_rows, col_width)
    layer_out = (own_share.astype(jnp.float32) + moe).astype(jnp.bfloat16)
    return (layer_out, kv_pages)


def solution(mesh):
    placed = (
        P("blk", "tok"),
        P("blk", "tok"),
        P("blk", "tok"),
        P("blk", "tok"),
        P(),
        P("blk", None),
        P("blk", None),
        P("blk"),
        P("tok", None),
        P(),
        P("blk", None, "tok"),
        P("blk", None, "tok"),
        P("blk", "tok", None),
    )
    return jax.shard_map(
        on_device,
        mesh=mesh,
        in_specs=placed,
        out_specs=(P("blk", "tok"), P("blk", None, None, "tok")),
        check_vma=False,
    )
```

```python
import functools

import jax
import jax.numpy as jnp
from jax import lax
from jax.experimental import pallas as pl
from jax.experimental.pallas import tpu as pltpu
from jax.sharding import PartitionSpec as P

HEAD_DIM = 128
REACH = 4
PAGE = 16
PLANE = 4
EPSILON = 1e-06


def after(value, *others):
    return lax.optimization_barrier((value, *others))[0]


def flipped(block, mask):
    return lax.ppermute(block, "blk", [(i, i ^ mask) for i in range(lax.axis_size("blk"))])


def next_plane(block):
    count = lax.axis_size("blk")
    return lax.ppermute(block, "blk", [(i, i + PLANE) for i in range(count - PLANE)])


def from_plane(block, ahead):
    count = lax.axis_size("blk")
    with jax.named_scope(f"from_plane_{ahead}"):
        return lax.ppermute(
            block, "blk", [((i + PLANE * ahead) % count, i) for i in range(count)]
        )


def to_plane(block, ahead):
    count = lax.axis_size("blk")
    with jax.named_scope(f"to_plane_{ahead}"):
        return lax.ppermute(
            block, "blk", [(i, (i + PLANE * ahead) % count) for i in range(count)]
        )


def from_core(block, ahead):
    count = lax.axis_size("tok")
    return lax.ppermute(block, "tok", [((i + ahead) % count, i) for i in range(count)])


def segment_starts(place_ref, lengths_ref, shape):
    token = place_ref[0] * shape[0] + lax.broadcasted_iota(jnp.int32, shape, 0)
    start = jnp.zeros(shape, jnp.int32)
    end = jnp.int32(0)
    for i in range(lengths_ref.shape[0]):
        end = end + lengths_ref[i]
        start = jnp.where(token >= end, end, start)
    return token, start


def rope_kernel(place_ref, lengths_ref, freq_ref, q_ref, k_ref, q_out, k_out):
    rows, width = q_ref.shape
    shape = (rows, HEAD_DIM)
    token, start = segment_starts(place_ref, lengths_ref, shape)
    angle = (token - start).astype(jnp.float32) * freq_ref[...]
    cosine, sine = jnp.cos(angle), jnp.sin(angle)
    lane = lax.broadcasted_iota(jnp.int32, shape, 1)
    sine = jnp.where(lane < HEAD_DIM // 2, -sine, sine)
    for source, target in ((k_ref, k_out), (q_ref, q_out)):
        for head in range(width // HEAD_DIM):
            columns = slice(head * HEAD_DIM, (head + 1) * HEAD_DIM)
            x = source[:, columns].astype(jnp.float32)
            turned = x * cosine + pltpu.roll(x, HEAD_DIM // 2, 1) * sine
            target[:, columns] = turned.astype(jnp.bfloat16)


def score_kernel(place_ref, lengths_ref, q_ref, *rest):
    *keys, out_ref = rest
    rows, width = q_ref.shape
    shape = (rows, rows)
    token, start = segment_starts(place_ref, lengths_ref, shape)
    blk = place_ref[0]
    column = lax.rem(blk, PLANE)
    bases = [blk, blk - PLANE]
    for mask in range(1, PLANE):
        other = column ^ mask
        bases.append(blk - column + other - jnp.where(other > column, PLANE, 0))
    lane = lax.broadcasted_iota(jnp.int32, shape, 1)
    ids = jnp.concatenate([base * rows + lane for base in bases], axis=1)
    token = jnp.concatenate([token] * len(keys), axis=1)
    start = jnp.concatenate([start] * len(keys), axis=1)
    allowed = (ids >= start) & (ids <= token)
    for head in range(width // HEAD_DIM):
        columns = slice(head * HEAD_DIM, (head + 1) * HEAD_DIM)
        key = jnp.concatenate([ref[:, columns] for ref in keys], axis=0)
        scores = lax.dot_general(
            q_ref[:, columns],
            key,
            (((1,), (1,)), ((), ())),
            preferred_element_type=jnp.float32,
        )
        scores = jnp.where(allowed, scores * HEAD_DIM ** (-0.5), -1e30)
        terms = jnp.exp(scores - jnp.max(scores, axis=1, keepdims=True))
        share = 1.0 / jnp.sum(terms, axis=1, keepdims=True)
        out_ref[head] = (terms * share).astype(jnp.bfloat16)


def mix_kernel(place_ref, prob_ref, weight_ref, residual_ref, *rest):
    *values, out_ref = rest
    heads = prob_ref.shape[0]
    mixed = []
    for head in range(heads):
        columns = slice(head * HEAD_DIM, (head + 1) * HEAD_DIM)
        value = jnp.concatenate([ref[:, columns] for ref in values], axis=0)
        product = jnp.dot(prob_ref[head], value, preferred_element_type=jnp.float32)
        mixed.append(product.astype(jnp.bfloat16))
    attention = jnp.concatenate(mixed, axis=1)
    out_ref[...] = jnp.dot(attention, weight_ref[...], preferred_element_type=jnp.float32)
    width = residual_ref.shape[1]
    own = pl.ds(pl.multiple_of(place_ref[1] * width, 128), width)
    out_ref[:, own] = out_ref[:, own] + residual_ref[...].astype(jnp.float32)


def norm_kernel(place_ref, gain_ref, lanes_ref, *rest):
    *addends, rows_out, share_out = rest
    rows, width = addends[0].shape
    part_rows = rows_out.shape[0]
    part_width = share_out.shape[1]
    own = pl.ds(pl.multiple_of(place_ref[1] * part_width, 128), part_width)
    share_out[...] = sum(ref[:, own] for ref in addends).astype(jnp.bfloat16)
    part = pl.ds(pl.multiple_of(place_ref[1] * part_rows, 16), part_rows)
    stream = sum(ref[part, :] for ref in addends).astype(jnp.bfloat16).astype(jnp.float32)
    scale = lax.rsqrt(jnp.mean(stream * stream, axis=1, keepdims=True) + EPSILON)
    rows_out[:, :width] = (stream * scale * gain_ref[...]).astype(jnp.bfloat16)
    rows_out[:, width:] = lanes_ref[part, :]


def local_call(body, out_shapes, scalars, arrays, flops=0, moved=0, limit=16):
    whole = pl.BlockSpec(memory_space=pltpu.VMEM)
    scalar = pl.BlockSpec(memory_space=pltpu.SMEM)
    moved = moved or sum(x.size * x.dtype.itemsize for x in (*arrays, *out_shapes))
    return pl.pallas_call(
        body,
        in_specs=[scalar] * len(scalars) + [whole] * len(arrays),
        out_specs=[whole] * len(out_shapes),
        out_shape=out_shapes,
        cost_estimate=pl.CostEstimate(flops=flops, bytes_accessed=moved, transcendentals=0),
        compiler_params=pltpu.CompilerParams(vmem_limit_bytes=limit << 20),
    )(*scalars, *arrays)


def gate_lanes(expert_ids, gate_weights, experts):
    hits = expert_ids[:, :, None] == jnp.arange(experts, dtype=jnp.int32)[None, None, :]
    gates = jnp.sum(jnp.where(hits, gate_weights[:, :, None], 0.0), axis=1)
    pieces = []
    for _ in range(3):
        piece = lax.reduce_precision(gates, 8, 7)
        pieces.append(piece.astype(jnp.bfloat16))
        gates = gates - piece
    lanes = jnp.concatenate(pieces, axis=1)
    return jnp.pad(lanes, ((0, 0), (0, -lanes.shape[1] % 128)))


def crossed(block, first, name="flip"):
    cores, count = lax.axis_size("tok"), lax.axis_size("blk")
    route = []
    for core in range(cores):
        mask = 1 if (core % 2 == 0) == first else 2
        route += [(core * count + i, core * count + (i ^ mask)) for i in range(count)]
    with jax.named_scope(name):
        return lax.ppermute(block, ("tok", "blk"), route)


def expert_kernel(experts, ahead, planes, plane, span, place_ref, near_ref, far_ref, gate_ref, up_ref, down_ref, *outs):
    width = gate_ref.shape[1]
    parts = len(outs)
    blocks, part_rows, part_width = outs[0].shape
    starts = [(i * planes + plane) * part_rows // span for i in range(2)]
    held = jnp.concatenate(
        [ref[start : start + part_rows] for ref in (near_ref, far_ref) for start in starts],
        axis=0,
    )
    rows = held[:, :width]
    lanes = held[:, width:].astype(jnp.float32)
    lane_ids = lax.broadcasted_iota(jnp.int32, lanes.shape, 1)
    named = (lane_ids < 3 * experts) & (lane_ids % experts == place_ref[0])
    weight = jnp.sum(jnp.where(named, lanes, 0.0), axis=1, keepdims=True)
    turned = (((1,), (1,)), ((), ()))
    gate_act = lax.dot_general(rows, gate_ref[...], turned, preferred_element_type=jnp.float32)
    up_act = lax.dot_general(rows, up_ref[...], turned, preferred_element_type=jnp.float32)
    hidden = (gate_act / (1.0 + jnp.exp(-gate_act)) * up_act).astype(jnp.bfloat16)
    for part in range(parts):
        start = lax.rem(place_ref[1] + part, parts) * part_width
        columns = pl.ds(pl.multiple_of(start, 128), part_width)
        product = jnp.dot(hidden, down_ref[:, columns], preferred_element_type=jnp.float32)
        product = (weight * product).astype(jnp.bfloat16)
        order = (0, 2, 1, 3) if (part - ahead) % 2 else (0, 1, 2, 3)
        for block in range(blocks):
            outs[part][order[block]] = product[block * part_rows : (block + 1) * part_rows]


def run_expert(place, near, far, w_gate, w_up, w_down, experts, parts, ahead, planes, plane, span):
    count = 2 * near.shape[0] // planes * span
    units, width = w_gate.shape
    out_shape = jax.ShapeDtypeStruct((PLANE, count // PLANE, width // parts), jnp.bfloat16)
    return local_call(
        functools.partial(expert_kernel, experts, ahead, planes, plane, span),
        [out_shape] * parts,
        [place],
        [near, far, w_gate, w_up, w_down],
        flops=6 * count * width * units,
    )


def wide(block):
    return block.astype(jnp.float32)


def narrow(block):
    return block.astype(jnp.bfloat16)


def second_share(totals):
    return narrow(jnp.stack([total[2:4] for total in totals]))


def first_share(totals):
    return narrow(jnp.stack([total[1] for total in totals]))


def merged(totals, got, count):
    return [total[0:count] + wide(got[i]) for i, total in enumerate(totals)]


def expert_outputs(place, rows, weights, experts, cores, planes, plane, span, waits):
    outs = []
    for ahead in range(cores):
        near, far = rows[ahead]
        near = after(near, *outs[-1:], *waits.get(ahead, []))
        outs.append(
            run_expert(
                place, near, far, *weights, experts, cores, ahead, planes, plane, span
            )
        )
    return outs


def core_totals(outs, cores, *waits):
    totals = []
    for rows_of in range(cores):
        total = wide(outs[rows_of][0])
        for ahead in range(1, cores):
            sent = outs[(rows_of + ahead) % cores][ahead]
            total = total + wide(after(from_core(sent, cores - ahead), *waits))
        totals.append(total)
    return totals


def on_device(
    q_proj,
    k_proj,
    v_proj,
    residual,
    prompt_lengths,
    expert_ids,
    gate_weights,
    page_table,
    out_weight,
    norm_gain,
    w_gate,
    w_up,
    w_down,
):
    tok_rows = q_proj.shape[0]
    col_width = residual.shape[1]
    model_width = norm_gain.shape[0]
    blk_index = lax.axis_index("blk")
    tok_index = lax.axis_index("tok")
    cores = lax.axis_size("tok")
    experts = lax.axis_size("blk")
    planes = experts // PLANE
    place = jnp.stack([blk_index, tok_index]).astype(jnp.int32)
    part_rows = tok_rows // cores
    half_dim = HEAD_DIM // 2
    inv_freq = 10000.0 ** (-jnp.arange(half_dim, dtype=jnp.float32) / half_dim)
    freq = jnp.concatenate([inv_freq, inv_freq])[None, :]
    rotated = jax.ShapeDtypeStruct(q_proj.shape, jnp.bfloat16)
    rot_query, rot_keys = local_call(
        rope_kernel, [rotated] * 2, [place, prompt_lengths], [freq, q_proj, k_proj]
    )
    column = blk_index % PLANE
    key_blocks, value_blocks = [
        [block, next_plane(block)] for block in (rot_keys, after(v_proj, rot_keys))
    ]
    for blocks in (key_blocks, value_blocks):
        own, below = blocks
        for mask in range(1, PLANE):
            blocks.append(flipped(jnp.where(column < column ^ mask, own, below), mask))
    heads = q_proj.shape[1] // HEAD_DIM
    probs_shape = (heads, tok_rows, len(key_blocks) * tok_rows)
    probs = local_call(
        score_kernel,
        [jax.ShapeDtypeStruct(probs_shape, jnp.bfloat16)],
        [place, prompt_lengths],
        [rot_query, *key_blocks],
        flops=2 * tok_rows * probs_shape[2] * heads * HEAD_DIM,
    )[0]
    page_count = tok_rows // PAGE
    local_page = page_table - blk_index * page_count
    kv_rows = jnp.stack([rot_keys, v_proj], axis=1).reshape(page_count, PAGE, 2, -1)
    kv_pages = jnp.zeros_like(kv_rows).at[local_page].set(kv_rows)
    lanes = gate_lanes(expert_ids, gate_weights, experts)
    probs = after(probs, kv_pages, lanes)
    mixed = local_call(
        mix_kernel,
        [jax.ShapeDtypeStruct((tok_rows, model_width), jnp.float32)],
        [place],
        [probs, out_weight, residual, *value_blocks],
        flops=2 * tok_rows * (probs_shape[2] + model_width) * heads * HEAD_DIM,
    )[0]
    if cores == 2:
        addends = [mixed, from_core(mixed, 1)]
    else:
        addends = [lax.psum(mixed, "tok")]
    payload, own_share = local_call(
        norm_kernel,
        [
            jax.ShapeDtypeStruct((part_rows, model_width + lanes.shape[1]), jnp.bfloat16),
            jax.ShapeDtypeStruct((tok_rows, col_width), jnp.bfloat16),
        ],
        [place],
        [norm_gain[None, :], lanes, *addends],
    )
    if planes <= 4:
        groups = [[0]] + [sorted({i, planes - i}) for i in range(1, planes // 2 + 1)]
    else:
        groups = [[0]] + [list(range(i, min(i + 8, planes))) for i in range(1, planes, 8)]
    weights = (w_gate[0].T, w_up[0].T, w_down[0])
    run = functools.partial(
        expert_outputs, place, weights=weights, experts=experts, cores=cores
    )
    columns, nears, fars, rows = [], [], [], {}
    sent = payload
    for group in groups:
        columns.append(
            jnp.concatenate([from_plane(sent, ahead) if ahead else sent for ahead in group])
        )
        sent = after(payload, columns[-1])
    for number, column in enumerate(columns):
        if number > 1:
            column = after(column, nears[-1])
        nears.append(
            jnp.concatenate([column, crossed(column, True, f"gather_first_{number}")])
        )
        fars.append(crossed(nears[-1], False, f"gather_second_{number}"))
    def rows_of_cores(number, *waits):
        near, far = nears[number], after(fars[number], *waits)
        return [
            (from_core(near, i), from_core(far, i)) if i else (near, far) for i in range(cores)
        ]

    outs = run(rows=rows_of_cores(0), planes=1, plane=0, span=1, waits={0: [columns[2]]})
    own_totals = core_totals(outs, cores)
    sent = after(second_share(own_totals), nears[-1])
    own_second = crossed(sent, False, "scatter_second_0")
    own_totals = merged(own_totals, own_second, 2)
    seconds, firsts, flips, returned = [], [], [], []
    span_of = 1 if planes <= 4 else 8
    steps = [
        (number, plane, group[plane : plane + span_of])
        for number, group in enumerate(groups)
        for plane in range(0, len(group), span_of)
    ]
    steps.sort(key=lambda step: step[2][0])
    for number, plane, aheads in steps[1:]:
        waits = {0: [outs], cores - 1: [*seconds[-1:]]}
        if len(seconds) > 1:
            waits[0].append(own_second)
        if number not in rows:
            rows[number] = rows_of_cores(number, outs if number == 1 else outs[0])
        outs = run(
            rows=rows[number],
            planes=len(groups[number]),
            plane=plane,
            span=len(aheads),
            waits=waits,
        )
        totals = core_totals(outs, cores, *firsts[-1:], *flips[-2:-1])
        seconds.append(second_share(totals))
        got = crossed(seconds[-1], False, f"scatter_second_{aheads[0]}")
        totals = merged(totals, got, 2)
        firsts.append(first_share(totals))
        got = crossed(firsts[-1], True, f"scatter_first_{aheads[0]}")
        rows_of = merged([total[0] for total in totals], got, None)
        blocks = []
        for i, ahead in enumerate(aheads):
            piece = [part[i * part_rows : (i + 1) * part_rows] for part in rows_of]
            blocks.append(narrow(jnp.concatenate(piece)))
            returned.append(to_plane(blocks[-1], ahead))
        flips.append(blocks)
    own_first = after(first_share(own_totals), *flips[-2:-1])
    own_got = crossed(own_first, True, "scatter_first_0")
    moe = jnp.concatenate(merged([total[0] for total in own_totals], own_got, None))
    moe = moe + sum(wide(block) for block in returned)
    moe = jnp.roll(moe.reshape(cores, part_rows, col_width), tok_index, axis=0)
    moe = moe.reshape(tok_rows, col_width)
    layer_out = (own_share.astype(jnp.float32) + moe).astype(jnp.bfloat16)
    return (layer_out, kv_pages)


def solution(mesh):
    placed = (
        P("blk", "tok"),
        P("blk", "tok"),
        P("blk", "tok"),
        P("blk", "tok"),
        P(),
        P("blk", None),
        P("blk", None),
        P("blk"),
        P("tok", None),
        P(),
        P("blk", None, "tok"),
        P("blk", None, "tok"),
        P("blk", "tok", None),
    )
    return jax.shard_map(
        on_device,
        mesh=mesh,
        in_specs=placed,
        out_specs=(P("blk", "tok"), P("blk", None, None, "tok")),
        check_vma=False,
    )
```

```python
import functools

import jax
import jax.numpy as jnp
from jax import lax
from jax.experimental import pallas as pl
from jax.experimental.pallas import tpu as pltpu
from jax.sharding import PartitionSpec as P

HEAD_DIM = 128
REACH = 4
PAGE = 16
PLANE = 4
EPSILON = 1e-06


def after(value, *others):
    return lax.optimization_barrier((value, *others))[0]


def flipped(block, mask):
    return lax.ppermute(block, "blk", [(i, i ^ mask) for i in range(lax.axis_size("blk"))])


def next_plane(block):
    count = lax.axis_size("blk")
    return lax.ppermute(block, "blk", [(i, i + PLANE) for i in range(count - PLANE)])


def from_plane(block, ahead):
    count = lax.axis_size("blk")
    with jax.named_scope(f"from_plane_{ahead}"):
        return lax.ppermute(
            block, "blk", [((i + PLANE * ahead) % count, i) for i in range(count)]
        )


def to_plane(block, ahead):
    count = lax.axis_size("blk")
    with jax.named_scope(f"to_plane_{ahead}"):
        return lax.ppermute(
            block, "blk", [(i, (i + PLANE * ahead) % count) for i in range(count)]
        )


def from_core(block, ahead):
    count = lax.axis_size("tok")
    return lax.ppermute(block, "tok", [((i + ahead) % count, i) for i in range(count)])


def segment_starts(place_ref, lengths_ref, shape):
    token = place_ref[0] * shape[0] + lax.broadcasted_iota(jnp.int32, shape, 0)
    start = jnp.zeros(shape, jnp.int32)
    end = jnp.int32(0)
    for i in range(lengths_ref.shape[0]):
        end = end + lengths_ref[i]
        start = jnp.where(token >= end, end, start)
    return token, start


def rope_kernel(place_ref, lengths_ref, freq_ref, q_ref, k_ref, q_out, k_out):
    rows, width = q_ref.shape
    shape = (rows, HEAD_DIM)
    token, start = segment_starts(place_ref, lengths_ref, shape)
    angle = (token - start).astype(jnp.float32) * freq_ref[...]
    cosine, sine = jnp.cos(angle), jnp.sin(angle)
    lane = lax.broadcasted_iota(jnp.int32, shape, 1)
    sine = jnp.where(lane < HEAD_DIM // 2, -sine, sine)
    for source, target in ((k_ref, k_out), (q_ref, q_out)):
        for head in range(width // HEAD_DIM):
            columns = slice(head * HEAD_DIM, (head + 1) * HEAD_DIM)
            x = source[:, columns].astype(jnp.float32)
            turned = x * cosine + pltpu.roll(x, HEAD_DIM // 2, 1) * sine
            target[:, columns] = turned.astype(jnp.bfloat16)


def score_kernel(place_ref, lengths_ref, q_ref, *rest):
    *keys, out_ref = rest
    rows, width = q_ref.shape
    shape = (rows, rows)
    token, start = segment_starts(place_ref, lengths_ref, shape)
    blk = place_ref[0]
    column = lax.rem(blk, PLANE)
    bases = [blk, blk - PLANE]
    for mask in range(1, PLANE):
        other = column ^ mask
        bases.append(blk - column + other - jnp.where(other > column, PLANE, 0))
    lane = lax.broadcasted_iota(jnp.int32, shape, 1)
    ids = jnp.concatenate([base * rows + lane for base in bases], axis=1)
    token = jnp.concatenate([token] * len(keys), axis=1)
    start = jnp.concatenate([start] * len(keys), axis=1)
    allowed = (ids >= start) & (ids <= token)
    for head in range(width // HEAD_DIM):
        columns = slice(head * HEAD_DIM, (head + 1) * HEAD_DIM)
        key = jnp.concatenate([ref[:, columns] for ref in keys], axis=0)
        scores = lax.dot_general(
            q_ref[:, columns],
            key,
            (((1,), (1,)), ((), ())),
            preferred_element_type=jnp.float32,
        )
        scores = jnp.where(allowed, scores * HEAD_DIM ** (-0.5), -1e30)
        terms = jnp.exp(scores - jnp.max(scores, axis=1, keepdims=True))
        share = 1.0 / jnp.sum(terms, axis=1, keepdims=True)
        out_ref[head] = (terms * share).astype(jnp.bfloat16)


def mix_kernel(place_ref, prob_ref, weight_ref, residual_ref, *rest):
    *values, out_ref = rest
    heads = prob_ref.shape[0]
    mixed = []
    for head in range(heads):
        columns = slice(head * HEAD_DIM, (head + 1) * HEAD_DIM)
        value = jnp.concatenate([ref[:, columns] for ref in values], axis=0)
        product = jnp.dot(prob_ref[head], value, preferred_element_type=jnp.float32)
        mixed.append(product.astype(jnp.bfloat16))
    attention = jnp.concatenate(mixed, axis=1)
    out_ref[...] = jnp.dot(attention, weight_ref[...], preferred_element_type=jnp.float32)
    width = residual_ref.shape[1]
    own = pl.ds(pl.multiple_of(place_ref[1] * width, 128), width)
    out_ref[:, own] = out_ref[:, own] + residual_ref[...].astype(jnp.float32)


def norm_kernel(place_ref, gain_ref, lanes_ref, *rest):
    *addends, rows_out, share_out = rest
    rows, width = addends[0].shape
    part_rows = rows_out.shape[0]
    part_width = share_out.shape[1]
    own = pl.ds(pl.multiple_of(place_ref[1] * part_width, 128), part_width)
    share_out[...] = sum(ref[:, own] for ref in addends).astype(jnp.bfloat16)
    part = pl.ds(pl.multiple_of(place_ref[1] * part_rows, 16), part_rows)
    stream = sum(ref[part, :] for ref in addends).astype(jnp.bfloat16).astype(jnp.float32)
    scale = lax.rsqrt(jnp.mean(stream * stream, axis=1, keepdims=True) + EPSILON)
    rows_out[:, :width] = (stream * scale * gain_ref[...]).astype(jnp.bfloat16)
    rows_out[:, width:] = lanes_ref[part, :]


def local_call(body, out_shapes, scalars, arrays, flops=0, moved=0, limit=16):
    whole = pl.BlockSpec(memory_space=pltpu.VMEM)
    scalar = pl.BlockSpec(memory_space=pltpu.SMEM)
    moved = moved or sum(x.size * x.dtype.itemsize for x in (*arrays, *out_shapes))
    return pl.pallas_call(
        body,
        in_specs=[scalar] * len(scalars) + [whole] * len(arrays),
        out_specs=[whole] * len(out_shapes),
        out_shape=out_shapes,
        cost_estimate=pl.CostEstimate(flops=flops, bytes_accessed=moved, transcendentals=0),
        compiler_params=pltpu.CompilerParams(vmem_limit_bytes=limit << 20),
    )(*scalars, *arrays)


def gate_lanes(expert_ids, gate_weights, experts):
    hits = expert_ids[:, :, None] == jnp.arange(experts, dtype=jnp.int32)[None, None, :]
    gates = jnp.sum(jnp.where(hits, gate_weights[:, :, None], 0.0), axis=1)
    pieces = []
    for _ in range(3):
        piece = lax.reduce_precision(gates, 8, 7)
        pieces.append(piece.astype(jnp.bfloat16))
        gates = gates - piece
    lanes = jnp.concatenate(pieces, axis=1)
    return jnp.pad(lanes, ((0, 0), (0, -lanes.shape[1] % 128)))


def crossed(block, first, name="flip"):
    cores, count = lax.axis_size("tok"), lax.axis_size("blk")
    route = []
    for core in range(cores):
        mask = 1 if (core % 2 == 0) == first else 2
        route += [(core * count + i, core * count + (i ^ mask)) for i in range(count)]
    with jax.named_scope(name):
        return lax.ppermute(block, ("tok", "blk"), route)


def expert_kernel(experts, ahead, planes, plane, span, place_ref, near_ref, far_ref, gate_ref, up_ref, down_ref, *outs):
    width = gate_ref.shape[1]
    parts = len(outs)
    blocks, part_rows, part_width = outs[0].shape
    starts = [(i * planes + plane) * part_rows // span for i in range(2)]
    held = jnp.concatenate(
        [ref[start : start + part_rows] for ref in (near_ref, far_ref) for start in starts],
        axis=0,
    )
    rows = held[:, :width]
    lanes = held[:, width:].astype(jnp.float32)
    lane_ids = lax.broadcasted_iota(jnp.int32, lanes.shape, 1)
    named = (lane_ids < 3 * experts) & (lane_ids % experts == place_ref[0])
    weight = jnp.sum(jnp.where(named, lanes, 0.0), axis=1, keepdims=True)
    turned = (((1,), (1,)), ((), ()))
    gate_act = lax.dot_general(rows, gate_ref[...], turned, preferred_element_type=jnp.float32)
    up_act = lax.dot_general(rows, up_ref[...], turned, preferred_element_type=jnp.float32)
    hidden = (gate_act / (1.0 + jnp.exp(-gate_act)) * up_act).astype(jnp.bfloat16)
    for part in range(parts):
        start = lax.rem(place_ref[1] + part, parts) * part_width
        columns = pl.ds(pl.multiple_of(start, 128), part_width)
        product = jnp.dot(hidden, down_ref[:, columns], preferred_element_type=jnp.float32)
        product = (weight * product).astype(jnp.bfloat16)
        order = (0, 2, 1, 3) if (part - ahead) % 2 else (0, 1, 2, 3)
        for block in range(blocks):
            outs[part][order[block]] = product[block * part_rows : (block + 1) * part_rows]


def run_expert(place, near, far, w_gate, w_up, w_down, experts, parts, ahead, planes, plane, span):
    count = 2 * near.shape[0] // planes * span
    units, width = w_gate.shape
    out_shape = jax.ShapeDtypeStruct((PLANE, count // PLANE, width // parts), jnp.bfloat16)
    return local_call(
        functools.partial(expert_kernel, experts, ahead, planes, plane, span),
        [out_shape] * parts,
        [place],
        [near, far, w_gate, w_up, w_down],
        flops=6 * count * width * units,
    )


def wide(block):
    return block.astype(jnp.float32)


def narrow(block):
    return block.astype(jnp.bfloat16)


def second_share(totals):
    return narrow(jnp.stack([total[2:4] for total in totals]))


def first_share(totals):
    return narrow(jnp.stack([total[1] for total in totals]))


def merged(totals, got, count):
    return [total[0:count] + wide(got[i]) for i, total in enumerate(totals)]


def expert_outputs(place, rows, weights, experts, cores, planes, plane, span, waits):
    outs = []
    for ahead in range(cores):
        near, far = rows[ahead]
        near = after(near, *outs[-1:], *waits.get(ahead, []))
        outs.append(
            run_expert(
                place, near, far, *weights, experts, cores, ahead, planes, plane, span
            )
        )
    return outs


def core_totals(outs, cores, *waits):
    totals = []
    for rows_of in range(cores):
        total = wide(outs[rows_of][0])
        for ahead in range(1, cores):
            sent = outs[(rows_of + ahead) % cores][ahead]
            total = total + wide(after(from_core(sent, cores - ahead), *waits))
        totals.append(total)
    return totals


def on_device(
    q_proj,
    k_proj,
    v_proj,
    residual,
    prompt_lengths,
    expert_ids,
    gate_weights,
    page_table,
    out_weight,
    norm_gain,
    w_gate,
    w_up,
    w_down,
):
    tok_rows = q_proj.shape[0]
    col_width = residual.shape[1]
    model_width = norm_gain.shape[0]
    blk_index = lax.axis_index("blk")
    tok_index = lax.axis_index("tok")
    cores = lax.axis_size("tok")
    experts = lax.axis_size("blk")
    planes = experts // PLANE
    place = jnp.stack([blk_index, tok_index]).astype(jnp.int32)
    part_rows = tok_rows // cores
    half_dim = HEAD_DIM // 2
    inv_freq = 10000.0 ** (-jnp.arange(half_dim, dtype=jnp.float32) / half_dim)
    freq = jnp.concatenate([inv_freq, inv_freq])[None, :]
    rotated = jax.ShapeDtypeStruct(q_proj.shape, jnp.bfloat16)
    rot_query, rot_keys = local_call(
        rope_kernel, [rotated] * 2, [place, prompt_lengths], [freq, q_proj, k_proj]
    )
    column = blk_index % PLANE
    key_blocks, value_blocks = [
        [block, next_plane(block)] for block in (rot_keys, after(v_proj, rot_keys))
    ]
    for blocks in (key_blocks, value_blocks):
        own, below = blocks
        for mask in range(1, PLANE):
            blocks.append(flipped(jnp.where(column < column ^ mask, own, below), mask))
    heads = q_proj.shape[1] // HEAD_DIM
    probs_shape = (heads, tok_rows, len(key_blocks) * tok_rows)
    probs = local_call(
        score_kernel,
        [jax.ShapeDtypeStruct(probs_shape, jnp.bfloat16)],
        [place, prompt_lengths],
        [rot_query, *key_blocks],
        flops=2 * tok_rows * probs_shape[2] * heads * HEAD_DIM,
    )[0]
    page_count = tok_rows // PAGE
    local_page = page_table - blk_index * page_count
    kv_rows = jnp.stack([rot_keys, v_proj], axis=1).reshape(page_count, PAGE, 2, -1)
    kv_pages = jnp.zeros_like(kv_rows).at[local_page].set(kv_rows)
    lanes = gate_lanes(expert_ids, gate_weights, experts)
    probs = after(probs, kv_pages, lanes)
    mixed = local_call(
        mix_kernel,
        [jax.ShapeDtypeStruct((tok_rows, model_width), jnp.float32)],
        [place],
        [probs, out_weight, residual, *value_blocks],
        flops=2 * tok_rows * (probs_shape[2] + model_width) * heads * HEAD_DIM,
    )[0]
    if cores == 2:
        addends = [mixed, from_core(mixed, 1)]
    else:
        addends = [lax.psum(mixed, "tok")]
    payload, own_share = local_call(
        norm_kernel,
        [
            jax.ShapeDtypeStruct((part_rows, model_width + lanes.shape[1]), jnp.bfloat16),
            jax.ShapeDtypeStruct((tok_rows, col_width), jnp.bfloat16),
        ],
        [place],
        [norm_gain[None, :], lanes, *addends],
    )
    if planes <= 4:
        groups = [[0]] + [sorted({i, planes - i}) for i in range(1, planes // 2 + 1)]
    else:
        groups = [[0]] + [list(range(i, min(i + 8, planes))) for i in range(1, planes, 8)]
    weights = (w_gate[0].T, w_up[0].T, w_down[0])
    run = functools.partial(
        expert_outputs, place, weights=weights, experts=experts, cores=cores
    )
    columns, nears, fars, rows = [], [], [], {}
    sent = payload
    for group in groups:
        columns.append(
            jnp.concatenate([from_plane(sent, ahead) if ahead else sent for ahead in group])
        )
        sent = after(payload, columns[-1])
    def rows_of_cores(number, *waits):
        near, far = nears[number], after(fars[number], *waits)
        return [
            (from_core(near, i), from_core(far, i)) if i else (near, far) for i in range(cores)
        ]

    def gather(number, *waits):
        column = after(columns[number], *waits)
        got = crossed(column, True, f"gather_first_{number}")
        nears.append(jnp.concatenate([column, got]))
        fars.append(crossed(nears[-1], False, f"gather_second_{number}"))

    gather(0)
    gather(1, nears[0], fars[0])
    outs = run(rows=rows_of_cores(0), planes=1, plane=0, span=1, waits={})
    own_totals = core_totals(outs, cores)
    seconds, firsts, flips, returned = [], [], [], []
    span_of = 1 if planes <= 4 else 8
    steps = [
        (number, plane, group[plane : plane + span_of])
        for number, group in enumerate(groups)
        for plane in range(0, len(group), span_of)
    ]
    for number, plane, aheads in steps[1:]:
        waits = {0: [outs], cores - 1: [*seconds[-1:]]}
        if len(seconds) > 1:
            waits[0].append(own_second)
        if number not in rows:
            rows[number] = rows_of_cores(number, outs if number == 1 else outs[0])
        outs = run(
            rows=rows[number],
            planes=len(groups[number]),
            plane=plane,
            span=len(aheads),
            waits=waits,
        )
        if len(seconds) == 0:
            gather(2, nears[1], outs[0])
            sent = after(second_share(own_totals), nears[-1])
            own_second = crossed(sent, False, "scatter_second_0")
            own_totals = merged(own_totals, own_second, 2)
        totals = core_totals(outs, cores, *firsts[-1:], *flips[-2:-1])
        seconds.append(second_share(totals))
        got = crossed(seconds[-1], False, f"scatter_second_{aheads[0]}")
        totals = merged(totals, got, 2)
        firsts.append(first_share(totals))
        got = crossed(firsts[-1], True, f"scatter_first_{aheads[0]}")
        rows_of = merged([total[0] for total in totals], got, None)
        blocks = []
        for i, ahead in enumerate(aheads):
            piece = [part[i * part_rows : (i + 1) * part_rows] for part in rows_of]
            blocks.append(narrow(jnp.concatenate(piece)))
            returned.append(to_plane(blocks[-1], ahead))
        flips.append(blocks)
    own_first = after(first_share(own_totals), *flips[-2:-1])
    own_got = crossed(own_first, True, "scatter_first_0")
    moe = jnp.concatenate(merged([total[0] for total in own_totals], own_got, None))
    moe = moe + sum(wide(block) for block in returned)
    moe = jnp.roll(moe.reshape(cores, part_rows, col_width), tok_index, axis=0)
    moe = moe.reshape(tok_rows, col_width)
    layer_out = (own_share.astype(jnp.float32) + moe).astype(jnp.bfloat16)
    return (layer_out, kv_pages)


def solution(mesh):
    placed = (
        P("blk", "tok"),
        P("blk", "tok"),
        P("blk", "tok"),
        P("blk", "tok"),
        P(),
        P("blk", None),
        P("blk", None),
        P("blk"),
        P("tok", None),
        P(),
        P("blk", None, "tok"),
        P("blk", None, "tok"),
        P("blk", "tok", None),
    )
    return jax.shard_map(
        on_device,
        mesh=mesh,
        in_specs=placed,
        out_specs=(P("blk", "tok"), P("blk", None, None, "tok")),
        check_vma=False,
    )
```

```python
import functools

import jax
import jax.numpy as jnp
from jax import lax
from jax.experimental import pallas as pl
from jax.experimental.pallas import tpu as pltpu
from jax.sharding import PartitionSpec as P

HEAD_DIM = 128
REACH = 4
PAGE = 16
PLANE = 4
EPSILON = 1e-06


def after(value, *others):
    return lax.optimization_barrier((value, *others))[0]


def flipped(block, mask):
    return lax.ppermute(block, "blk", [(i, i ^ mask) for i in range(lax.axis_size("blk"))])


def next_plane(block):
    count = lax.axis_size("blk")
    return lax.ppermute(block, "blk", [(i, i + PLANE) for i in range(count - PLANE)])


def from_plane(block, ahead):
    count = lax.axis_size("blk")
    return lax.ppermute(
        block, "blk", [((i + PLANE * ahead) % count, i) for i in range(count)]
    )


def to_plane(block, ahead):
    count = lax.axis_size("blk")
    return lax.ppermute(
        block, "blk", [(i, (i + PLANE * ahead) % count) for i in range(count)]
    )


def from_core(block, ahead):
    count = lax.axis_size("tok")
    return lax.ppermute(block, "tok", [((i + ahead) % count, i) for i in range(count)])


def segment_starts(place_ref, lengths_ref, shape):
    token = place_ref[0] * shape[0] + lax.broadcasted_iota(jnp.int32, shape, 0)
    start = jnp.zeros(shape, jnp.int32)
    end = jnp.int32(0)
    for i in range(lengths_ref.shape[0]):
        end = end + lengths_ref[i]
        start = jnp.where(token >= end, end, start)
    return token, start


def rope_kernel(place_ref, lengths_ref, freq_ref, q_ref, k_ref, q_out, k_out):
    rows, width = q_ref.shape
    shape = (rows, HEAD_DIM)
    token, start = segment_starts(place_ref, lengths_ref, shape)
    angle = (token - start).astype(jnp.float32) * freq_ref[...]
    cosine, sine = jnp.cos(angle), jnp.sin(angle)
    lane = lax.broadcasted_iota(jnp.int32, shape, 1)
    sine = jnp.where(lane < HEAD_DIM // 2, -sine, sine)
    for source, target in ((k_ref, k_out), (q_ref, q_out)):
        for head in range(width // HEAD_DIM):
            columns = slice(head * HEAD_DIM, (head + 1) * HEAD_DIM)
            x = source[:, columns].astype(jnp.float32)
            turned = x * cosine + pltpu.roll(x, HEAD_DIM // 2, 1) * sine
            target[:, columns] = turned.astype(jnp.bfloat16)


def score_kernel(place_ref, lengths_ref, q_ref, weight_ref, *rest):
    *keys, out_ref = rest
    rows, width = q_ref.shape
    shape = (rows, rows)
    token, start = segment_starts(place_ref, lengths_ref, shape)
    blk = place_ref[0]
    column = lax.rem(blk, PLANE)
    bases = [blk, blk - PLANE]
    for mask in range(1, PLANE):
        other = column ^ mask
        bases.append(blk - column + other - jnp.where(other > column, PLANE, 0))
    lane = lax.broadcasted_iota(jnp.int32, shape, 1)
    ids = jnp.concatenate([base * rows + lane for base in bases], axis=1)
    token = jnp.concatenate([token] * len(keys), axis=1)
    start = jnp.concatenate([start] * len(keys), axis=1)
    allowed = (ids >= start) & (ids <= token)
    for head in range(width // HEAD_DIM):
        columns = slice(head * HEAD_DIM, (head + 1) * HEAD_DIM)
        key = jnp.concatenate([ref[:, columns] for ref in keys], axis=0)
        scores = lax.dot_general(
            q_ref[:, columns],
            key,
            (((1,), (1,)), ((), ())),
            preferred_element_type=jnp.float32,
        )
        scores = jnp.where(allowed, scores * HEAD_DIM ** (-0.5), -1e30)
        terms = jnp.exp(scores - jnp.max(scores, axis=1, keepdims=True))
        share = 1.0 / jnp.sum(terms, axis=1, keepdims=True)
        out_ref[head] = (terms * share).astype(jnp.bfloat16)


def mix_kernel(place_ref, prob_ref, weight_ref, residual_ref, *rest):
    *values, out_ref = rest
    heads = prob_ref.shape[0]
    mixed = []
    for head in range(heads):
        columns = slice(head * HEAD_DIM, (head + 1) * HEAD_DIM)
        value = jnp.concatenate([ref[:, columns] for ref in values], axis=0)
        product = jnp.dot(prob_ref[head], value, preferred_element_type=jnp.float32)
        mixed.append(product.astype(jnp.bfloat16))
    attention = jnp.concatenate(mixed, axis=1)
    out_ref[...] = jnp.dot(attention, weight_ref[...], preferred_element_type=jnp.float32)
    width = residual_ref.shape[1]
    own = pl.ds(pl.multiple_of(place_ref[1] * width, 128), width)
    out_ref[:, own] = out_ref[:, own] + residual_ref[...].astype(jnp.float32)


def norm_kernel(place_ref, gain_ref, lanes_ref, *rest):
    *addends, rows_out, share_out = rest
    rows, width = addends[0].shape
    part_rows = rows_out.shape[0]
    part_width = share_out.shape[1]
    own = pl.ds(pl.multiple_of(place_ref[1] * part_width, 128), part_width)
    share_out[...] = sum(ref[:, own] for ref in addends).astype(jnp.bfloat16)
    part = pl.ds(pl.multiple_of(place_ref[1] * part_rows, 16), part_rows)
    stream = sum(ref[part, :] for ref in addends).astype(jnp.bfloat16).astype(jnp.float32)
    scale = lax.rsqrt(jnp.mean(stream * stream, axis=1, keepdims=True) + EPSILON)
    rows_out[:, :width] = (stream * scale * gain_ref[...]).astype(jnp.bfloat16)
    rows_out[:, width:] = lanes_ref[part, :]


def local_call(body, out_shapes, scalars, arrays, flops=0, limit=16):
    whole = pl.BlockSpec(memory_space=pltpu.VMEM)
    scalar = pl.BlockSpec(memory_space=pltpu.SMEM)
    moved = sum(x.size * x.dtype.itemsize for x in (*arrays, *out_shapes))
    return pl.pallas_call(
        body,
        in_specs=[scalar] * len(scalars) + [whole] * len(arrays),
        out_specs=[whole] * len(out_shapes),
        out_shape=out_shapes,
        cost_estimate=pl.CostEstimate(flops=flops, bytes_accessed=moved, transcendentals=0),
        compiler_params=pltpu.CompilerParams(vmem_limit_bytes=limit << 20),
    )(*scalars, *arrays)


def gate_lanes(expert_ids, gate_weights, experts):
    hits = expert_ids[:, :, None] == jnp.arange(experts, dtype=jnp.int32)[None, None, :]
    gates = jnp.sum(jnp.where(hits, gate_weights[:, :, None], 0.0), axis=1)
    pieces = []
    for _ in range(3):
        piece = lax.reduce_precision(gates, 8, 7)
        pieces.append(piece.astype(jnp.bfloat16))
        gates = gates - piece
    lanes = jnp.concatenate(pieces, axis=1)
    return jnp.pad(lanes, ((0, 0), (0, -lanes.shape[1] % 128)))


def crossed(block, first):
    cores, count = lax.axis_size("tok"), lax.axis_size("blk")
    route = []
    for core in range(cores):
        mask = 1 if (core % 2 == 0) == first else 2
        route += [(core * count + i, core * count + (i ^ mask)) for i in range(count)]
    return lax.ppermute(block, ("tok", "blk"), route)


def expert_kernel(experts, ahead, place_ref, near_ref, far_ref, gate_ref, up_ref, down_ref, *outs):
    width = gate_ref.shape[1]
    parts = len(outs)
    blocks, part_rows, part_width = outs[0].shape
    held = jnp.concatenate([near_ref[...], far_ref[...]], axis=0)
    rows = held[:, :width]
    lanes = held[:, width:].astype(jnp.float32)
    lane_ids = lax.broadcasted_iota(jnp.int32, lanes.shape, 1)
    named = (lane_ids < 3 * experts) & (lane_ids % experts == place_ref[0])
    weight = jnp.sum(jnp.where(named, lanes, 0.0), axis=1, keepdims=True)
    turned = (((1,), (1,)), ((), ()))
    gate_act = lax.dot_general(rows, gate_ref[...], turned, preferred_element_type=jnp.float32)
    up_act = lax.dot_general(rows, up_ref[...], turned, preferred_element_type=jnp.float32)
    hidden = (gate_act / (1.0 + jnp.exp(-gate_act)) * up_act).astype(jnp.bfloat16)
    for part in range(parts):
        start = lax.rem(place_ref[1] + part, parts) * part_width
        columns = pl.ds(pl.multiple_of(start, 128), part_width)
        product = jnp.dot(hidden, down_ref[:, columns], preferred_element_type=jnp.float32)
        product = (weight * product).astype(jnp.bfloat16)
        order = (0, 2, 1, 3) if (part - ahead) % 2 else (0, 1, 2, 3)
        for block in range(blocks):
            outs[part][order[block]] = product[block * part_rows : (block + 1) * part_rows]


def run_expert(place, near, far, w_gate, w_up, w_down, experts, parts, ahead):
    count = 2 * near.shape[0]
    units, width = w_gate.shape
    out_shape = jax.ShapeDtypeStruct((PLANE, count // PLANE, width // parts), jnp.bfloat16)
    return local_call(
        functools.partial(expert_kernel, experts, ahead),
        [out_shape] * parts,
        [place],
        [near, far, w_gate, w_up, w_down],
        flops=6 * count * width * units,
    )


def wide(block):
    return block.astype(jnp.float32)


def narrow(block):
    return block.astype(jnp.bfloat16)


def second_share(totals):
    return narrow(jnp.stack([total[2:4] for total in totals]))


def first_share(totals):
    return narrow(jnp.stack([total[1] for total in totals]))


def merged(totals, got, count):
    return [total[0:count] + wide(got[i]) for i, total in enumerate(totals)]


def expert_outputs(place, near, far, weights, experts, cores, waits):
    outs = []
    for ahead in range(cores):
        near_rows = from_core(near, ahead) if ahead else near
        far_rows = from_core(far, ahead) if ahead else far
        near_rows = after(near_rows, *outs[-1:], *waits.get(ahead, []))
        outs.append(run_expert(place, near_rows, far_rows, *weights, experts, cores, ahead))
    return outs


def core_totals(outs, cores):
    totals = []
    for rows_of in range(cores):
        total = wide(outs[rows_of][0])
        for ahead in range(1, cores):
            sent = outs[(rows_of + ahead) % cores][ahead]
            total = total + wide(from_core(sent, cores - ahead))
        totals.append(total)
    return totals


def on_device(
    q_proj,
    k_proj,
    v_proj,
    residual,
    prompt_lengths,
    expert_ids,
    gate_weights,
    page_table,
    out_weight,
    norm_gain,
    w_gate,
    w_up,
    w_down,
):
    tok_rows = q_proj.shape[0]
    col_width = residual.shape[1]
    model_width = norm_gain.shape[0]
    blk_index = lax.axis_index("blk")
    tok_index = lax.axis_index("tok")
    cores = lax.axis_size("tok")
    experts = lax.axis_size("blk")
    planes = experts // PLANE
    place = jnp.stack([blk_index, tok_index]).astype(jnp.int32)
    part_rows = tok_rows // cores
    half_dim = HEAD_DIM // 2
    inv_freq = 10000.0 ** (-jnp.arange(half_dim, dtype=jnp.float32) / half_dim)
    freq = jnp.concatenate([inv_freq, inv_freq])[None, :]
    rotated = jax.ShapeDtypeStruct(q_proj.shape, jnp.bfloat16)
    rot_query, rot_keys = local_call(
        rope_kernel, [rotated] * 2, [place, prompt_lengths], [freq, q_proj, k_proj]
    )
    column = blk_index % PLANE
    key_blocks, value_blocks = [
        [block, next_plane(block)] for block in (rot_keys, after(v_proj, rot_keys))
    ]
    for blocks in (key_blocks, value_blocks):
        own, below = blocks
        for mask in range(1, PLANE):
            blocks.append(flipped(jnp.where(column < column ^ mask, own, below), mask))
    heads = q_proj.shape[1] // HEAD_DIM
    probs_shape = (heads, tok_rows, len(key_blocks) * tok_rows)
    probs = local_call(
        score_kernel,
        [jax.ShapeDtypeStruct(probs_shape, jnp.bfloat16)],
        [place, prompt_lengths],
        [rot_query, out_weight, *key_blocks],
        flops=2 * tok_rows * probs_shape[2] * heads * HEAD_DIM,
    )[0]
    page_count = tok_rows // PAGE
    local_page = page_table - blk_index * page_count
    kv_rows = jnp.stack([rot_keys, v_proj], axis=1).reshape(page_count, PAGE, 2, -1)
    kv_pages = jnp.zeros_like(kv_rows).at[local_page].set(kv_rows)
    lanes = gate_lanes(expert_ids, gate_weights, experts)
    probs = after(probs, kv_pages, lanes)
    mixed = local_call(
        mix_kernel,
        [jax.ShapeDtypeStruct((tok_rows, model_width), jnp.float32)],
        [place],
        [probs, out_weight, residual, *value_blocks],
        flops=2 * tok_rows * (probs_shape[2] + model_width) * heads * HEAD_DIM,
    )[0]
    if cores == 2:
        addends = [mixed, from_core(mixed, 1)]
    else:
        addends = [lax.psum(mixed, "tok")]
    payload, own_share = local_call(
        norm_kernel,
        [
            jax.ShapeDtypeStruct((part_rows, model_width + lanes.shape[1]), jnp.bfloat16),
            jax.ShapeDtypeStruct((tok_rows, col_width), jnp.bfloat16),
        ],
        [place],
        [norm_gain[None, :], lanes, *addends],
    )
    weights = (w_gate[0].T, w_up[0].T, w_down[0])
    if planes <= 4:
        groups = [[0]] + [sorted({i, planes - i}) for i in range(1, planes // 2 + 1)]
    else:
        groups = [[0]] + [list(range(i, min(i + 8, planes))) for i in range(1, planes, 8)]
    nears, fars = [], []
    for number, group in enumerate(groups):
        sent = after(payload, nears[0]) if number > 1 else payload
        column = jnp.concatenate([from_plane(sent, ahead) if ahead else sent for ahead in group])
        if number > 1:
            column = after(column, nears[-1])
        nears.append(jnp.concatenate([column, crossed(column, True)]))
        fars.append(crossed(nears[-1], False))
    weights = (w_gate[0].T, w_up[0].T, w_down[0])
    run = functools.partial(
        expert_outputs, place, weights=weights, experts=experts, cores=cores
    )
    outs = run(nears[0], fars[0], waits={})
    own_totals = core_totals(outs, cores)
    got = crossed(after(second_share(own_totals), nears[-1]), False)
    own_totals = merged(own_totals, got, 2)
    own_got = crossed(first_share(own_totals), True)
    totals, sents = [], []
    for number in range(1, len(groups)):
        waits = {0: [outs]}
        if number == len(groups) - 1:
            waits = {0: [outs, got], cores - 1: [own_got, *sents]}
        outs = run(nears[number], fars[number], waits=waits)
        totals.append(core_totals(outs, cores))
        sents.append(second_share(totals[-1]))
    got_list, ready = [], []
    for pair, sent in zip(totals, sents, strict=True):
        pair = merged(pair, after(crossed(sent, False), *ready), 2)
        ready = [first_share(pair)]
        got_list.append((pair, crossed(ready[0], True)))
    totals = [pair for pair, _ in got_list]
    gots = [got for _, got in got_list]
    results = {}
    for group, pair, came in zip(
        groups, [own_totals, *totals], [own_got, *gots], strict=True
    ):
        rows_of = merged([total[0] for total in pair], came, None)
        for i, ahead in enumerate(group):
            results[ahead] = jnp.concatenate(
                [rows[i * part_rows : (i + 1) * part_rows] for rows in rows_of]
            )
    moe = results[0]
    for ahead in range(1, planes):
        moe = moe + wide(to_plane(narrow(results[ahead]), ahead))
    moe = jnp.roll(moe.reshape(cores, part_rows, col_width), tok_index, axis=0)
    moe = moe.reshape(tok_rows, col_width)
    layer_out = (own_share.astype(jnp.float32) + moe).astype(jnp.bfloat16)
    return (layer_out, kv_pages)


def solution(mesh):
    placed = (
        P("blk", "tok"),
        P("blk", "tok"),
        P("blk", "tok"),
        P("blk", "tok"),
        P(),
        P("blk", None),
        P("blk", None),
        P("blk"),
        P("tok", None),
        P(),
        P("blk", None, "tok"),
        P("blk", None, "tok"),
        P("blk", "tok", None),
    )
    return jax.shard_map(
        on_device,
        mesh=mesh,
        in_specs=placed,
        out_specs=(P("blk", "tok"), P("blk", None, None, "tok")),
        check_vma=False,
    )
```

```python
import functools

import jax
import jax.numpy as jnp
from jax import lax
from jax.experimental import pallas as pl
from jax.experimental.pallas import tpu as pltpu
from jax.sharding import PartitionSpec as P

HEAD_DIM = 128
REACH = 4
PAGE = 16
PLANE = 4
EPSILON = 1e-06


def after(value, *others):
    return lax.optimization_barrier((value, *others))[0]


def flipped(block, mask):
    return lax.ppermute(block, "blk", [(i, i ^ mask) for i in range(lax.axis_size("blk"))])


def next_plane(block):
    count = lax.axis_size("blk")
    return lax.ppermute(block, "blk", [(i, i + PLANE) for i in range(count - PLANE)])


def from_plane(block, ahead):
    count = lax.axis_size("blk")
    return lax.ppermute(
        block, "blk", [((i + PLANE * ahead) % count, i) for i in range(count)]
    )


def to_plane(block, ahead):
    count = lax.axis_size("blk")
    return lax.ppermute(
        block, "blk", [(i, (i + PLANE * ahead) % count) for i in range(count)]
    )


def from_core(block, ahead):
    count = lax.axis_size("tok")
    return lax.ppermute(block, "tok", [((i + ahead) % count, i) for i in range(count)])


def segment_starts(place_ref, lengths_ref, shape):
    token = place_ref[0] * shape[0] + lax.broadcasted_iota(jnp.int32, shape, 0)
    start = jnp.zeros(shape, jnp.int32)
    end = jnp.int32(0)
    for i in range(lengths_ref.shape[0]):
        end = end + lengths_ref[i]
        start = jnp.where(token >= end, end, start)
    return token, start


def rope_kernel(place_ref, lengths_ref, freq_ref, q_ref, k_ref, q_out, k_out):
    rows, width = q_ref.shape
    shape = (rows, HEAD_DIM)
    token, start = segment_starts(place_ref, lengths_ref, shape)
    angle = (token - start).astype(jnp.float32) * freq_ref[...]
    cosine, sine = jnp.cos(angle), jnp.sin(angle)
    lane = lax.broadcasted_iota(jnp.int32, shape, 1)
    sine = jnp.where(lane < HEAD_DIM // 2, -sine, sine)
    for source, target in ((k_ref, k_out), (q_ref, q_out)):
        for head in range(width // HEAD_DIM):
            columns = slice(head * HEAD_DIM, (head + 1) * HEAD_DIM)
            x = source[:, columns].astype(jnp.float32)
            turned = x * cosine + pltpu.roll(x, HEAD_DIM // 2, 1) * sine
            target[:, columns] = turned.astype(jnp.bfloat16)


def score_kernel(place_ref, lengths_ref, q_ref, weight_ref, *rest):
    *keys, out_ref = rest
    rows, width = q_ref.shape
    shape = (rows, rows)
    token, start = segment_starts(place_ref, lengths_ref, shape)
    blk = place_ref[0]
    column = lax.rem(blk, PLANE)
    bases = [blk, blk - PLANE]
    for mask in range(1, PLANE):
        other = column ^ mask
        bases.append(blk - column + other - jnp.where(other > column, PLANE, 0))
    lane = lax.broadcasted_iota(jnp.int32, shape, 1)
    ids = jnp.concatenate([base * rows + lane for base in bases], axis=1)
    token = jnp.concatenate([token] * len(keys), axis=1)
    start = jnp.concatenate([start] * len(keys), axis=1)
    allowed = (ids >= start) & (ids <= token)
    for head in range(width // HEAD_DIM):
        columns = slice(head * HEAD_DIM, (head + 1) * HEAD_DIM)
        key = jnp.concatenate([ref[:, columns] for ref in keys], axis=0)
        scores = lax.dot_general(
            q_ref[:, columns],
            key,
            (((1,), (1,)), ((), ())),
            preferred_element_type=jnp.float32,
        )
        scores = jnp.where(allowed, scores * HEAD_DIM ** (-0.5), -1e30)
        terms = jnp.exp(scores - jnp.max(scores, axis=1, keepdims=True))
        share = 1.0 / jnp.sum(terms, axis=1, keepdims=True)
        out_ref[head] = (terms * share).astype(jnp.bfloat16)


def mix_kernel(place_ref, prob_ref, weight_ref, residual_ref, *rest):
    *values, out_ref = rest
    heads = prob_ref.shape[0]
    mixed = []
    for head in range(heads):
        columns = slice(head * HEAD_DIM, (head + 1) * HEAD_DIM)
        value = jnp.concatenate([ref[:, columns] for ref in values], axis=0)
        product = jnp.dot(prob_ref[head], value, preferred_element_type=jnp.float32)
        mixed.append(product.astype(jnp.bfloat16))
    attention = jnp.concatenate(mixed, axis=1)
    out_ref[...] = jnp.dot(attention, weight_ref[...], preferred_element_type=jnp.float32)
    width = residual_ref.shape[1]
    own = pl.ds(pl.multiple_of(place_ref[1] * width, 128), width)
    out_ref[:, own] = out_ref[:, own] + residual_ref[...].astype(jnp.float32)


def norm_kernel(place_ref, gain_ref, lanes_ref, *rest):
    *addends, rows_out, share_out = rest
    rows, width = addends[0].shape
    part_rows = rows_out.shape[0]
    part_width = share_out.shape[1]
    own = pl.ds(pl.multiple_of(place_ref[1] * part_width, 128), part_width)
    share_out[...] = sum(ref[:, own] for ref in addends).astype(jnp.bfloat16)
    part = pl.ds(pl.multiple_of(place_ref[1] * part_rows, 16), part_rows)
    stream = sum(ref[part, :] for ref in addends).astype(jnp.bfloat16).astype(jnp.float32)
    scale = lax.rsqrt(jnp.mean(stream * stream, axis=1, keepdims=True) + EPSILON)
    rows_out[:, :width] = (stream * scale * gain_ref[...]).astype(jnp.bfloat16)
    rows_out[:, width:] = lanes_ref[part, :]


def local_call(body, out_shapes, scalars, arrays, flops=0, limit=16):
    whole = pl.BlockSpec(memory_space=pltpu.VMEM)
    scalar = pl.BlockSpec(memory_space=pltpu.SMEM)
    moved = sum(x.size * x.dtype.itemsize for x in (*arrays, *out_shapes))
    return pl.pallas_call(
        body,
        in_specs=[scalar] * len(scalars) + [whole] * len(arrays),
        out_specs=[whole] * len(out_shapes),
        out_shape=out_shapes,
        cost_estimate=pl.CostEstimate(flops=flops, bytes_accessed=moved, transcendentals=0),
        compiler_params=pltpu.CompilerParams(vmem_limit_bytes=limit << 20),
    )(*scalars, *arrays)


def gate_lanes(expert_ids, gate_weights, experts):
    hits = expert_ids[:, :, None] == jnp.arange(experts, dtype=jnp.int32)[None, None, :]
    gates = jnp.sum(jnp.where(hits, gate_weights[:, :, None], 0.0), axis=1)
    pieces = []
    for _ in range(3):
        piece = lax.reduce_precision(gates, 8, 7)
        pieces.append(piece.astype(jnp.bfloat16))
        gates = gates - piece
    lanes = jnp.concatenate(pieces, axis=1)
    return jnp.pad(lanes, ((0, 0), (0, -lanes.shape[1] % 128)))


def crossed(block, first):
    cores, count = lax.axis_size("tok"), lax.axis_size("blk")
    route = []
    for core in range(cores):
        mask = 1 if (core % 2 == 0) == first else 2
        route += [(core * count + i, core * count + (i ^ mask)) for i in range(count)]
    return lax.ppermute(block, ("tok", "blk"), route)


def expert_kernel(experts, ahead, place_ref, near_ref, far_ref, gate_ref, up_ref, down_ref, *outs):
    width = gate_ref.shape[1]
    parts = len(outs)
    blocks, part_rows, part_width = outs[0].shape
    held = jnp.concatenate([near_ref[...], far_ref[...]], axis=0)
    rows = held[:, :width]
    lanes = held[:, width:].astype(jnp.float32)
    lane_ids = lax.broadcasted_iota(jnp.int32, lanes.shape, 1)
    named = (lane_ids < 3 * experts) & (lane_ids % experts == place_ref[0])
    weight = jnp.sum(jnp.where(named, lanes, 0.0), axis=1, keepdims=True)
    turned = (((1,), (1,)), ((), ()))
    gate_act = lax.dot_general(rows, gate_ref[...], turned, preferred_element_type=jnp.float32)
    up_act = lax.dot_general(rows, up_ref[...], turned, preferred_element_type=jnp.float32)
    hidden = (gate_act / (1.0 + jnp.exp(-gate_act)) * up_act).astype(jnp.bfloat16)
    for part in range(parts):
        start = lax.rem(place_ref[1] + part, parts) * part_width
        columns = pl.ds(pl.multiple_of(start, 128), part_width)
        product = jnp.dot(hidden, down_ref[:, columns], preferred_element_type=jnp.float32)
        product = (weight * product).astype(jnp.bfloat16)
        order = (0, 2, 1, 3) if (part - ahead) % 2 else (0, 1, 2, 3)
        for block in range(blocks):
            outs[part][order[block]] = product[block * part_rows : (block + 1) * part_rows]


def run_expert(place, near, far, w_gate, w_up, w_down, experts, parts, ahead):
    count = 2 * near.shape[0]
    units, width = w_gate.shape
    out_shape = jax.ShapeDtypeStruct((PLANE, count // PLANE, width // parts), jnp.bfloat16)
    return local_call(
        functools.partial(expert_kernel, experts, ahead),
        [out_shape] * parts,
        [place],
        [near, far, w_gate, w_up, w_down],
        flops=6 * count * width * units,
    )


def wide(block):
    return block.astype(jnp.float32)


def narrow(block):
    return block.astype(jnp.bfloat16)


def second_share(totals):
    return narrow(jnp.stack([total[2:4] for total in totals]))


def first_share(totals):
    return narrow(jnp.stack([total[1] for total in totals]))


def merged(totals, got, count):
    return [total[0:count] + wide(got[i]) for i, total in enumerate(totals)]


def expert_outputs(place, near, far, weights, experts, cores, waits):
    outs = []
    for ahead in range(cores):
        near_rows = from_core(near, ahead) if ahead else near
        far_rows = from_core(far, ahead) if ahead else far
        near_rows = after(near_rows, *outs[-1:], *waits.get(ahead, []))
        outs.append(run_expert(place, near_rows, far_rows, *weights, experts, cores, ahead))
    return outs


def core_totals(outs, cores):
    totals = []
    for rows_of in range(cores):
        total = wide(outs[rows_of][0])
        for ahead in range(1, cores):
            sent = outs[(rows_of + ahead) % cores][ahead]
            total = total + wide(from_core(sent, cores - ahead))
        totals.append(total)
    return totals


def on_device(
    q_proj,
    k_proj,
    v_proj,
    residual,
    prompt_lengths,
    expert_ids,
    gate_weights,
    page_table,
    out_weight,
    norm_gain,
    w_gate,
    w_up,
    w_down,
):
    tok_rows = q_proj.shape[0]
    col_width = residual.shape[1]
    model_width = norm_gain.shape[0]
    blk_index = lax.axis_index("blk")
    tok_index = lax.axis_index("tok")
    cores = lax.axis_size("tok")
    experts = lax.axis_size("blk")
    planes = experts // PLANE
    place = jnp.stack([blk_index, tok_index]).astype(jnp.int32)
    part_rows = tok_rows // cores
    half_dim = HEAD_DIM // 2
    inv_freq = 10000.0 ** (-jnp.arange(half_dim, dtype=jnp.float32) / half_dim)
    freq = jnp.concatenate([inv_freq, inv_freq])[None, :]
    rotated = jax.ShapeDtypeStruct(q_proj.shape, jnp.bfloat16)
    rot_query, rot_keys = local_call(
        rope_kernel, [rotated] * 2, [place, prompt_lengths], [freq, q_proj, k_proj]
    )
    column = blk_index % PLANE
    key_blocks, value_blocks = [
        [block, next_plane(block)] for block in (rot_keys, after(v_proj, rot_keys))
    ]
    for blocks in (key_blocks, value_blocks):
        own, below = blocks
        for mask in range(1, PLANE):
            blocks.append(flipped(jnp.where(column < column ^ mask, own, below), mask))
    heads = q_proj.shape[1] // HEAD_DIM
    probs_shape = (heads, tok_rows, len(key_blocks) * tok_rows)
    probs = local_call(
        score_kernel,
        [jax.ShapeDtypeStruct(probs_shape, jnp.bfloat16)],
        [place, prompt_lengths],
        [rot_query, out_weight, *key_blocks],
        flops=2 * tok_rows * probs_shape[2] * heads * HEAD_DIM,
    )[0]
    page_count = tok_rows // PAGE
    local_page = page_table - blk_index * page_count
    kv_rows = jnp.stack([rot_keys, v_proj], axis=1).reshape(page_count, PAGE, 2, -1)
    kv_pages = jnp.zeros_like(kv_rows).at[local_page].set(kv_rows)
    lanes = gate_lanes(expert_ids, gate_weights, experts)
    probs = after(probs, kv_pages, lanes)
    mixed = local_call(
        mix_kernel,
        [jax.ShapeDtypeStruct((tok_rows, model_width), jnp.float32)],
        [place],
        [probs, out_weight, residual, *value_blocks],
        flops=2 * tok_rows * (probs_shape[2] + model_width) * heads * HEAD_DIM,
    )[0]
    if cores == 2:
        addends = [mixed, from_core(mixed, 1)]
    else:
        addends = [lax.psum(mixed, "tok")]
    payload, own_share = local_call(
        norm_kernel,
        [
            jax.ShapeDtypeStruct((part_rows, model_width + lanes.shape[1]), jnp.bfloat16),
            jax.ShapeDtypeStruct((tok_rows, col_width), jnp.bfloat16),
        ],
        [place],
        [norm_gain[None, :], lanes, *addends],
    )
    weights = (w_gate[0].T, w_up[0].T, w_down[0])
    if planes <= 4:
        groups = [[0]] + [sorted({i, planes - i}) for i in range(1, planes // 2 + 1)]
    else:
        groups = [[0]] + [list(range(i, min(i + 8, planes))) for i in range(1, planes, 8)]
    nears, fars = [], []
    for number, group in enumerate(groups):
        sent = after(payload, nears[0]) if number > 1 else payload
        column = jnp.concatenate([from_plane(sent, ahead) if ahead else sent for ahead in group])
        if number > 1:
            column = after(column, nears[-1])
        nears.append(jnp.concatenate([column, crossed(column, True)]))
        fars.append(crossed(nears[-1], False))
    weights = (w_gate[0].T, w_up[0].T, w_down[0])
    run = functools.partial(
        expert_outputs, place, weights=weights, experts=experts, cores=cores
    )
    outs = run(nears[0], fars[0], waits={})
    own_totals = core_totals(outs, cores)
    got = crossed(after(second_share(own_totals), nears[-1]), False)
    own_totals = merged(own_totals, got, 2)
    own_got = crossed(first_share(own_totals), True)
    totals, sents = [], []
    for number in range(1, len(groups)):
        waits = {0: [outs]}
        if number == len(groups) - 1:
            waits = {0: [outs, got], cores - 1: [own_got, *sents]}
        outs = run(nears[number], fars[number], waits=waits)
        totals.append(core_totals(outs, cores))
        sents.append(second_share(totals[-1]))
    got_list, ready = [], []
    for pair, sent in zip(totals, sents, strict=True):
        pair = merged(pair, after(crossed(sent, False), *ready), 2)
        ready = [crossed(first_share(pair), True)]
        got_list.append((pair, ready[0]))
    totals = [pair for pair, _ in got_list]
    gots = [got for _, got in got_list]
    results = {}
    for group, pair, came in zip(
        groups, [own_totals, *totals], [own_got, *gots], strict=True
    ):
        rows_of = merged([total[0] for total in pair], came, None)
        for i, ahead in enumerate(group):
            results[ahead] = jnp.concatenate(
                [rows[i * part_rows : (i + 1) * part_rows] for rows in rows_of]
            )
    moe = results[0]
    for ahead in range(1, planes):
        moe = moe + wide(to_plane(narrow(results[ahead]), ahead))
    moe = jnp.roll(moe.reshape(cores, part_rows, col_width), tok_index, axis=0)
    moe = moe.reshape(tok_rows, col_width)
    layer_out = (own_share.astype(jnp.float32) + moe).astype(jnp.bfloat16)
    return (layer_out, kv_pages)


def solution(mesh):
    placed = (
        P("blk", "tok"),
        P("blk", "tok"),
        P("blk", "tok"),
        P("blk", "tok"),
        P(),
        P("blk", None),
        P("blk", None),
        P("blk"),
        P("tok", None),
        P(),
        P("blk", None, "tok"),
        P("blk", None, "tok"),
        P("blk", "tok", None),
    )
    return jax.shard_map(
        on_device,
        mesh=mesh,
        in_specs=placed,
        out_specs=(P("blk", "tok"), P("blk", None, None, "tok")),
        check_vma=False,
    )
```

```python
import functools

import jax
import jax.numpy as jnp
from jax import lax
from jax.experimental import pallas as pl
from jax.experimental.pallas import tpu as pltpu
from jax.sharding import PartitionSpec as P

HEAD_DIM = 128
REACH = 4
PAGE = 16
PLANE = 4
EPSILON = 1e-06


def after(value, *others):
    return lax.optimization_barrier((value, *others))[0]


def flipped(block, mask):
    return lax.ppermute(block, "blk", [(i, i ^ mask) for i in range(lax.axis_size("blk"))])


def next_plane(block):
    count = lax.axis_size("blk")
    return lax.ppermute(block, "blk", [(i, i + PLANE) for i in range(count - PLANE)])


def from_plane(block, ahead):
    count = lax.axis_size("blk")
    return lax.ppermute(
        block, "blk", [((i + PLANE * ahead) % count, i) for i in range(count)]
    )


def to_plane(block, ahead):
    count = lax.axis_size("blk")
    return lax.ppermute(
        block, "blk", [(i, (i + PLANE * ahead) % count) for i in range(count)]
    )


def from_core(block, ahead):
    count = lax.axis_size("tok")
    return lax.ppermute(block, "tok", [((i + ahead) % count, i) for i in range(count)])


def segment_starts(place_ref, lengths_ref, shape):
    token = place_ref[0] * shape[0] + lax.broadcasted_iota(jnp.int32, shape, 0)
    start = jnp.zeros(shape, jnp.int32)
    end = jnp.int32(0)
    for i in range(lengths_ref.shape[0]):
        end = end + lengths_ref[i]
        start = jnp.where(token >= end, end, start)
    return token, start


def rope_kernel(place_ref, lengths_ref, freq_ref, q_ref, k_ref, q_out, k_out):
    rows, width = q_ref.shape
    shape = (rows, HEAD_DIM)
    token, start = segment_starts(place_ref, lengths_ref, shape)
    angle = (token - start).astype(jnp.float32) * freq_ref[...]
    cosine, sine = jnp.cos(angle), jnp.sin(angle)
    lane = lax.broadcasted_iota(jnp.int32, shape, 1)
    sine = jnp.where(lane < HEAD_DIM // 2, -sine, sine)
    for source, target in ((k_ref, k_out), (q_ref, q_out)):
        for head in range(width // HEAD_DIM):
            columns = slice(head * HEAD_DIM, (head + 1) * HEAD_DIM)
            x = source[:, columns].astype(jnp.float32)
            turned = x * cosine + pltpu.roll(x, HEAD_DIM // 2, 1) * sine
            target[:, columns] = turned.astype(jnp.bfloat16)


def score_kernel(place_ref, lengths_ref, q_ref, weight_ref, *rest):
    *keys, out_ref = rest
    rows, width = q_ref.shape
    shape = (rows, rows)
    token, start = segment_starts(place_ref, lengths_ref, shape)
    blk = place_ref[0]
    column = lax.rem(blk, PLANE)
    bases = [blk, blk - PLANE]
    for mask in range(1, PLANE):
        other = column ^ mask
        bases.append(blk - column + other - jnp.where(other > column, PLANE, 0))
    lane = lax.broadcasted_iota(jnp.int32, shape, 1)
    ids = jnp.concatenate([base * rows + lane for base in bases], axis=1)
    token = jnp.concatenate([token] * len(keys), axis=1)
    start = jnp.concatenate([start] * len(keys), axis=1)
    allowed = (ids >= start) & (ids <= token)
    for head in range(width // HEAD_DIM):
        columns = slice(head * HEAD_DIM, (head + 1) * HEAD_DIM)
        key = jnp.concatenate([ref[:, columns] for ref in keys], axis=0)
        scores = lax.dot_general(
            q_ref[:, columns],
            key,
            (((1,), (1,)), ((), ())),
            preferred_element_type=jnp.float32,
        )
        scores = jnp.where(allowed, scores * HEAD_DIM ** (-0.5), -1e30)
        terms = jnp.exp(scores - jnp.max(scores, axis=1, keepdims=True))
        share = 1.0 / jnp.sum(terms, axis=1, keepdims=True)
        out_ref[head] = (terms * share).astype(jnp.bfloat16)


def mix_kernel(place_ref, prob_ref, weight_ref, residual_ref, *rest):
    *values, out_ref = rest
    heads = prob_ref.shape[0]
    mixed = []
    for head in range(heads):
        columns = slice(head * HEAD_DIM, (head + 1) * HEAD_DIM)
        value = jnp.concatenate([ref[:, columns] for ref in values], axis=0)
        product = jnp.dot(prob_ref[head], value, preferred_element_type=jnp.float32)
        mixed.append(product.astype(jnp.bfloat16))
    attention = jnp.concatenate(mixed, axis=1)
    out_ref[...] = jnp.dot(attention, weight_ref[...], preferred_element_type=jnp.float32)
    width = residual_ref.shape[1]
    own = pl.ds(pl.multiple_of(place_ref[1] * width, 128), width)
    out_ref[:, own] = out_ref[:, own] + residual_ref[...].astype(jnp.float32)


def norm_kernel(place_ref, gain_ref, lanes_ref, *rest):
    *addends, rows_out, share_out = rest
    rows, width = addends[0].shape
    part_rows = rows_out.shape[0]
    part_width = share_out.shape[1]
    own = pl.ds(pl.multiple_of(place_ref[1] * part_width, 128), part_width)
    share_out[...] = sum(ref[:, own] for ref in addends).astype(jnp.bfloat16)
    part = pl.ds(pl.multiple_of(place_ref[1] * part_rows, 16), part_rows)
    stream = sum(ref[part, :] for ref in addends).astype(jnp.bfloat16).astype(jnp.float32)
    scale = lax.rsqrt(jnp.mean(stream * stream, axis=1, keepdims=True) + EPSILON)
    rows_out[:, :width] = (stream * scale * gain_ref[...]).astype(jnp.bfloat16)
    rows_out[:, width:] = lanes_ref[part, :]


def local_call(body, out_shapes, scalars, arrays, flops=0, limit=16, fetch=False):
    whole = pl.BlockSpec(memory_space=pltpu.VMEM)
    scalar = pl.BlockSpec(memory_space=pltpu.SMEM)
    moved = sum(x.size * x.dtype.itemsize for x in (*arrays, *out_shapes))
    ins, outs, extra = [whole] * len(arrays), [whole] * len(out_shapes), {}
    if fetch:
        ins = [pl.BlockSpec(x.shape, lambda i: (0, 0)) for x in arrays]
        outs = [pl.BlockSpec(x.shape, lambda i: (0, 0)) for x in out_shapes]
        extra = {"grid": (1,)}
    return pl.pallas_call(
        body,
        in_specs=[scalar] * len(scalars) + ins,
        out_specs=outs,
        **extra,
        out_shape=out_shapes,
        cost_estimate=pl.CostEstimate(flops=flops, bytes_accessed=moved, transcendentals=0),
        compiler_params=pltpu.CompilerParams(vmem_limit_bytes=limit << 20),
    )(*scalars, *arrays)


def gate_lanes(expert_ids, gate_weights, experts):
    hits = expert_ids[:, :, None] == jnp.arange(experts, dtype=jnp.int32)[None, None, :]
    gates = jnp.sum(jnp.where(hits, gate_weights[:, :, None], 0.0), axis=1)
    pieces = []
    for _ in range(3):
        piece = lax.reduce_precision(gates, 8, 7)
        pieces.append(piece.astype(jnp.bfloat16))
        gates = gates - piece
    lanes = jnp.concatenate(pieces, axis=1)
    return jnp.pad(lanes, ((0, 0), (0, -lanes.shape[1] % 128)))


def crossed(block, first):
    cores, count = lax.axis_size("tok"), lax.axis_size("blk")
    route = []
    for core in range(cores):
        mask = 1 if (core % 2 == 0) == first else 2
        route += [(core * count + i, core * count + (i ^ mask)) for i in range(count)]
    return lax.ppermute(block, ("tok", "blk"), route)


def expert_kernel(experts, ahead, place_ref, near_ref, far_ref, gate_ref, up_ref, down_ref, *outs):
    width = gate_ref.shape[1]
    parts = len(outs)
    blocks, part_rows, part_width = outs[0].shape
    held = jnp.concatenate([near_ref[...], far_ref[...]], axis=0)
    rows = held[:, :width]
    lanes = held[:, width:].astype(jnp.float32)
    lane_ids = lax.broadcasted_iota(jnp.int32, lanes.shape, 1)
    named = (lane_ids < 3 * experts) & (lane_ids % experts == place_ref[0])
    weight = jnp.sum(jnp.where(named, lanes, 0.0), axis=1, keepdims=True)
    turned = (((1,), (1,)), ((), ()))
    gate_act = lax.dot_general(rows, gate_ref[...], turned, preferred_element_type=jnp.float32)
    up_act = lax.dot_general(rows, up_ref[...], turned, preferred_element_type=jnp.float32)
    hidden = (gate_act / (1.0 + jnp.exp(-gate_act)) * up_act).astype(jnp.bfloat16)
    for part in range(parts):
        start = lax.rem(place_ref[1] + part, parts) * part_width
        columns = pl.ds(pl.multiple_of(start, 128), part_width)
        product = jnp.dot(hidden, down_ref[:, columns], preferred_element_type=jnp.float32)
        product = (weight * product).astype(jnp.bfloat16)
        order = (0, 2, 1, 3) if (part - ahead) % 2 else (0, 1, 2, 3)
        for block in range(blocks):
            outs[part][order[block]] = product[block * part_rows : (block + 1) * part_rows]


def run_expert(place, near, far, w_gate, w_up, w_down, experts, parts, ahead):
    count = 2 * near.shape[0]
    units, width = w_gate.shape
    out_shape = jax.ShapeDtypeStruct((PLANE, count // PLANE, width // parts), jnp.bfloat16)
    return local_call(
        functools.partial(expert_kernel, experts, ahead),
        [out_shape] * parts,
        [place],
        [near, far, w_gate, w_up, w_down],
        flops=6 * count * width * units,
    )


def wide(block):
    return block.astype(jnp.float32)


def narrow(block):
    return block.astype(jnp.bfloat16)


def second_share(totals):
    return narrow(jnp.stack([total[2:4] for total in totals]))


def first_share(totals):
    return narrow(jnp.stack([total[1] for total in totals]))


def merged(totals, got, count):
    return [total[0:count] + wide(got[i]) for i, total in enumerate(totals)]


def expert_outputs(place, near, far, weights, experts, cores, waits):
    outs = []
    for ahead in range(cores):
        near_rows = from_core(near, ahead) if ahead else near
        far_rows = from_core(far, ahead) if ahead else far
        near_rows = after(near_rows, *outs[-1:], *waits.get(ahead, []))
        outs.append(run_expert(place, near_rows, far_rows, *weights, experts, cores, ahead))
    return outs


def core_totals(outs, cores):
    totals = []
    for rows_of in range(cores):
        total = wide(outs[rows_of][0])
        for ahead in range(1, cores):
            sent = outs[(rows_of + ahead) % cores][ahead]
            total = total + wide(from_core(sent, cores - ahead))
        totals.append(total)
    return totals


def on_device(
    q_proj,
    k_proj,
    v_proj,
    residual,
    prompt_lengths,
    expert_ids,
    gate_weights,
    page_table,
    out_weight,
    norm_gain,
    w_gate,
    w_up,
    w_down,
):
    tok_rows = q_proj.shape[0]
    col_width = residual.shape[1]
    model_width = norm_gain.shape[0]
    blk_index = lax.axis_index("blk")
    tok_index = lax.axis_index("tok")
    cores = lax.axis_size("tok")
    experts = lax.axis_size("blk")
    planes = experts // PLANE
    place = jnp.stack([blk_index, tok_index]).astype(jnp.int32)
    part_rows = tok_rows // cores
    half_dim = HEAD_DIM // 2
    inv_freq = 10000.0 ** (-jnp.arange(half_dim, dtype=jnp.float32) / half_dim)
    freq = jnp.concatenate([inv_freq, inv_freq])[None, :]
    rotated = jax.ShapeDtypeStruct(q_proj.shape, jnp.bfloat16)
    rot_query, rot_keys = local_call(
        rope_kernel, [rotated] * 2, [place, prompt_lengths], [freq, q_proj, k_proj], fetch=True
    )
    column = blk_index % PLANE
    key_blocks, value_blocks = [
        [block, next_plane(block)] for block in (rot_keys, after(v_proj, rot_keys))
    ]
    for blocks in (key_blocks, value_blocks):
        own, below = blocks
        for mask in range(1, PLANE):
            blocks.append(flipped(jnp.where(column < column ^ mask, own, below), mask))
    heads = q_proj.shape[1] // HEAD_DIM
    probs_shape = (heads, tok_rows, len(key_blocks) * tok_rows)
    probs = local_call(
        score_kernel,
        [jax.ShapeDtypeStruct(probs_shape, jnp.bfloat16)],
        [place, prompt_lengths],
        [rot_query, out_weight, *key_blocks],
        flops=2 * tok_rows * probs_shape[2] * heads * HEAD_DIM,
    )[0]
    page_count = tok_rows // PAGE
    local_page = page_table - blk_index * page_count
    kv_rows = jnp.stack([rot_keys, v_proj], axis=1).reshape(page_count, PAGE, 2, -1)
    kv_pages = jnp.zeros_like(kv_rows).at[local_page].set(kv_rows)
    lanes = gate_lanes(expert_ids, gate_weights, experts)
    probs = after(probs, kv_pages, lanes)
    mixed = local_call(
        mix_kernel,
        [jax.ShapeDtypeStruct((tok_rows, model_width), jnp.float32)],
        [place],
        [probs, out_weight, residual, *value_blocks],
        flops=2 * tok_rows * (probs_shape[2] + model_width) * heads * HEAD_DIM,
    )[0]
    if cores == 2:
        addends = [mixed, from_core(mixed, 1)]
    else:
        addends = [lax.psum(mixed, "tok")]
    payload, own_share = local_call(
        norm_kernel,
        [
            jax.ShapeDtypeStruct((part_rows, model_width + lanes.shape[1]), jnp.bfloat16),
            jax.ShapeDtypeStruct((tok_rows, col_width), jnp.bfloat16),
        ],
        [place],
        [norm_gain[None, :], lanes, *addends],
    )
    weights = (w_gate[0].T, w_up[0].T, w_down[0])
    if planes <= 4:
        groups = [[0]] + [sorted({i, planes - i}) for i in range(1, planes // 2 + 1)]
    else:
        groups = [[0]] + [list(range(i, min(i + 8, planes))) for i in range(1, planes, 8)]
    nears, fars = [], []
    for number, group in enumerate(groups):
        sent = after(payload, nears[0]) if number > 1 else payload
        column = jnp.concatenate([from_plane(sent, ahead) if ahead else sent for ahead in group])
        if number > 1:
            column = after(column, nears[-1])
        nears.append(jnp.concatenate([column, crossed(column, True)]))
        fars.append(crossed(nears[-1], False))
    weights = (w_gate[0].T, w_up[0].T, w_down[0])
    run = functools.partial(
        expert_outputs, place, weights=weights, experts=experts, cores=cores
    )
    outs = run(nears[0], fars[0], waits={})
    own_totals = core_totals(outs, cores)
    got = crossed(after(second_share(own_totals), nears[-1]), False)
    own_totals = merged(own_totals, got, 2)
    own_got = crossed(first_share(own_totals), True)
    totals, sents = [], []
    for number in range(1, len(groups)):
        waits = {0: [outs]}
        if number == len(groups) - 1:
            waits = {0: [outs, got], cores - 1: [own_got, *sents]}
        outs = run(nears[number], fars[number], waits=waits)
        totals.append(core_totals(outs, cores))
        sents.append(second_share(totals[-1]))
    got_list, ready = [], []
    for pair, sent in zip(totals, sents, strict=True):
        pair = merged(pair, after(crossed(sent, False), *ready), 2)
        ready = [first_share(pair)]
        got_list.append((pair, crossed(ready[0], True)))
    totals = [pair for pair, _ in got_list]
    gots = [got for _, got in got_list]
    results = {}
    for group, pair, came in zip(
        groups, [own_totals, *totals], [own_got, *gots], strict=True
    ):
        rows_of = merged([total[0] for total in pair], came, None)
        for i, ahead in enumerate(group):
            results[ahead] = jnp.concatenate(
                [rows[i * part_rows : (i + 1) * part_rows] for rows in rows_of]
            )
    moe = results[0]
    for ahead in range(1, planes):
        moe = moe + wide(to_plane(narrow(results[ahead]), ahead))
    moe = jnp.roll(moe.reshape(cores, part_rows, col_width), tok_index, axis=0)
    moe = moe.reshape(tok_rows, col_width)
    layer_out = (own_share.astype(jnp.float32) + moe).astype(jnp.bfloat16)
    return (layer_out, kv_pages)


def solution(mesh):
    placed = (
        P("blk", "tok"),
        P("blk", "tok"),
        P("blk", "tok"),
        P("blk", "tok"),
        P(),
        P("blk", None),
        P("blk", None),
        P("blk"),
        P("tok", None),
        P(),
        P("blk", None, "tok"),
        P("blk", None, "tok"),
        P("blk", "tok", None),
    )
    return jax.shard_map(
        on_device,
        mesh=mesh,
        in_specs=placed,
        out_specs=(P("blk", "tok"), P("blk", None, None, "tok")),
        check_vma=False,
    )
```
